32 devices in a mesh: section: 2 (over x), expert: 4 (over z), shard: 4 (over y, core).
Axes of the slice: x: 2, y: 2, z: 4, core: 2. Of those that a mesh axis runs over, the one named last changes fastest.
Arguments:
- inputs: bfloat16 [4, 2048, 1536], P(None, ('expert', 'shard')), may hold values from -6 to 6
- segments: int32 [4, 4, 512], P(None, 'expert'), may hold values from 0 to 63, as said below
- routes: int32 [4, 2048, 4], P(None, ('expert', 'shard')), may hold values from 0 to 15, all different within a row; in each aligned block of 128 rows (0 to 127, 128 to 255, ..., all dimensions but the last counted through in order) at most 40 rows name the same one
- gate_weights: float32 [4, 2048, 4], P(None, ('expert', 'shard')), may hold values from 0.1 to 0.4
- query_weight: float32 [2, 1536, 1536], P('section', ('expert', 'shard')), may hold values from -0.21875 to 0.21875
- key_value_weight: float32 [2, 1536, 512], P('section', ('expert', 'shard')), may hold values from -0.21875 to 0.21875
- output_weight: float32 [2, 1536, 1536], P('section', ('expert', 'shard')), may hold values from -0.875 to 0.875
- norm_gains: float32 [2, 2, 1536], P('section', None, ('expert', 'shard')), may hold values from 0.5 to 1.5
- expert_gate_up: float32 [2, 16, 1536, 1536], P('section', 'expert', 'shard'), may hold values from -0.15625 to 0.15625
- expert_down: float32 [2, 16, 768, 1536], P('section', 'expert', 'shard'), may hold values from -0.21875 to 0.21875
- cotangent: bfloat16 [4, 2048, 1536], P(None, ('expert', 'shard')), may hold values from -6 to 6
Outputs:
- output: float32 [4, 2048, 1536], P('section', ('expert', 'shard'))
- input_grad: float32 [4, 2048, 1536], P('section', ('expert', 'shard'))
- query_grad: float32 [2, 1536, 1536], P('section', ('expert', 'shard'))
- key_value_grad: float32 [2, 1536, 512], P('section', ('expert', 'shard'))
- output_weight_grad: float32 [2, 1536, 1536], P('section', ('expert', 'shard'))
- gain_grad: float32 [2, 2, 1536], P('section', None, ('expert', 'shard'))
- gate_up_grad: float32 [2, 16, 1536, 1536], P('section', 'expert', 'shard')
- down_grad: float32 [2, 16, 768, 1536], P('section', 'expert', 'shard')
The draws below stay inside these ranges and needn't reach their ends.
Inputs may be any that keep to these rules, and one draw needn't show every extreme that they name: `routes`: each row names 4 different experts. In each block of 128 rows (the rows of one device in one micro-batch), no expert is named by more than 40 rows, and in some blocks one is named by exactly 40. `segments`: along each sequence the numbers start at 0 and never fall.
All inputs are finite; a program needn't handle non-finite values.
Results may differ from the reference program's by a relative error of at most 0.025.
The reference program's roundings to bfloat16 on the way count: a program that leaves them out, or rounds other values in their place, can miss the bound.
Values may be sent and summed in bfloat16 or wider, within the bound.
A program may use at most 320 MiB of HBM per device.

```python
import math
import jax
import jax.numpy as jnp
import numpy as np
from jax import lax

D = 1536
HEADS = 12
KV_HEADS = 2
HD = 128
FF = 768
TOPK = 4
MICRO = 4
TOK_DEV = 128
EXPERTS = 16
LEN = 512
SEQS = 4
TOKENS = 2048
CAP = 40
N_SECTION = 2


def draw_segments(key, part):
    key = jax.random.fold_in(key, 11)
    rate_key, cut_key, whole_key, pick_key = jax.random.split(key, 4)
    power_exps = jax.random.randint(rate_key, (MICRO, SEQS, 1), 4, 10)
    period = jnp.left_shift(jnp.ones_like(power_exps), power_exps)
    random_draws = jax.random.randint(cut_key, (MICRO, SEQS, LEN), 0, 1048576)
    position = jnp.arange(LEN, dtype=jnp.int32)[None, None, :]
    cut_flags = (random_draws % period == 0) & (position > 0)
    whole_micro = jax.random.randint(whole_key, (1, SEQS, 1), 0, MICRO)
    micro_ids = jnp.arange(MICRO, dtype=jnp.int32)[:, None, None]
    seq_ids = jnp.arange(SEQS, dtype=jnp.int32)[None, :, None]
    aligned_seq = jax.random.randint(pick_key, (1, 1, 1), 0, SEQS)
    aligned_micro = (whole_micro + 1) % MICRO
    aligned_here = (seq_ids == aligned_seq) & (micro_ids == aligned_micro)
    aligned_cuts = (position % 8 == 0) & (position > 0)
    cut_flags = jnp.where(aligned_here, aligned_cuts, cut_flags)
    cut_flags = cut_flags & (micro_ids != whole_micro)
    counted = jnp.cumsum(cut_flags.astype(jnp.int32), axis=2)
    return jnp.minimum(counted, LEN // 8 - 1).astype(jnp.int32)


def block_levels(stream_key, dims, shards, least, largest):
    def one(axis_at, parts):
        draws = jax.random.uniform(jax.random.fold_in(jax.random.fold_in(stream_key, 6), axis_at), (parts,), jnp.float32, least / len(shards), largest / len(shards))
        return jnp.repeat(jnp.exp(draws), dims[axis_at] // parts).reshape((-1,) + (1,) * (len(dims) - axis_at - 1))

    factor_of = one(*shards[0])
    for cut in shards[1:]:
        factor_of = factor_of * one(*cut)
    return factor_of


def deal_out(own_key, own, number, rows, number_of, top, bound, slope):
    order = jax.random.permutation(own_key, number_of)
    crowded, common = load_shares(number_of, rows * top, bound, slope, True), load_shares(number_of, rows * top, bound, slope, False)
    places = jnp.arange(number_of)

    def named(tallies, offset_by):
        used = int((tallies > 0).sum())
        fixed = max(1, used // 4)
        moved = fixed + (places - fixed + offset_by * (used - fixed)) % max(1, number_of - fixed)
        return jnp.zeros((number_of,), jnp.int32).at[order[jnp.where(places < fixed, places, moved)]].set(jnp.asarray(tallies, jnp.int32))

    tallies = jnp.where(number % 4 == 0, named(crowded, number // 4), named(common, number - number // 4 - 1))
    mixed = jax.random.permutation(jax.random.fold_in(own, 3), number_of)
    donor, receiver = mixed[0:number_of // 2 * 2:2], mixed[1:number_of // 2 * 2:2]
    slack = jnp.minimum(tallies[donor] - 1, bound - tallies[receiver]) // 2
    slack = jnp.where((donor == order[0]) | (receiver == order[0]) | (tallies[receiver] == 0), 0, jnp.maximum(slack, 0))
    moved = jax.random.randint(jax.random.fold_in(own, 4), (number_of // 2,), 0, 1 << 20) % (slack + 1)
    tallies = tallies.at[donor].add(-moved).at[receiver].add(moved)
    labels = jnp.searchsorted(jnp.cumsum(tallies), jnp.arange(rows * top), side="right").astype(jnp.int32)
    listing = labels.reshape(top, rows).T
    listing = listing[jax.random.permutation(jax.random.fold_in(own, 1), rows)]
    offset_by = jax.random.randint(jax.random.fold_in(own, 2), (rows, 1), 0, top)
    return jnp.take_along_axis(listing, (jnp.arange(top)[None, :] + offset_by) % top, axis=1)


def load_shares(count, total, reach, slope, full):
    portions = [(1 << 20) // math.isqrt(grade ** slope) + 1 for grade in range(1, count + 1)]
    largest = reach if full else min(reach, max(-(-total // count), total * portions[0] // sum(portions)))
    least = 1 if total - largest >= count - 1 else 0
    given, surplus = [largest] + [least] * (count - 1), total - largest - least * (count - 1)
    while surplus > 0:
        free = [i for i in range(1, count) if given[i] < largest] or [i for i in range(1, count) if given[i] < reach]
        whole, left = sum([portions[i] for i in free]), surplus
        for i in free:
            addition = min(reach - given[i], max(1, left * portions[i] // whole), surplus)
            given[i] = given[i] + addition
            surplus = surplus - addition
    return np.array(given)


def gaussian(own_key, extent, deviation, limit, cuts=(), kind=jnp.bfloat16):
    drawn = jax.random.normal(own_key, extent, jnp.float32) * deviation
    if len(cuts) > 0:
        drawn = block_levels(own_key, extent, cuts, -0.22, 0.18) * drawn
    return jnp.clip(drawn, min=-limit, max=limit).astype(kind)


def setup_inputs(seed: int = 0) -> dict:
    keys = jax.random.split(jax.random.key(seed), 12)
    inputs = gaussian(keys[0], (MICRO, TOKENS, D), 1.0, 6.0, ((1, 16),))
    segments = draw_segments(jax.random.fold_in(keys[11], 71), 0)
    routes_keys = jax.random.split(jax.random.fold_in(keys[2], 1), MICRO * TOKENS // TOK_DEV)
    routes_turns = jax.random.permutation(jax.random.fold_in(keys[2], 3), MICRO * TOKENS // TOK_DEV)
    routes = jax.vmap(lambda own, number: deal_out(jax.random.fold_in(keys[2], 2), own, number, TOK_DEV, EXPERTS, TOPK, CAP, 1))(routes_keys, routes_turns).reshape((MICRO, TOKENS, TOPK))
    gate_weights = jnp.clip(0.1 + 0.3 * jax.random.uniform(keys[3], (MICRO, TOKENS, TOPK), jnp.float32) ** block_levels(keys[3], (MICRO, TOKENS, TOPK), ((1, 16),), -0.2, 0.2), 0.1, 0.4)
    query_weight = gaussian(keys[4], (N_SECTION, D, HEADS * HD), (D // 2) ** -0.5, 0.21875, ((0, 2), (1, 16)), jnp.float32)
    key_value_weight = gaussian(keys[5], (N_SECTION, D, 2 * KV_HEADS * HD), (D // 2) ** -0.5, 0.21875, ((0, 2), (1, 16)), jnp.float32)
    output_weight = gaussian(keys[6], (N_SECTION, HEADS * HD, D), (D // 32) ** -0.5, 0.875, ((0, 2), (1, 16)), jnp.float32)
    norm_gains = jnp.clip(1.0 + 0.1 * jax.random.normal(keys[7], (N_SECTION, 2, D), jnp.float32), 0.5, 1.5)
    expert_gate_up = gaussian(keys[8], (N_SECTION, EXPERTS, D, 2 * FF), D ** -0.5, 0.15625, ((0, 2), (1, 4), (2, 4)), jnp.float32)
    expert_down = gaussian(keys[9], (N_SECTION, EXPERTS, FF, D), FF ** -0.5, 0.21875, ((0, 2), (1, 4), (2, 4)), jnp.float32)
    cotangent = gaussian(keys[10], (MICRO, TOKENS, D), 1.0, 6.0, ((1, 16),))
    return {"inputs": inputs, "segments": segments, "routes": routes, "gate_weights": gate_weights, "query_weight": query_weight, "key_value_weight": key_value_weight, "output_weight": output_weight, "norm_gains": norm_gains, "expert_gate_up": expert_gate_up, "expert_down": expert_down, "cotangent": cotangent}


@jax.custom_vjp
def low(v):
    return lax.optimization_barrier(v.astype(jnp.bfloat16)).astype(jnp.float32)

@jax.custom_vjp
def low_back(v):
    return v

def low_keep(v):
    return (low(v), None)

def low_pass(kept, grad):
    return (grad,)

def back_keep(v):
    return (v, None)

def back_low(kept, grad):
    return (low(grad),)
low.defvjp(low_keep, low_pass)
low_back.defvjp(back_keep, back_low)
highest = lax.Precision.HIGHEST
epsilon = 1e-06
rope_base = 10000.0

def product(left, right):
    return jnp.dot(left, right, precision=highest, preferred_element_type=jnp.float32)

def normed(hidden, gain_row):
    return hidden * lax.rsqrt(lax.optimization_barrier(jnp.mean(hidden * hidden, axis=-1, keepdims=True)) + epsilon) * gain_row

def rotate(values, cosine, sine_table):
    width_half = values.shape[-1] // 2
    first_part = values[..., :width_half]
    second_part = values[..., width_half:]
    return jnp.concatenate([first_part * cosine - second_part * sine_table, second_part * cosine + first_part * sine_table], axis=-1)

def attend(pieces):
    queries, keys_values, segment = pieces
    length = queries.shape[0]
    group_size = HEADS // KV_HEADS
    stacked = queries.reshape(length, KV_HEADS, group_size, HD).transpose(1, 2, 0, 3).reshape(KV_HEADS, group_size * length, HD)
    key_rows = keys_values[:, :KV_HEADS * HD].reshape(length, KV_HEADS, HD)
    value_rows = keys_values[:, KV_HEADS * HD:].reshape(length, KV_HEADS, HD)
    raw_scores = low_back(jnp.einsum('hqd,khd->hqk', stacked, key_rows, precision=highest))
    position = jnp.arange(length, dtype=jnp.int32)
    query_place = jnp.tile(position, group_size)
    query_segment = jnp.tile(segment, group_size)
    allowed = (query_segment[:, None] == segment[None, :]) & (query_place[:, None] >= position[None, :])
    scores = jnp.where(allowed[None], raw_scores * HD ** (-0.5), -1e+30)
    row_max = lax.optimization_barrier(jnp.max(scores, axis=-1, keepdims=True))
    weights = jnp.exp(scores - row_max)
    probs_low = low(weights / lax.optimization_barrier(jnp.sum(weights, axis=-1, keepdims=True)))
    mixed_rows = jnp.einsum('hqk,khd->hqd', probs_low, value_rows, precision=highest)
    mixed_rows = mixed_rows.reshape(KV_HEADS, group_size, length, HD).transpose(2, 0, 1, 3).reshape(length, HEADS * HD)
    return low(low_back(mixed_rows))

def expert_apply(pieces):
    expert_rows, gate_up_weight, down_weight = pieces
    gate_up = low_back(product(expert_rows, low(gate_up_weight)))
    hidden_rows = low(jax.nn.silu(gate_up[:, :FF]) * gate_up[:, FF:])
    return low(low_back(product(hidden_rows, low(down_weight))))

def slot_places(routes_block):
    flat_routes = routes_block.reshape(-1)
    one_hot = (flat_routes[:, None] == jnp.arange(EXPERTS, dtype=jnp.int32)[None, :]).astype(jnp.int32)
    slot_rank = lax.optimization_barrier(jnp.sum((jnp.cumsum(one_hot, axis=0) - one_hot) * one_hot, axis=1))
    return (flat_routes.astype(jnp.int32), slot_rank.astype(jnp.int32))

def layer_apply(hidden, weights, segment, routes_now, gates_now):
    query_weight, key_value_weight, output_weight, gain_pair, gate_up_weight, down_weight = weights
    tokens = hidden.shape[0]
    width_kv = KV_HEADS * HD
    position = (jnp.arange(tokens, dtype=jnp.int32) % LEN).astype(jnp.float32)
    frequency = rope_base ** (-jnp.arange(HD // 2, dtype=jnp.float32) / (HD // 2))
    angles = position[:, None] * frequency[None, :]
    cosine = jnp.cos(angles)[:, None, :]
    sine_table = jnp.sin(angles)[:, None, :]
    normed_one = low(normed(hidden, low(gain_pair[0])))
    queries = low_back(product(normed_one, low(query_weight)))
    keys_values = low_back(product(normed_one, low(key_value_weight)))
    queries = low(rotate(queries.reshape(tokens, HEADS, HD), cosine, sine_table).reshape(tokens, HEADS * HD))
    key_rows = rotate(keys_values[:, :width_kv].reshape(tokens, KV_HEADS, HD), cosine, sine_table).reshape(tokens, width_kv)
    keys_values = low(jnp.concatenate([key_rows, keys_values[:, width_kv:]], axis=1))
    mixed_rows = lax.map(jax.checkpoint(attend), (queries.reshape(SEQS, LEN, HEADS * HD), keys_values.reshape(SEQS, LEN, 2 * width_kv), segment))
    middle = hidden + low_back(product(mixed_rows.reshape(tokens, HEADS * HD), low(output_weight)))
    normed_two = low(normed(middle, low(gain_pair[1])))
    blocks = tokens // TOK_DEV
    owner_ids, slot_rank = jax.vmap(slot_places)(routes_now.reshape(blocks, TOK_DEV, TOPK))
    block_ids = jnp.arange(blocks, dtype=jnp.int32)[:, None]
    slot_place = (owner_ids * (blocks * CAP) + block_ids * CAP + slot_rank).reshape(-1).astype(jnp.int32)
    slot_total = EXPERTS * blocks * CAP
    source = (jnp.arange(tokens * TOPK, dtype=jnp.int32) // TOPK).astype(jnp.int32)
    anchor = jnp.zeros((slot_total,), jnp.int32).at[slot_place].set(source)
    filled = jnp.zeros((slot_total,), jnp.float32).at[slot_place].set(1.0)
    expert_rows = low_back(normed_two[anchor] * filled[:, None])
    outputs = lax.map(jax.checkpoint(expert_apply), (expert_rows.reshape(EXPERTS, blocks * CAP, D), gate_up_weight, down_weight))
    picked = outputs.reshape(slot_total, D)[slot_place].reshape(tokens, TOPK, D)
    return middle + lax.optimization_barrier(jnp.sum(picked * gates_now[:, :, None], axis=1))

def forward(inputs, query_weight, key_value_weight, output_weight, norm_gains, expert_gate_up, expert_down, segments, routes, gate_weights):
    results = []
    for micro_index in range(MICRO):
        hidden = inputs[micro_index]
        for section_index in range(N_SECTION):
            if section_index > 0:
                hidden = low(low_back(hidden))
            weights = (query_weight[section_index], key_value_weight[section_index], output_weight[section_index], norm_gains[section_index], expert_gate_up[section_index], expert_down[section_index])
            hidden = layer_apply(hidden, weights, segments[micro_index], routes[micro_index], gate_weights[micro_index])
        results.append(hidden)
    return jnp.stack(results)

def reference(inputs, segments, routes, gate_weights, query_weight, key_value_weight, output_weight, norm_gains, expert_gate_up, expert_down, cotangent):

    def run_all(start, weight_q, weight_kv, weight_o, gain_all, weight_in, weight_down):
        return forward(start, weight_q, weight_kv, weight_o, gain_all, weight_in, weight_down, segments, routes, gate_weights)
    result, pullback = jax.vjp(run_all, inputs.astype(jnp.float32), query_weight, key_value_weight, output_weight, norm_gains, expert_gate_up, expert_down)
    gradients = pullback(cotangent.astype(jnp.float32))
    return (result, gradients[0], gradients[1], gradients[2], gradients[3], gradients[4], gradients[5], gradients[6])
```

```python
import functools

import jax
import jax.numpy as jnp
from jax import lax
from jax.experimental import pallas as pl
from jax.experimental.pallas import tpu as pltpu
from jax.sharding import PartitionSpec as P

D = 1536
HEADS = 12
KV_HEADS = 2
HD = 128
FF = 768
TOPK = 4
EXP_DEV = 4
MICRO = 4
GROUP = HEADS // KV_HEADS
WQ = HEADS * HD
WK = KV_HEADS * HD
SCALE = HD ** (-0.5)

epsilon = 1e-06
rope_base = 10000.0

MESH = pl.DeviceIdType.MESH
F32 = jnp.float32
BF16 = jnp.bfloat16
DMA = pltpu.SemaphoreType.DMA
VMEM_LIMIT = 60 * 2**20


class Plan:
    def __init__(self, mesh_shape, tokens):
        self.nx, self.nz, self.ns = mesh_shape
        self.tokens = tokens
        self.micro = MICRO // self.nx
        self.rows = self.micro * tokens
        self.ranks = self.nx * self.ns
        self.group = self.ranks // EXP_DEV
        self.halves = self.group // self.micro
        self.sources = self.ranks // self.halves
        self.experts = EXP_DEV * self.nz
        self.capacity = 5 * tokens * TOPK // (4 * self.experts)
        self.slots = -(-self.capacity // 16) * 16


def me():
    return lax.axis_index("section"), lax.axis_index("expert"), lax.axis_index("shard")


def remote(src, dst, send, recv, device):
    return pltpu.make_async_remote_copy(
        src_ref=src,
        dst_ref=dst,
        send_sem=send,
        recv_sem=recv,
        device_id=device,
        device_id_type=MESH,
    )


def greet_plane(plan, along=False):
    x, z, s = me()
    barrier = pltpu.get_barrier_semaphore()
    mine = x * plan.ns + s
    for step in range(1, plan.ranks):
        other = (mine + step) % plan.ranks
        pl.semaphore_signal(
            barrier, inc=1, device_id=(other // plan.ns, z, other % plan.ns), device_id_type=MESH
        )
    total = plan.ranks - 1
    if along:
        for step in range(1, plan.nz):
            pl.semaphore_signal(
                barrier, inc=1, device_id=(x, (z + step) % plan.nz, s), device_id_type=MESH
            )
        total += plan.nz - 1
    pl.semaphore_wait(barrier, total)


def nearest(place, index, count):
    left = place
    right = count - 1 - place
    short = jnp.minimum(left, right)
    odd = index % 2
    near = place + (1 - 2 * odd) * ((index + 1) // 2)
    far = jnp.where(left < right, index, count - 1 - index)
    return jnp.where(index <= 2 * short, near, far)


def moe_kernel(plan, backward, *refs):
    if backward:
        (rows_in, put, take, w_in, w_down, gate_up, out, sent_save, grad_save) = refs[:9]
        scratch = refs[9:]
    else:
        (rows_in, put, take, w_in, w_down, base, out, sent_save, gate_up, hidden) = refs[:10]
        scratch = refs[10:]
    (
        line,
        sbuf,
        xbuf,
        ybuf,
        rbuf,
        pbuf,
        qbuf,
        win_v,
        wdown_v,
        gbuf,
        zbuf,
        line_recv,
        line_right,
        line_left,
        to_send,
        to_recv,
        back_send,
        back_recv,
        sum_send,
        sum_recv,
        local_sem,
        save_sem,
    ) = scratch
    x, z, s = me()
    nz, ns = plan.nz, plan.ns
    rank = x * ns + s
    own_expert = rank // plan.group
    own_micro = (rank % plan.group) // plan.halves
    own_half = rank % plan.halves
    part = ns // plan.halves
    own_source = x * part + s // plan.halves
    slots = plan.slots
    tokens = plan.tokens
    many = plan.sources * slots

    load_in = pltpu.make_async_copy(w_in, win_v, local_sem.at[0])
    load_down = pltpu.make_async_copy(w_down, wdown_v, local_sem.at[1])
    load_in.start()
    load_down.start()
    greet_plane(plan, along=True)

    def along(block, step, own):
        src = rows_in if own else line.at[block]
        sem = line_right if step > 0 else line_left
        return remote(src, line.at[block], sem.at[block], line_recv.at[block], (x, z + step, s))

    def owner(expert, micro):
        rank_to = expert * plan.group + micro * plan.halves + s % plan.halves
        return rank_to // ns, rank_to % ns

    def dispatch_copy(block, expert, micro):
        to_x, to_s = owner(expert, micro)
        return remote(
            sbuf.at[block, micro, expert],
            xbuf.at[block, own_source],
            to_send.at[block, micro, expert],
            to_recv.at[block, own_source],
            (to_x, z, to_s),
        )

    def return_copy(block, source):
        to_x = source // part
        to_s = (source % part) * plan.halves + own_half
        return to_x, to_s, remote(
            ybuf.at[block, source],
            rbuf.at[block, own_micro, own_expert],
            back_send.at[block, source],
            back_recv.at[block, own_micro, own_expert],
            (to_x, z, to_s),
        )

    def sum_copy(block):
        return remote(
            pbuf.at[block], qbuf.at[z], sum_send.at[block], sum_recv.at[z], (x, block, s)
        )

    def wait_saved(slot):
        if backward:
            pltpu.make_async_copy(gbuf.at[slot], grad_save.at[0], save_sem.at[1, slot]).wait()
        else:
            pltpu.make_async_copy(gbuf.at[slot], gate_up.at[0], save_sem.at[1, slot]).wait()
            pltpu.make_async_copy(zbuf.at[slot], hidden.at[0], save_sem.at[2, slot]).wait()

    @pl.when(z + 1 < nz)
    def _():
        along(z, 1, True).start()

    @pl.when(z > 0)
    def _():
        along(z, -1, True).start()

    own_copy = pltpu.make_async_copy(rows_in, line.at[z], local_sem.at[2])
    own_copy.start()
    own_copy.wait()

    def stage_put(index):
        block = nearest(z, index, nz)

        @pl.when(block < z)
        def _():
            along(block, 1, False).wait_recv()

            @pl.when(z + 1 < nz)
            def _():
                along(block, 1, False).start()

        @pl.when(block > z)
        def _():
            along(block, -1, False).wait_recv()

            @pl.when(z > 0)
            def _():
                along(block, -1, False).start()

        for micro in range(plan.micro):
            laid = jnp.dot(
                put[block, micro],
                line[block, pl.ds(micro * tokens, tokens), :],
                preferred_element_type=F32,
            ).astype(BF16)
            for expert in range(EXP_DEV):
                sbuf[block, micro, expert] = laid[expert * slots : (expert + 1) * slots]
        for micro in range(plan.micro):
            for expert in range(EXP_DEV):
                to_x, to_s = owner(expert, micro)
                here = (to_x == x) & (to_s == s)

                @pl.when(here)
                def _():
                    pltpu.make_async_copy(
                        sbuf.at[block, micro, expert],
                        xbuf.at[block, own_source],
                        to_recv.at[block, own_source],
                    ).start()

                @pl.when(jnp.logical_not(here))
                def _():
                    dispatch_copy(block, expert, micro).start()

    def stage_expert(index):
        block = nearest(z, index, nz)
        slot = index % 2
        for source in range(plan.sources):
            pltpu.make_async_copy(
                xbuf.at[block, source], xbuf.at[block, source], to_recv.at[block, source]
            ).wait()

        @pl.when(index >= 2)
        def _():
            wait_saved(slot)

        if backward:
            load = pltpu.make_async_copy(gate_up.at[block], gbuf.at[slot], local_sem.at[3])
            load.start()
            load.wait()
        pltpu.make_async_copy(xbuf.at[block], sent_save.at[block], save_sem.at[0, block]).start()

        taken = xbuf[block].reshape(many, D)
        half = 256

        def middle(step, _):
            at = pl.multiple_of(step * half, half)
            if backward:
                grad_hidden = lax.dot_general(
                    taken,
                    wdown_v[pl.ds(at, half), :],
                    (((1,), (1,)), ((), ())),
                    preferred_element_type=F32,
                )
                gate = gbuf[slot, :, pl.ds(at, half)].astype(F32)
                up = gbuf[slot, :, pl.ds(FF + at, half)].astype(F32)
                sig = 1.0 / (1.0 + jnp.exp(-gate))
                gs = gate * sig
                grad_gate = grad_hidden * up * (sig + gs * (1.0 - sig))
                gbuf[slot, :, pl.ds(at, half)] = grad_gate.astype(BF16)
                gbuf[slot, :, pl.ds(FF + at, half)] = (grad_hidden * gs).astype(BF16)
            else:
                gate = jnp.dot(taken, win_v[:, pl.ds(at, half)], preferred_element_type=F32)
                up = jnp.dot(taken, win_v[:, pl.ds(FF + at, half)], preferred_element_type=F32)
                gbuf[slot, :, pl.ds(at, half)] = gate.astype(BF16)
                gbuf[slot, :, pl.ds(FF + at, half)] = up.astype(BF16)
                zbuf[slot, :, pl.ds(at, half)] = (gate / (1.0 + jnp.exp(-gate)) * up).astype(BF16)
            return 0

        lax.fori_loop(0, FF // half, middle, 0)
        if backward:
            pltpu.make_async_copy(gbuf.at[slot], grad_save.at[block], save_sem.at[1, slot]).start()
        else:
            pltpu.make_async_copy(gbuf.at[slot], gate_up.at[block], save_sem.at[1, slot]).start()
            pltpu.make_async_copy(zbuf.at[slot], hidden.at[block], save_sem.at[2, slot]).start()

        def last(step, _):
            at = pl.multiple_of(step * half, half)
            if backward:
                result = lax.dot_general(
                    gbuf[slot],
                    win_v[pl.ds(at, half), :],
                    (((1,), (1,)), ((), ())),
                    preferred_element_type=F32,
                )
            else:
                result = jnp.dot(
                    zbuf[slot], wdown_v[:, pl.ds(at, half)], preferred_element_type=F32
                )
            ybuf[block, :, :, pl.ds(at, half)] = result.astype(BF16).reshape(
                plan.sources, slots, half
            )
            return 0

        lax.fori_loop(0, D // half, last, 0)
        for source in range(plan.sources):
            to_x, to_s, copy = return_copy(block, source)
            here = (to_x == x) & (to_s == s)

            @pl.when(here)
            def _():
                pltpu.make_async_copy(
                    ybuf.at[block, source],
                    rbuf.at[block, own_micro, own_expert],
                    back_recv.at[block, own_micro, own_expert],
                ).start()

            @pl.when(jnp.logical_not(here))
            def _():
                copy.start()

    def stage_take(index):
        block = nearest(z, index, nz)
        for micro in range(plan.micro):
            for expert in range(EXP_DEV):
                pltpu.make_async_copy(
                    rbuf.at[block, micro, expert],
                    rbuf.at[block, micro, expert],
                    back_recv.at[block, micro, expert],
                ).wait()
        for micro in range(plan.micro):
            got = lax.dot_general(
                take[block, micro],
                rbuf[block, micro].reshape(EXP_DEV * slots, D),
                (((0,), (0,)), ((), ())),
                preferred_element_type=F32,
            )

            @pl.when(block == z)
            def _():
                at = pl.ds(micro * tokens, tokens)
                if backward:
                    out[at, :] = got
                else:
                    out[at, :] = base[at, :] + got

            @pl.when(block != z)
            def _():
                pbuf[block, pl.ds(micro * tokens, tokens), :] = got.astype(BF16)

        @pl.when(block != z)
        def _():
            sum_copy(block).start()

    def body(index, _):
        @pl.when(index < nz)
        def _():
            stage_put(index)

        @pl.when(index == 1)
        def _():
            load_in.wait()
            load_down.wait()

        @pl.when((index >= 1) & (index < nz + 1))
        def _():
            stage_expert(index - 1)

        @pl.when(index >= 2)
        def _():
            stage_take(index - 2)

        return 0

    lax.fori_loop(0, nz + 2, body, 0)

    def finish(block, _):
        @pl.when(block != z)
        def _():
            pltpu.make_async_copy(qbuf.at[block], qbuf.at[block], sum_recv.at[block]).wait()
            out[...] += qbuf[block].astype(F32)

        return 0

    lax.fori_loop(0, nz, finish, 0)

    def drain(block, _):
        @pl.when((block <= z) & (z + 1 < nz))
        def _():
            along(block, 1, False).wait_send()

        @pl.when((block >= z) & (z > 0))
        def _():
            along(block, -1, False).wait_send()

        for micro in range(plan.micro):
            for expert in range(EXP_DEV):
                to_x, to_s = owner(expert, micro)

                @pl.when(jnp.logical_not((to_x == x) & (to_s == s)))
                def _():
                    dispatch_copy(block, expert, micro).wait_send()

        for source in range(plan.sources):
            to_x, to_s, copy = return_copy(block, source)

            @pl.when(jnp.logical_not((to_x == x) & (to_s == s)))
            def _():
                copy.wait_send()

        @pl.when(block != z)
        def _():
            sum_copy(block).wait_send()

        pltpu.make_async_copy(xbuf.at[block], sent_save.at[block], save_sem.at[0, block]).wait()
        return 0

    lax.fori_loop(0, nz, drain, 0)
    for slot in range(2):
        wait_saved(slot)


def moe_call(plan, backward, collective_id, rows_in, put, take, w_in, w_down, last):
    nz, micro, slots, many = plan.nz, plan.micro, plan.slots, plan.sources * plan.slots
    vmem = pl.BlockSpec(memory_space=pltpu.VMEM)
    hbm = pl.BlockSpec(memory_space=pltpu.HBM)
    saved = (nz, plan.sources, slots, D)
    shape = jax.ShapeDtypeStruct
    outs = [shape((plan.rows, D), F32), shape(saved, BF16), shape((nz, many, 2 * FF), BF16)]
    if not backward:
        outs.append(shape((nz, many, FF), BF16))
    return pl.pallas_call(
        functools.partial(moe_kernel, plan, backward),
        out_shape=outs,
        in_specs=[vmem, vmem, vmem, hbm, hbm, hbm if backward else vmem],
        out_specs=[vmem] + [hbm] * (len(outs) - 1),
        scratch_shapes=[
            pltpu.VMEM((nz, plan.rows, D), BF16),
            pltpu.VMEM((nz, micro, EXP_DEV, slots, D), BF16),
            pltpu.VMEM(saved, BF16),
            pltpu.VMEM(saved, BF16),
            pltpu.VMEM((nz, micro, EXP_DEV, slots, D), BF16),
            pltpu.VMEM((nz, plan.rows, D), BF16),
            pltpu.VMEM((nz, plan.rows, D), BF16),
            pltpu.VMEM((D, 2 * FF), BF16),
            pltpu.VMEM((FF, D), BF16),
            pltpu.VMEM((2, many, 2 * FF), BF16),
            pltpu.VMEM((2, many, FF), BF16),
            DMA((nz,)),
            DMA((nz,)),
            DMA((nz,)),
            DMA((nz, micro, EXP_DEV)),
            DMA((nz, plan.sources)),
            DMA((nz, plan.sources)),
            DMA((nz, micro, EXP_DEV)),
            DMA((nz,)),
            DMA((nz,)),
            DMA((4,)),
            DMA((3, nz)),
        ],
        compiler_params=pltpu.CompilerParams(
            collective_id=collective_id, has_side_effects=True, vmem_limit_bytes=VMEM_LIMIT
        ),
    )(rows_in, put, take, w_in, w_down, last)


def spread_kernel(plan, *refs):
    ins, outs = refs[:2], refs[2:4]
    send, recv, pass_send, pass_recv, local_sem = refs[4:]
    x, z, s = me()
    nx, ns, group = plan.nx, plan.ns, plan.group
    rank = x * ns + s
    own_expert, own_part = rank // group, rank % group
    greet_plane(plan)

    def first(expert, which):
        to = expert * group + s % group
        return to, remote(
            ins[which].at[expert],
            outs[which].at[x, s],
            send.at[expert, which],
            recv.at[x, s, which],
            (to // ns, z, to % ns),
        )

    def onward(layer, source, step, which):
        to = own_expert * group + (own_part + step) % group
        return remote(
            outs[which].at[layer, source],
            outs[which].at[layer, source],
            pass_send.at[layer, source, step - 1, which],
            recv.at[layer, source, which],
            (to // ns, z, to % ns),
        )

    for which in range(2):
        for expert in range(EXP_DEV):
            to, copy = first(expert, which)

            @pl.when(to == rank)
            def _():
                pltpu.make_async_copy(
                    ins[which].at[expert], outs[which].at[x, s], recv.at[x, s, which]
                ).start()

            @pl.when(to != rank)
            def _():
                copy.start()

    def arrived(layer, source, which):
        pltpu.make_async_copy(
            outs[which].at[layer, source], outs[which].at[layer, source], recv.at[layer, source, which]
        ).wait()

    for layer in range(nx):
        for k in range(ns // group):
            source = k * group + own_part
            for which in range(2):
                arrived(layer, source, which)
                for step in range(1, group):
                    onward(layer, source, step, which).start()
    for layer in range(nx):
        for k in range(ns // group):
            for step in range(1, group):
                source = k * group + (own_part + step) % group
                for which in range(2):
                    arrived(layer, source, which)
    for which in range(2):
        for expert in range(EXP_DEV):
            to, copy = first(expert, which)

            @pl.when(to != rank)
            def _():
                copy.wait_send()

    for layer in range(nx):
        for k in range(ns // group):
            source = k * group + own_part
            for which in range(2):
                for step in range(1, group):
                    onward(layer, source, step, which).wait_send()


def spread_call(plan, collective_id, gate_up, down):
    nx, ns = plan.nx, plan.ns
    hbm = pl.BlockSpec(memory_space=pltpu.HBM)
    outs = [jax.ShapeDtypeStruct((nx, ns) + part.shape[1:], BF16) for part in (gate_up, down)]
    return pl.pallas_call(
        functools.partial(spread_kernel, plan),
        out_shape=outs,
        in_specs=[hbm, hbm],
        out_specs=[hbm, hbm],
        scratch_shapes=[
            DMA((EXP_DEV, 2)),
            DMA((nx, ns, 2)),
            DMA((nx, ns, plan.group - 1, 2)),
            DMA((1,)),
            DMA((1,)),
        ],
        compiler_params=pltpu.CompilerParams(collective_id=collective_id, has_side_effects=True),
    )(gate_up, down)


def collect_kernel(plan, layer, *refs):
    ins, outs = refs[:2], refs[2:4]
    parts, stage = refs[4:6], refs[6:8]
    swap_send, swap_recv, send, recv = refs[8:]
    x, z, s = me()
    ns, group = plan.ns, plan.group
    rank = x * ns + s
    own_expert, own_part = rank // group, rank % group
    each = ns // group
    greet_plane(plan)

    def swap(k, step, which):
        part_to = (own_part + step) % group
        to = own_expert * group + part_to
        return remote(
            ins[which].at[k * group + part_to],
            parts[which].at[step - 1, k],
            swap_send.at[step - 1, k, which],
            swap_recv.at[step - 1, k, which],
            (to // ns, z, to % ns),
        )

    def home(k, which):
        return remote(
            stage[which].at[k],
            outs[which].at[own_expert],
            send.at[k, which],
            recv.at[own_expert, which],
            (layer, z, k * group + own_part),
        )

    for k in range(each):
        for which in range(2):
            for step in range(1, group):
                swap(k, step, which).start()
    for k in range(each):
        for which in range(2):
            for step in range(1, group):
                swap(k, step, which).wait_recv()
            total = ins[which][k * group + own_part].astype(F32)
            for step in range(1, group):
                total += parts[which][step - 1, k].astype(F32)
            stage[which][k] = total.astype(BF16)
            here = (x == layer) & (s == k * group + own_part)

            @pl.when(here)
            def _():
                pltpu.make_async_copy(
                    stage[which].at[k], outs[which].at[own_expert], recv.at[own_expert, which]
                ).start()

            @pl.when(jnp.logical_not(here))
            def _():
                home(k, which).start()

    @pl.when(x == layer)
    def _():
        for which in range(2):
            for expert in range(EXP_DEV):
                pltpu.make_async_copy(
                    outs[which].at[expert], outs[which].at[expert], recv.at[expert, which]
                ).wait()

    for k in range(each):
        for which in range(2):
            for step in range(1, group):
                swap(k, step, which).wait_send()
            here = (x == layer) & (s == k * group + own_part)

            @pl.when(jnp.logical_not(here))
            def _():
                home(k, which).wait_send()


def collect_call(plan, layer, collective_id, gate_up, down):
    ns, group = plan.ns, plan.group
    each = ns // group
    vmem = pl.BlockSpec(memory_space=pltpu.VMEM)
    hbm = pl.BlockSpec(memory_space=pltpu.HBM)
    values = [part.reshape(ns, part.shape[0] // ns, D) for part in (gate_up, down)]
    return pl.pallas_call(
        functools.partial(collect_kernel, plan, layer),
        out_shape=[jax.ShapeDtypeStruct((EXP_DEV,) + part.shape[1:], BF16) for part in values],
        in_specs=[vmem, vmem],
        out_specs=[hbm, hbm],
        scratch_shapes=[pltpu.VMEM((group - 1, each) + part.shape[1:], BF16) for part in values]
        + [pltpu.VMEM((each,) + part.shape[1:], BF16) for part in values]
        + [
            DMA((group - 1, each, 2)),
            DMA((group - 1, each, 2)),
            DMA((each, 2)),
            DMA((EXP_DEV, 2)),
        ],
        compiler_params=pltpu.CompilerParams(
            collective_id=collective_id, has_side_effects=True, vmem_limit_bytes=VMEM_LIMIT
        ),
    )(*values)


def rotate(values, cosine, sine_table):
    width_half = values.shape[-1] // 2
    first_part = values[..., :width_half]
    second_part = values[..., width_half:]
    return jnp.concatenate(
        [
            first_part * cosine - second_part * sine_table,
            second_part * cosine + first_part * sine_table,
        ],
        axis=-1,
    )


def norm_forward(hidden, gain_row):
    inverse = lax.rsqrt(jnp.mean(hidden * hidden, axis=-1, keepdims=True) + epsilon)
    return (hidden * inverse * gain_row, inverse)


def norm_backward(hidden, inverse, gain_row, grad_normed):
    scaled = grad_normed * gain_row
    gain_term = jnp.sum(grad_normed * hidden * inverse, axis=0)
    row_inner = jnp.mean(scaled * hidden, axis=-1, keepdims=True)
    return (inverse * scaled - hidden * inverse * inverse * inverse * row_inner, gain_term)


def slot_tables(plan, routes, gates):
    experts, nz = plan.experts, plan.nz
    named = routes[..., None] == jnp.arange(experts, dtype=jnp.int32)
    gate = jnp.sum(jnp.where(named, gates[..., None], 0.0), axis=2)
    named = jnp.any(named, axis=2)
    earlier = jnp.tril(jnp.ones((plan.tokens, plan.tokens), BF16), -1)
    rank = jnp.einsum("ut,mte->mue", earlier, named.astype(BF16), preferred_element_type=F32)
    table = jnp.stack([jnp.where(named, rank, -1.0), gate])
    table = table.reshape(2, plan.micro, plan.tokens, nz, EXP_DEV).transpose(3, 0, 1, 4, 2)
    table = lax.all_to_all(table, "expert", split_axis=0, concat_axis=0, tiled=True)
    rank, gate = table[:, 0], table[:, 1]
    hit = rank[:, :, :, None, :] == jnp.arange(plan.slots, dtype=F32)[:, None]
    shape = (nz, plan.micro, EXP_DEV * plan.slots, plan.tokens)
    one = hit.astype(BF16).reshape(shape)
    weighted = jnp.where(hit, gate[:, :, :, None, :], 0.0).astype(BF16).reshape(shape)
    return one, weighted


def shards(
    inputs,
    segments,
    routes,
    gate_weights,
    query_weight,
    key_value_weight,
    output_weight,
    norm_gains,
    expert_gate_up,
    expert_down,
    cotangent,
):
    section = lax.axis_index("section")
    shard_index = lax.axis_index("shard")
    tokens = inputs.shape[1]
    plan = Plan((lax.axis_size("section"), lax.axis_size("expert"), lax.axis_size("shard")), tokens)
    micro, rows, layers = plan.micro, plan.rows, plan.nx
    length = tokens * plan.ns

    def mine(value):
        return lax.dynamic_slice_in_dim(value, section * micro, micro, 0)

    everywhere = ("section", "expert", "shard")
    weight_q = lax.all_gather(query_weight[0].astype(BF16), everywhere, axis=0, tiled=True)
    weight_kv = lax.all_gather(key_value_weight[0].astype(BF16), everywhere, axis=0, tiled=True)
    weight_o = lax.all_gather(output_weight[0].astype(BF16), everywhere, axis=0, tiled=True)
    weight_q, weight_kv, weight_o = (
        part.reshape((layers, D) + part.shape[1:]) for part in (weight_q, weight_kv, weight_o)
    )
    gains = lax.all_gather(norm_gains.astype(BF16), everywhere, axis=0, tiled=True)
    gains = (
        gains.reshape(layers, plan.nz * plan.ns, 2, -1)
        .transpose(0, 2, 1, 3)
        .reshape(layers, 2, D)
        .astype(F32)
    )
    wide_in, wide_down = spread_call(
        plan, 1, expert_gate_up[0].astype(BF16), expert_down[0].astype(BF16)
    )
    wide_in = wide_in.reshape(layers, D, 2 * FF)
    wide_down = wide_down.reshape(layers, FF, D)
    one, weighted = slot_tables(plan, mine(routes), mine(gate_weights))

    offset = shard_index * tokens
    position = (offset + jnp.arange(tokens, dtype=jnp.int32)).astype(F32)
    frequency = rope_base ** (-jnp.arange(HD // 2, dtype=F32) / (HD // 2))
    angles = position[:, None] * frequency[None, :]
    cosine = jnp.cos(angles)[:, None, :]
    sine_table = jnp.sin(angles)[:, None, :]
    segment_all = mine(segments)[:, 0]
    segment_own = lax.dynamic_slice_in_dim(segment_all, offset, tokens, 1)
    query_place = offset + jnp.arange(tokens, dtype=jnp.int32)
    key_place = jnp.arange(length, dtype=jnp.int32)
    allowed = (segment_own[:, :, None] == segment_all[:, None, :]) & (
        query_place[:, None] >= key_place[None, :]
    )
    allowed = jnp.tile(allowed, (1, GROUP, 1))[:, None]

    def stack_heads(values):
        return (
            values.reshape(micro, tokens, KV_HEADS, GROUP, HD)
            .transpose(0, 2, 3, 1, 4)
            .reshape(micro, KV_HEADS, GROUP * tokens, HD)
        )

    def unstack_heads(values):
        return (
            values.reshape(micro, KV_HEADS, GROUP, tokens, HD)
            .transpose(0, 3, 1, 2, 4)
            .reshape(micro, tokens, HEADS, HD)
        )

    def split_kv(all_kv):
        key_rows = all_kv[..., :WK].reshape(micro, length, KV_HEADS, HD)
        value_rows = all_kv[..., WK:].reshape(micro, length, KV_HEADS, HD)
        return key_rows, value_rows

    def score(stacked, key_rows):
        raw = jnp.einsum("mhqd,mkhd->mhqk", stacked, key_rows, preferred_element_type=F32)
        return jnp.where(allowed, raw * SCALE, -1e30)

    def attend_forward(layer, start):
        normed, inverse = norm_forward(start, gains[layer, 0])
        low = normed.astype(BF16)
        queries = jnp.dot(low, weight_q[layer], preferred_element_type=F32)
        keys_values = jnp.dot(low, weight_kv[layer], preferred_element_type=F32)
        queries_low = rotate(
            queries.reshape(micro, tokens, HEADS, HD), cosine, sine_table
        ).astype(BF16)
        key_rot = rotate(
            keys_values[:, :WK].reshape(micro, tokens, KV_HEADS, HD), cosine, sine_table
        ).reshape(rows, WK)
        local_kv = jnp.concatenate([key_rot, keys_values[:, WK:]], axis=1).astype(BF16)
        local_kv = local_kv.reshape(micro, tokens, 2 * WK)
        all_kv = jnp.stack(
            [lax.all_gather(local_kv[i], "shard", axis=0, tiled=True) for i in range(micro)]
        )
        stacked = stack_heads(queries_low)
        key_rows, value_rows = split_kv(all_kv)
        scores = score(stacked, key_rows)
        row_max = jnp.max(scores, axis=-1, keepdims=True)
        weights = jnp.exp(scores - row_max)
        row_sum = jnp.sum(weights, axis=-1, keepdims=True)
        probs = (weights / row_sum).astype(BF16)
        mixed = jnp.einsum("mhqk,mkhd->mhqd", probs, value_rows, preferred_element_type=F32)
        mixed_low = unstack_heads(mixed.astype(BF16)).reshape(rows, WQ)
        middle = start + jnp.dot(mixed_low, weight_o[layer], preferred_element_type=F32)
        return middle, (start, inverse, low, stacked, all_kv, row_max, row_sum, mixed_low)

    def attend_backward(layer, saved, grad_middle):
        start, inverse, low, stacked, all_kv, row_max, row_sum, mixed_low = saved
        branch = grad_middle.astype(BF16)
        out_term = jnp.einsum("tq,td->qd", mixed_low, branch, preferred_element_type=F32)
        grad_mixed = jnp.einsum(
            "td,qd->tq", branch, weight_o[layer], preferred_element_type=F32
        ).astype(BF16)
        grad_stacked = stack_heads(grad_mixed)
        key_rows, value_rows = split_kv(all_kv)
        scores = score(stacked, key_rows)
        probs = jnp.exp(scores - row_max) / row_sum
        grad_probs = jnp.einsum(
            "mhqd,mkhd->mhqk", grad_stacked, value_rows, preferred_element_type=F32
        )
        inner = jnp.sum(grad_probs * probs, axis=-1, keepdims=True)
        grad_raw = (probs * (grad_probs - inner) * SCALE).astype(BF16)
        grad_queries = jnp.einsum(
            "mhqk,mkhd->mhqd", grad_raw, key_rows, preferred_element_type=F32
        )
        grad_keys = jnp.einsum("mhqk,mhqd->mkhd", grad_raw, stacked, preferred_element_type=F32)
        grad_values = jnp.einsum(
            "mhqk,mhqd->mkhd", probs.astype(BF16), grad_stacked, preferred_element_type=F32
        )
        partial = jnp.concatenate(
            [grad_keys.reshape(micro, length, WK), grad_values.reshape(micro, length, WK)], axis=2
        ).astype(BF16)
        grad_kv = jnp.concatenate(
            [
                lax.psum_scatter(partial[i], "shard", scatter_dimension=0, tiled=True)
                for i in range(micro)
            ]
        ).astype(F32)
        grad_q_low = (
            rotate(unstack_heads(grad_queries), cosine, -sine_table).reshape(rows, WQ).astype(BF16)
        )
        grad_k = rotate(
            grad_kv[:, :WK].reshape(micro, tokens, KV_HEADS, HD), cosine, -sine_table
        ).reshape(rows, WK)
        grad_kv_low = jnp.concatenate([grad_k, grad_kv[:, WK:]], axis=1).astype(BF16)
        query_term = jnp.einsum("td,tq->dq", low, grad_q_low, preferred_element_type=F32)
        kv_term = jnp.einsum("td,tk->dk", low, grad_kv_low, preferred_element_type=F32)
        grad_normed = jnp.einsum(
            "tq,dq->td", grad_q_low, weight_q[layer], preferred_element_type=F32
        ) + jnp.einsum("tk,dk->td", grad_kv_low, weight_kv[layer], preferred_element_type=F32)
        grad_from, gain_term = norm_backward(start, inverse, gains[layer, 0], grad_normed)
        return grad_middle + grad_from, (query_term, kv_term, out_term, gain_term)

    hidden = mine(inputs).reshape(rows, D).astype(F32)
    kept = []
    for layer in range(layers):
        if layer > 0:
            hidden = hidden.astype(BF16).astype(F32)
        middle, saved = attend_forward(layer, hidden)
        normed, inverse = norm_forward(middle, gains[layer, 1])
        hidden, sent, gate_up, hidden_low = moe_call(
            plan,
            False,
            2 + layer,
            normed.astype(BF16),
            one,
            weighted,
            wide_in[layer],
            wide_down[layer],
            middle,
        )
        kept.append((saved, middle, inverse, sent, gate_up, hidden_low))
    output = hidden.reshape(micro, tokens, D)

    grad = mine(cotangent).reshape(rows, D)
    attention_terms = [None] * layers
    expert_terms = [None] * layers
    for layer in reversed(range(layers)):
        saved, middle, inverse, sent, gate_up, hidden_low = kept[layer]
        grad_low = grad.astype(BF16)
        grad_out = grad_low.astype(F32)
        grad_moe, grad_sent, grad_both = moe_call(
            plan,
            True,
            2 + layers + layer,
            grad_low,
            weighted,
            one,
            wide_in[layer],
            wide_down[layer],
            gate_up,
        )
        in_term = jnp.einsum(
            "rd,rf->df",
            sent.reshape(-1, D),
            grad_both.reshape(-1, 2 * FF),
            preferred_element_type=F32,
        ).astype(BF16)
        down_term = jnp.einsum(
            "rf,rd->fd",
            hidden_low.reshape(-1, FF),
            grad_sent.reshape(-1, D),
            preferred_element_type=F32,
        ).astype(BF16)
        expert_terms[layer] = collect_call(plan, layer, 2 + 2 * layers + layer, in_term, down_term)
        grad_from, gain_two = norm_backward(middle, inverse, gains[layer, 1], grad_moe)
        grad, terms = attend_backward(layer, saved, grad_out + grad_from)
        attention_terms[layer] = terms[:3] + (jnp.stack([terms[3], gain_two]),)
    input_grad = grad.reshape(micro, tokens, D)

    def scattered(parts):
        both = jnp.concatenate([part.astype(BF16) for part in parts])
        return lax.psum_scatter(both, everywhere, scatter_dimension=0, tiled=True).astype(F32)[None]

    query_grad, key_value_grad, output_weight_grad = (
        scattered([terms[i] for terms in attention_terms]) for i in range(3)
    )
    gain_parts = jnp.stack([terms[3] for terms in attention_terms])
    gain_parts = gain_parts.reshape(layers, 2, plan.nz * plan.ns, -1).transpose(0, 2, 1, 3)
    gain_grad = lax.psum_scatter(
        gain_parts.reshape((layers * plan.nz * plan.ns,) + (2, gain_parts.shape[-1])),
        everywhere,
        scatter_dimension=0,
        tiled=True,
    )
    gate_up_grad, down_grad = (
        sum(
            jnp.where(section == layer, expert_terms[layer][i], 0) for layer in range(layers)
        ).astype(F32)[None]
        for i in range(2)
    )
    return (
        output,
        input_grad,
        query_grad,
        key_value_grad,
        output_weight_grad,
        gain_grad,
        gate_up_grad,
        down_grad,
    )


def solution(mesh):
    placed = (
        P(None, ("expert", "shard"), None),
        P(None, "expert", None),
        P(None, ("expert", "shard"), None),
        P(None, ("expert", "shard"), None),
        P("section", ("expert", "shard"), None),
        P("section", ("expert", "shard"), None),
        P("section", ("expert", "shard"), None),
        P("section", None, ("expert", "shard")),
        P("section", "expert", "shard", None),
        P("section", "expert", "shard", None),
        P(None, ("expert", "shard"), None),
    )
    return jax.shard_map(
        shards,
        mesh=mesh,
        in_specs=placed,
        out_specs=(
            P("section", ("expert", "shard"), None),
            P("section", ("expert", "shard"), None),
            P("section", ("expert", "shard"), None),
            P("section", ("expert", "shard"), None),
            P("section", ("expert", "shard"), None),
            P("section", None, ("expert", "shard")),
            P("section", "expert", "shard", None),
            P("section", "expert", "shard", None),
        ),
        check_vma=False,
    )
```

```python
import functools

import jax
import jax.numpy as jnp
from jax import lax
from jax.experimental import pallas as pl
from jax.experimental.pallas import tpu as pltpu
from jax.sharding import PartitionSpec as P

D = 1536
HEADS = 12
KV_HEADS = 2
HD = 128
FF = 768
TOPK = 4
EXP_DEV = 4
MICRO = 4
GROUP = HEADS // KV_HEADS
WQ = HEADS * HD
WK = KV_HEADS * HD
SCALE = HD ** (-0.5)

epsilon = 1e-06
rope_base = 10000.0

MESH = pl.DeviceIdType.MESH
F32 = jnp.float32
BF16 = jnp.bfloat16
DMA = pltpu.SemaphoreType.DMA
VMEM_LIMIT = 60 * 2**20


class Plan:
    def __init__(self, mesh_shape, tokens):
        self.nx, self.nz, self.ns = mesh_shape
        self.tokens = tokens
        self.micro = MICRO // self.nx
        self.rows = self.micro * tokens
        self.ranks = self.nx * self.ns
        self.group = self.ranks // EXP_DEV
        self.halves = self.group // 2
        self.sources = self.ranks // self.halves
        self.experts = EXP_DEV * self.nz
        self.capacity = 5 * tokens * TOPK // (4 * self.experts)
        self.slots = -(-self.micro * self.capacity // 16) * 16
        self.blocks = self.nz // 2
        self.many = self.sources * self.slots


def me():
    return lax.axis_index("section"), lax.axis_index("expert"), lax.axis_index("shard")


def remote(src, dst, send, recv, device):
    return pltpu.make_async_remote_copy(
        src_ref=src,
        dst_ref=dst,
        send_sem=send,
        recv_sem=recv,
        device_id=device,
        device_id_type=MESH,
    )


def landed(ref, sem):
    pltpu.make_async_copy(ref, ref, sem).wait()


def greet_plane(plan, along=False):
    x, z, s = me()
    barrier = pltpu.get_barrier_semaphore()
    mine = x * plan.ns + s
    for step in range(1, plan.ranks):
        other = (mine + step) % plan.ranks
        pl.semaphore_signal(
            barrier, inc=1, device_id=(other // plan.ns, z, other % plan.ns), device_id_type=MESH
        )
    total = plan.ranks - 1
    if along:
        for step in range(1, plan.nz):
            pl.semaphore_signal(
                barrier, inc=1, device_id=(x, (z + step) % plan.nz, s), device_id_type=MESH
            )
        total += plan.nz - 1
    pl.semaphore_wait(barrier, total)


def nearest(place, index, count):
    left = place
    right = count - 1 - place
    short = jnp.minimum(left, right)
    odd = index % 2
    near = place + (1 - 2 * odd) * ((index + 1) // 2)
    far = jnp.where(left < right, index, count - 1 - index)
    return jnp.where(index <= 2 * short, near, far)


HALF = D // 2
TILE = 256


def moe_kernel(plan, backward, *refs):
    if backward:
        (rows_in, put, take, w_in, w_down, gate_up, out, sent_save, grad_save) = refs[:9]
        scratch = refs[9:]
    else:
        (rows_in, put, take, w_in, w_down, base, out, sent_save, gate_up, hidden) = refs[:10]
        scratch = refs[10:]
    (
        line,
        sbuf,
        xbuf,
        ybuf,
        rbuf,
        pbuf,
        qbuf,
        win_v,
        wdown_v,
        gbuf,
        zbuf,
        line_recv,
        line_right,
        line_left,
        to_send,
        to_recv,
        back_send,
        back_recv,
        sum_send,
        sum_recv,
        local_sem,
        save_sem,
    ) = scratch
    x, z, s = me()
    nz, ns, slots, many = plan.nz, plan.ns, plan.slots, plan.many
    rank = x * ns + s
    own_expert = rank // plan.group
    own_turn = (rank % plan.group) // plan.halves
    own_half = rank % plan.halves
    part = ns // plan.halves
    own_source = x * part + s // plan.halves
    chunk = plan.tokens

    load_in = pltpu.make_async_copy(w_in, win_v, local_sem.at[0])
    load_down = pltpu.make_async_copy(w_down, wdown_v, local_sem.at[1])
    load_in.start()
    load_down.start()
    if backward:
        load_gate = pltpu.make_async_copy(gate_up, gbuf, local_sem.at[3])
        load_gate.start()
    greet_plane(plan, along=True)

    def along(block, piece, step, own):
        at = pl.ds(piece * chunk, chunk)
        src = rows_in.at[at] if own else line.at[block, at]
        sem = line_right if step > 0 else line_left
        return remote(
            src,
            line.at[block, at],
            sem.at[block, piece],
            line_recv.at[block, piece],
            (x, z + step, s),
        )

    def owner(block, expert):
        rank_to = expert * plan.group + (block % 2) * plan.halves + s % plan.halves
        return rank_to // ns, rank_to % ns

    def dispatch_copy(block, expert):
        to_x, to_s = owner(block, expert)
        here = (to_x == x) & (to_s == s)
        return here, remote(
            sbuf.at[block, expert],
            xbuf.at[block // 2, own_source],
            to_send.at[block, expert],
            to_recv.at[block // 2, own_source],
            (to_x, z, to_s),
        )

    def return_copy(block, half, source):
        to_x = source // part
        to_s = (source % part) * plan.halves + own_half
        here = (to_x == x) & (to_s == s)
        return here, remote(
            ybuf.at[block // 2, half, source],
            rbuf.at[block, half, own_expert],
            back_send.at[block // 2, half, source],
            back_recv.at[block, half, own_expert],
            (to_x, z, to_s),
        )

    def sum_copy(block, half):
        rightward = (block > z).astype(jnp.int32)
        to = z - 1 + 2 * rightward
        into = jnp.where((rightward == 1) & (block == to), nz, block)
        return remote(
            pbuf.at[block, half],
            qbuf.at[into, half],
            sum_send.at[block, half],
            sum_recv.at[into, half],
            (x, to, s),
        )

    for piece in range(plan.micro):

        @pl.when(z + 1 < nz)
        def _():
            along(z, piece, 1, True).start()

        @pl.when(z > 0)
        def _():
            along(z, piece, -1, True).start()

    own_copy = pltpu.make_async_copy(rows_in, line.at[z], local_sem.at[2])
    own_copy.start()
    own_copy.wait()

    def stage_put(index):
        block = nearest(z, index, nz)
        for piece in range(plan.micro):

            @pl.when(block < z)
            def _():
                along(block, piece, 1, False).wait_recv()

                @pl.when(z + 1 < nz)
                def _():
                    along(block, piece, 1, False).start()

            @pl.when(block > z)
            def _():
                along(block, piece, -1, False).wait_recv()

                @pl.when(z > 0)
                def _():
                    along(block, piece, -1, False).start()

        def lay(step, _):
            at = pl.ds(pl.multiple_of(step * TILE, TILE), TILE)
            laid = jnp.dot(put[block], line[block, :, at], preferred_element_type=F32)
            sbuf[block, :, :, at] = laid.astype(BF16).reshape(EXP_DEV, slots, TILE)
            return 0

        lax.fori_loop(0, D // TILE, lay, 0)
        for expert in range(EXP_DEV):
            here, copy = dispatch_copy(block, expert)

            @pl.when(here)
            def _():
                pltpu.make_async_copy(
                    sbuf.at[block, expert],
                    xbuf.at[block // 2, own_source],
                    to_recv.at[block // 2, own_source],
                ).start()

            @pl.when(jnp.logical_not(here))
            def _():
                copy.start()

    def stage_expert(index):
        block = nearest(z, index, nz)
        pair = block // 2
        for source in range(plan.sources):
            landed(xbuf.at[pair, source], to_recv.at[pair, source])
        pltpu.make_async_copy(xbuf.at[pair], sent_save.at[pair], save_sem.at[0, pair]).start()
        taken = xbuf[pair].reshape(many, D)

        def middle(step, _):
            at = pl.multiple_of(step * TILE, TILE)
            if backward:
                grad_hidden = lax.dot_general(
                    taken,
                    wdown_v[pl.ds(at, TILE), :],
                    (((1,), (1,)), ((), ())),
                    preferred_element_type=F32,
                )
                gate = gbuf[pair, :, pl.ds(at, TILE)].astype(F32)
                up = gbuf[pair, :, pl.ds(FF + at, TILE)].astype(F32)
                sig = 1.0 / (1.0 + jnp.exp(-gate))
                gs = gate * sig
                grad_gate = grad_hidden * up * (sig + gs * (1.0 - sig))
                gbuf[pair, :, pl.ds(at, TILE)] = grad_gate.astype(BF16)
                gbuf[pair, :, pl.ds(FF + at, TILE)] = (grad_hidden * gs).astype(BF16)
            else:
                gate = jnp.dot(taken, win_v[:, pl.ds(at, TILE)], preferred_element_type=F32)
                up = jnp.dot(taken, win_v[:, pl.ds(FF + at, TILE)], preferred_element_type=F32)
                gbuf[pair, :, pl.ds(at, TILE)] = gate.astype(BF16)
                gbuf[pair, :, pl.ds(FF + at, TILE)] = up.astype(BF16)
                zbuf[pair, :, pl.ds(at, TILE)] = (gate / (1.0 + jnp.exp(-gate)) * up).astype(BF16)
            return 0

        lax.fori_loop(0, FF // TILE, middle, 0)
        if backward:
            pltpu.make_async_copy(gbuf.at[pair], grad_save.at[pair], save_sem.at[1, pair]).start()
        else:
            pltpu.make_async_copy(gbuf.at[pair], gate_up.at[pair], save_sem.at[1, pair]).start()
            pltpu.make_async_copy(zbuf.at[pair], hidden.at[pair], save_sem.at[2, pair]).start()

        def last(step, _):
            half = step // (HALF // TILE)
            at = pl.multiple_of(step * TILE, TILE)
            inside = pl.multiple_of((step % (HALF // TILE)) * TILE, TILE)
            if backward:
                result = lax.dot_general(
                    gbuf[pair],
                    win_v[pl.ds(at, TILE), :],
                    (((1,), (1,)), ((), ())),
                    preferred_element_type=F32,
                )
            else:
                result = jnp.dot(
                    zbuf[pair], wdown_v[:, pl.ds(at, TILE)], preferred_element_type=F32
                )
            ybuf[pair, half, :, :, pl.ds(inside, TILE)] = result.astype(BF16).reshape(
                plan.sources, slots, TILE
            )

            @pl.when(step % (HALF // TILE) == HALF // TILE - 1)
            def _():
                for source in range(plan.sources):
                    here, copy = return_copy(block, half, source)

                    @pl.when(here)
                    def _():
                        pltpu.make_async_copy(
                            ybuf.at[pair, half, source],
                            rbuf.at[block, half, own_expert],
                            back_recv.at[block, half, own_expert],
                        ).start()

                    @pl.when(jnp.logical_not(here))
                    def _():
                        copy.start()

            return 0

        lax.fori_loop(0, D // TILE, last, 0)

    def stage_take(index):
        block = nearest(z, index, nz)
        origin = ((block < z) & (z == nz - 1)) | ((block > z) & (z == 0))
        for half in range(2):
            for expert in range(EXP_DEV):
                landed(rbuf.at[block, half, expert], back_recv.at[block, half, expert])
            got = lax.dot_general(
                take[block],
                rbuf[block, half].reshape(EXP_DEV * slots, HALF),
                (((0,), (0,)), ((), ())),
                preferred_element_type=F32,
            )

            @pl.when(block == z)
            def _():
                at = pl.ds(half * HALF, HALF)
                if backward:
                    out[:, at] = got
                else:
                    out[:, at] = base[:, at] + got

            @pl.when(block != z)
            def _():
                pbuf[block, half] = got.astype(BF16)

            @pl.when(origin)
            def _():
                sum_copy(block, half).start()

    def relay(turn):
        lower = z < nz // 2
        first = jnp.where(lower, nz - 1 - z, z)
        early = turn < first
        ahead = jnp.where(early, turn + 1, turn - first + 1)
        rightward = lower == early
        block = jnp.where(rightward, z + ahead, z - ahead)

        @pl.when((z > 0) & (z < nz - 1))
        def _():
            for half in range(2):
                landed(qbuf.at[block, half], sum_recv.at[block, half])
                pbuf[block, half] = (
                    pbuf[block, half].astype(F32) + qbuf[block, half].astype(F32)
                ).astype(BF16)
                sum_copy(block, half).start()

    def body(index, _):
        @pl.when(index < nz)
        def _():
            stage_put(index)

        @pl.when(index == 1)
        def _():
            load_in.wait()
            load_down.wait()
            if backward:
                load_gate.wait()

        before = nearest(z, jnp.clip(index - 1, 0, nz - 1), nz)

        @pl.when((index >= 1) & (index < nz + 1) & (before % 2 == own_turn))
        def _():
            stage_expert(index - 1)

        @pl.when(index == nz + 1)
        def _():
            relay(0)

        @pl.when(index >= 2)
        def _():
            stage_take(index - 2)

        return 0

    lax.fori_loop(0, nz + 2, body, 0)

    def onward(turn, _):
        relay(turn)
        return 0

    lax.fori_loop(1, nz - 1, onward, 0)
    for half in range(2):
        at = pl.ds(half * HALF, HALF)

        @pl.when(z + 1 < nz)
        def _():
            landed(qbuf.at[z, half], sum_recv.at[z, half])
            out[:, at] += qbuf[z, half].astype(F32)

        @pl.when(z > 0)
        def _():
            landed(qbuf.at[nz, half], sum_recv.at[nz, half])
            out[:, at] += qbuf[nz, half].astype(F32)

    def drain(block, _):
        for piece in range(plan.micro):

            @pl.when((block <= z) & (z + 1 < nz))
            def _():
                along(block, piece, 1, False).wait_send()

            @pl.when((block >= z) & (z > 0))
            def _():
                along(block, piece, -1, False).wait_send()

        for expert in range(EXP_DEV):
            here, copy = dispatch_copy(block, expert)

            @pl.when(jnp.logical_not(here))
            def _():
                copy.wait_send()

        @pl.when(block % 2 == own_turn)
        def _():
            for half in range(2):
                for source in range(plan.sources):
                    here, copy = return_copy(block, half, source)

                    @pl.when(jnp.logical_not(here))
                    def _():
                        copy.wait_send()

        @pl.when(block != z)
        def _():
            for half in range(2):
                sum_copy(block, half).wait_send()

        return 0

    lax.fori_loop(0, nz, drain, 0)
    for pair in range(plan.blocks):
        pltpu.make_async_copy(xbuf.at[pair], sent_save.at[pair], save_sem.at[0, pair]).wait()
        if backward:
            pltpu.make_async_copy(gbuf.at[pair], grad_save.at[pair], save_sem.at[1, pair]).wait()
        else:
            pltpu.make_async_copy(gbuf.at[pair], gate_up.at[pair], save_sem.at[1, pair]).wait()
            pltpu.make_async_copy(zbuf.at[pair], hidden.at[pair], save_sem.at[2, pair]).wait()


def moe_call(plan, backward, collective_id, rows_in, put, take, w_in, w_down, last):
    nz, blocks, slots, many, sources = plan.nz, plan.blocks, plan.slots, plan.many, plan.sources
    vmem = pl.BlockSpec(memory_space=pltpu.VMEM)
    hbm = pl.BlockSpec(memory_space=pltpu.HBM)
    saved = (blocks, sources, slots, D)
    shape = jax.ShapeDtypeStruct
    outs = [shape((plan.rows, D), F32), shape(saved, BF16), shape((blocks, many, 2 * FF), BF16)]
    if not backward:
        outs.append(shape((blocks, many, FF), BF16))
    return pl.pallas_call(
        functools.partial(moe_kernel, plan, backward),
        out_shape=outs,
        in_specs=[vmem, vmem, vmem, hbm, hbm, hbm if backward else vmem],
        out_specs=[vmem] + [hbm] * (len(outs) - 1),
        scratch_shapes=[
            pltpu.VMEM((nz, plan.rows, D), BF16),
            pltpu.VMEM((nz, EXP_DEV, slots, D), BF16),
            pltpu.VMEM(saved, BF16),
            pltpu.VMEM((blocks, 2, sources, slots, HALF), BF16),
            pltpu.VMEM((nz, 2, EXP_DEV, slots, HALF), BF16),
            pltpu.VMEM((nz, 2, plan.rows, HALF), BF16),
            pltpu.VMEM((nz + 1, 2, plan.rows, HALF), BF16),
            pltpu.VMEM((D, 2 * FF), BF16),
            pltpu.VMEM((FF, D), BF16),
            pltpu.VMEM((blocks, many, 2 * FF), BF16),
            pltpu.VMEM((blocks, many, FF), BF16),
            DMA((nz, plan.micro)),
            DMA((nz, plan.micro)),
            DMA((nz, plan.micro)),
            DMA((nz, EXP_DEV)),
            DMA((blocks, sources)),
            DMA((blocks, 2, sources)),
            DMA((nz, 2, EXP_DEV)),
            DMA((nz, 2)),
            DMA((nz + 1, 2)),
            DMA((4,)),
            DMA((3, blocks)),
        ],
        compiler_params=pltpu.CompilerParams(
            collective_id=collective_id, has_side_effects=True, vmem_limit_bytes=VMEM_LIMIT
        ),
        cost_estimate=pl.CostEstimate(
            flops=100_000_000_000, bytes_accessed=30_000_000, transcendentals=0
        ),
    )(rows_in, put, take, w_in, w_down, last)


def expert_spread(plan, ins, outs, send, recv, pass_send, pass_recv):
    x, z, s = me()
    nx, ns, group = plan.nx, plan.ns, plan.group
    rank = x * ns + s
    own_expert, own_part = rank // group, rank % group
    own = [(layer, k) for layer in range(nx) for k in range(ns // group)]

    def first(expert, which):
        to = expert * group + s % group
        return to == rank, remote(
            ins[which].at[expert],
            outs[which].at[x, s],
            send.at[expert, which],
            recv.at[x, s, which],
            (to // ns, z, to % ns),
        )

    def onward(layer, source, step, which):
        to = own_expert * group + (own_part + step) % group
        return remote(
            outs[which].at[layer, source],
            outs[which].at[layer, source],
            pass_send.at[layer, source, step - 1, which],
            pass_recv.at[layer, source, which],
            (to // ns, z, to % ns),
        )

    def start():
        for which in range(2):
            for expert in range(EXP_DEV):
                here, copy = first(expert, which)

                @pl.when(here)
                def _():
                    pltpu.make_async_copy(
                        ins[which].at[expert], outs[which].at[x, s], recv.at[x, s, which]
                    ).start()

                @pl.when(jnp.logical_not(here))
                def _():
                    copy.start()

    def pass_on():
        for layer, k in own:
            source = k * group + own_part
            for which in range(2):
                landed(outs[which].at[layer, source], recv.at[layer, source, which])
                for step in range(1, group):
                    onward(layer, source, step, which).start()

    def finish():
        for layer, k in own:
            for step in range(1, group):
                source = k * group + (own_part + step) % group
                for which in range(2):
                    landed(outs[which].at[layer, source], pass_recv.at[layer, source, which])
        for which in range(2):
            for expert in range(EXP_DEV):
                here, copy = first(expert, which)

                @pl.when(jnp.logical_not(here))
                def _():
                    copy.wait_send()

        for layer, k in own:
            source = k * group + own_part
            for which in range(2):
                for step in range(1, group):
                    onward(layer, source, step, which).wait_send()

    return start, pass_on, finish


def spread_scratch(plan):
    nx, ns, group = plan.nx, plan.ns, plan.group
    return [
        DMA((EXP_DEV, 2)),
        DMA((nx, ns, 2)),
        DMA((nx, ns, group - 1, 2)),
        DMA((nx, ns, 2)),
    ]


def spread_kernel(plan, *refs):
    greet_plane(plan)
    start, pass_on, finish = expert_spread(plan, refs[:2], refs[2:4], *refs[4:])
    start()
    pass_on()
    finish()


def spread_call(plan, collective_id, gate_up, down):
    hbm = pl.BlockSpec(memory_space=pltpu.HBM)
    outs = [
        jax.ShapeDtypeStruct((plan.nx, plan.ns) + part.shape[1:], BF16) for part in (gate_up, down)
    ]
    return pl.pallas_call(
        functools.partial(spread_kernel, plan),
        out_shape=outs,
        in_specs=[hbm, hbm],
        out_specs=[hbm, hbm],
        scratch_shapes=spread_scratch(plan),
        compiler_params=pltpu.CompilerParams(collective_id=collective_id, has_side_effects=True),
    )(gate_up, down)


def gather_kernel(plan, *refs):
    ins, wide_ins = refs[:2], refs[2:4]
    outs, wide_outs = refs[4:6], refs[6:8]
    line_recv, right, left, copy_sem, plane_recv, to_core, to_x, to_y, spare = refs[8:17]
    x, z, s = me()
    nz = plan.nz
    greet_plane(plan, along=True)
    start, pass_on, finish = expert_spread(plan, wide_ins, wide_outs, *refs[17:])
    size = ins[0].shape[0] // 2
    pieces = [(half, which) for which in range(2) for half in range(2)]
    core = (x, z, s + 1 - 2 * (s % 2))
    across_x = (1 - x, z, s)
    across_y = (x, z, (s + 2) % 4)

    def spot(layer, block, shard, half, which):
        return outs[which].at[layer, block, shard, pl.ds(half * size, size)]

    def along(block, step, half, which, own):
        place = spot(x, block, s, half, which)
        src = ins[which].at[pl.ds(half * size, size)] if own else place
        sem = right if step > 0 else left
        return remote(
            src, place, sem.at[block, half, which], line_recv.at[block, half, which], (x, z + step, s)
        )

    def passed(layer, block, shard, half, which, sem, to):
        place = spot(layer, block, shard, half, which)
        return remote(
            place,
            place,
            sem.at[layer, block, shard // 2, half, which],
            plane_recv.at[layer, block, shard, half, which],
            to,
        )

    def arrived(layer, block, shard, half, which):
        landed(
            spot(layer, block, shard, half, which), plane_recv.at[layer, block, shard, half, which]
        )

    for half, which in pieces:

        @pl.when(z + 1 < nz)
        def _():
            along(z, 1, half, which, True).start()

        @pl.when(z > 0)
        def _():
            along(z, -1, half, which, True).start()

        pltpu.make_async_copy(
            ins[which].at[pl.ds(half * size, size)],
            spot(x, z, s, half, which),
            copy_sem.at[half, which],
        ).start()
    for half, which in pieces:
        pltpu.make_async_copy(
            ins[which].at[pl.ds(half * size, size)],
            spot(x, z, s, half, which),
            copy_sem.at[half, which],
        ).wait()
    start()

    def column(index):
        block = nearest(z, index, nz)
        for half, which in pieces:

            @pl.when(block < z)
            def _():
                along(block, 1, half, which, False).wait_recv()

                @pl.when(z + 1 < nz)
                def _():
                    along(block, 1, half, which, False).start()

            @pl.when(block > z)
            def _():
                along(block, -1, half, which, False).wait_recv()

                @pl.when(z > 0)
                def _():
                    along(block, -1, half, which, False).start()

            passed(x, block, s, half, which, to_x, across_x).start()
            passed(x, block, s, half, which, to_y, across_y).start()
            passed(x, block, s, half, which, to_core, core).start()

    def neighbours(index):
        block = nearest(z, index, nz)
        over = (s + 2) % 4
        for half, which in pieces:
            arrived(1 - x, block, s, half, which)
            if half == 0:
                passed(1 - x, block, s, half, which, to_y, across_y).start()
            passed(1 - x, block, s, half, which, to_core, core).start()
            arrived(x, block, over, half, which)
            if half == 1:
                passed(x, block, over, half, which, to_x, across_x).start()
            passed(x, block, over, half, which, to_core, core).start()

    def opposite(index):
        block = nearest(z, index, nz)
        over = (s + 2) % 4
        for half, which in pieces:
            arrived(1 - x, block, over, half, which)
            passed(1 - x, block, over, half, which, to_core, core).start()

    def body(index, _):
        @pl.when(index < nz)
        def _():
            column(index)

        @pl.when((index >= 1) & (index < nz + 1))
        def _():
            neighbours(index - 1)

        @pl.when(index >= 2)
        def _():
            opposite(index - 2)

        return 0

    lax.fori_loop(0, nz + 2, body, 0)
    pass_on()

    def drain(block, _):
        other = s + 1 - 2 * (s % 2)
        over = (s + 2) % 4
        for half, which in pieces:
            for layer in range(2):
                for row in range(2):
                    arrived(layer, block, row * 2 + other % 2, half, which)
                    passed(layer, block, row * 2 + s % 2, half, which, to_core, core).wait_send()

            @pl.when((block <= z) & (z + 1 < nz))
            def _():
                along(block, 1, half, which, False).wait_send()

            @pl.when((block >= z) & (z > 0))
            def _():
                along(block, -1, half, which, False).wait_send()

            passed(x, block, s, half, which, to_x, across_x).wait_send()
            passed(x, block, s, half, which, to_y, across_y).wait_send()
            if half == 0:
                passed(1 - x, block, s, half, which, to_y, across_y).wait_send()
            else:
                passed(x, block, over, half, which, to_x, across_x).wait_send()
        return 0

    lax.fori_loop(0, nz, drain, 0)
    finish()


def gather_call(plan, collective_id, attention, experts):
    hbm = pl.BlockSpec(memory_space=pltpu.HBM)
    nx, nz, ns = plan.nx, plan.nz, plan.ns
    outs = [jax.ShapeDtypeStruct((nx, nz, ns) + part.shape, BF16) for part in attention]
    outs += [jax.ShapeDtypeStruct((nx, ns) + part.shape[1:], BF16) for part in experts]
    return pl.pallas_call(
        functools.partial(gather_kernel, plan),
        out_shape=outs,
        in_specs=[hbm] * 4,
        out_specs=[hbm] * 4,
        scratch_shapes=[
            DMA((nz, 2, 2)),
            DMA((nz, 2, 2)),
            DMA((nz, 2, 2)),
            DMA((2, 2)),
            DMA((nx, nz, ns, 2, 2)),
            DMA((nx, nz, 2, 2, 2)),
            DMA((nx, nz, 2, 2, 2)),
            DMA((nx, nz, 2, 2, 2)),
            DMA((1,)),
        ]
        + spread_scratch(plan),
        compiler_params=pltpu.CompilerParams(collective_id=collective_id, has_side_effects=True),
    )(*attention, *experts)


def expert_collect(plan, ins, outs, parts, stage, load, swap_send, swap_recv, send, recv):
    x, z, s = me()
    ns, group = plan.ns, plan.group
    rank = x * ns + s
    own_expert, own_part = rank // group, rank % group
    order = [(k, kind) for kind in range(len(ins)) for k in range(ns // group)]

    def swap(k, step, kind):
        part_to = (own_part + step) % group
        to = own_expert * group + part_to
        return remote(
            ins[kind].at[k * group + part_to],
            parts[kind].at[step - 1, k],
            swap_send.at[step - 1, k, kind],
            swap_recv.at[step - 1, k, kind],
            (to // ns, z, to % ns),
        )

    def own(k, kind):
        return pltpu.make_async_copy(
            ins[kind].at[k * group + own_part], stage[kind].at[k], load.at[k, kind]
        )

    def home(k, kind):
        layer, which = kind // 2, kind % 2
        here = (x == layer) & (s == k * group + own_part)
        return here, remote(
            stage[kind].at[k],
            outs[which].at[own_expert],
            send.at[k, kind],
            recv.at[own_expert, which],
            (layer, z, k * group + own_part),
        )

    def start():
        for k, kind in order:
            own(k, kind).start()
            for step in range(1, group):
                swap(k, step, kind).start()

    def add(place):
        k, kind = order[place]
        own(k, kind).wait()
        for step in range(1, group):
            swap(k, step, kind).wait_recv()
        total = stage[kind][k].astype(F32)
        for step in range(1, group):
            total += parts[kind][step - 1, k].astype(F32)
        stage[kind][k] = total.astype(BF16)
        here, copy = home(k, kind)

        @pl.when(here)
        def _():
            which = kind % 2
            pltpu.make_async_copy(
                stage[kind].at[k], outs[which].at[own_expert], recv.at[own_expert, which]
            ).start()

        @pl.when(jnp.logical_not(here))
        def _():
            copy.start()

    def finish():
        for which in range(2):
            for expert in range(EXP_DEV):
                landed(outs[which].at[expert], recv.at[expert, which])
        for k, kind in order:
            for step in range(1, group):
                swap(k, step, kind).wait_send()
            here, copy = home(k, kind)

            @pl.when(jnp.logical_not(here))
            def _():
                copy.wait_send()

    return len(order), start, add, finish


def collect_scratch(plan, values):
    group, each, kinds = plan.group, plan.ns // plan.group, len(values)
    return (
        [pltpu.VMEM((group - 1, each) + part.shape[1:], BF16) for part in values]
        + [pltpu.VMEM((each,) + part.shape[1:], BF16) for part in values]
        + [
            DMA((each, kinds)),
            DMA((group - 1, each, kinds)),
            DMA((group - 1, each, kinds)),
            DMA((each, kinds)),
            DMA((EXP_DEV, 2)),
        ]
    )


def collect_kernel(plan, *refs):
    kinds = 2 * plan.nx
    ins, outs = refs[:kinds], refs[kinds : kinds + 2]
    parts, stage = refs[kinds + 2 : 2 * kinds + 2], refs[2 * kinds + 2 : 3 * kinds + 2]
    greet_plane(plan)
    count, start, add, finish = expert_collect(
        plan, ins, outs, parts, stage, *refs[3 * kinds + 2 :]
    )
    start()
    for place in range(count):
        add(place)
    finish()


def collect_call(plan, collective_id, terms):
    ns = plan.ns
    hbm = pl.BlockSpec(memory_space=pltpu.HBM)
    values = [part.reshape(ns, part.shape[0] // ns, D) for layer in terms for part in layer]
    return pl.pallas_call(
        functools.partial(collect_kernel, plan),
        out_shape=[jax.ShapeDtypeStruct((EXP_DEV,) + part.shape[1:], BF16) for part in values[:2]],
        in_specs=[hbm] * len(values),
        out_specs=[hbm, hbm],
        scratch_shapes=collect_scratch(plan, values),
        compiler_params=pltpu.CompilerParams(
            collective_id=collective_id, has_side_effects=True, vmem_limit_bytes=VMEM_LIMIT
        ),
    )(*values)


def reduce_kernel(plan, *refs):
    grads, wide_ins = (refs[0:2], refs[2:4]), refs[4:8]
    outs, wide_outs = refs[8:10], refs[10:12]
    scratch = refs[12:]
    mine, given, x_one, y_one, y_two, x_two, chain = (scratch[2 * i : 2 * i + 2] for i in range(7))
    (
        load_sem,
        core_send,
        core_recv,
        x_one_send,
        x_one_recv,
        y_one_send,
        y_one_recv,
        x_two_send,
        x_two_recv,
        y_two_send,
        y_two_recv,
        chain_send,
        chain_recv,
    ) = scratch[14:27]
    parts, stage = scratch[27:31], scratch[31:35]
    x, z, s = me()
    nz = plan.nz
    row, side = s // 2, s % 2
    core = (x, z, s + 1 - 2 * side)
    across_x = (1 - x, z, s)
    across_y = (x, z, (s + 2) % 4)
    size = grads[0][0].shape[2] // 2
    greet_plane(plan, along=True)
    count, start, add, finish = expert_collect(plan, wide_ins, wide_outs, parts, stage, *scratch[35:])
    both = range(2)
    low, high = pl.ds(0, size), pl.ds(size, size)

    def load(layer, block, to_row, which):
        return pltpu.make_async_copy(
            grads[layer][which].at[block, to_row * 2 + side],
            mine[which].at[layer, block, to_row],
            load_sem.at[layer, block, to_row, which],
        )

    def give(layer, block, to_row, which):
        return remote(
            grads[layer][which].at[block, to_row * 2 + 1 - side],
            given[which].at[layer, block, to_row],
            core_send.at[layer, block, to_row, which],
            core_recv.at[layer, block, to_row, which],
            core,
        )

    def send_x_one(block, to_row, which):
        return remote(
            mine[which].at[1 - x, block, to_row, low],
            x_one[which].at[block, to_row],
            x_one_send.at[block, to_row, which],
            x_one_recv.at[block, to_row, which],
            across_x,
        )

    def send_y_one(layer, block, which):
        return remote(
            mine[which].at[layer, block, 1 - row, high],
            y_one[which].at[layer, block],
            y_one_send.at[layer, block, which],
            y_one_recv.at[layer, block, which],
            across_y,
        )

    def send_y_two(block, which):
        return remote(
            mine[which].at[x, block, 1 - row, low],
            y_two[which].at[block],
            y_two_send.at[block, which],
            y_two_recv.at[block, which],
            across_y,
        )

    def send_x_two(block, which):
        return remote(
            mine[which].at[1 - x, block, row, high],
            x_two[which].at[block],
            x_two_send.at[block, which],
            x_two_recv.at[block, which],
            across_x,
        )

    def send_chain(block, which):
        rightward = (block > z).astype(jnp.int32)
        to = z - 1 + 2 * rightward
        into = jnp.where((rightward == 1) & (block == to), nz, block)
        return remote(
            mine[which].at[x, block, row],
            chain[which].at[into],
            chain_send.at[block, which],
            chain_recv.at[into, which],
            (x, to, s),
        )

    def gain(target, at, other):
        target[at] = (target[at].astype(F32) + other.astype(F32)).astype(BF16)

    def begin(index, _):
        block = nearest(z, nz - 1 - index, nz)
        for which in both:
            for layer in both:
                for to_row in both:
                    load(layer, block, to_row, which).start()
                    give(layer, block, to_row, which).start()
        return 0

    def stage_core(index):
        block = nearest(z, nz - 1 - index, nz)
        for which in both:
            for layer in both:
                for to_row in both:
                    load(layer, block, to_row, which).wait()
                    give(layer, block, to_row, which).wait_recv()
                    gain(mine[which], (layer, block, to_row), given[which][layer, block, to_row])
            for to_row in both:
                send_x_one(block, to_row, which).start()
            for layer in both:
                send_y_one(layer, block, which).start()

    def stage_first(index):
        block = nearest(z, nz - 1 - index, nz)
        for which in both:
            for to_row in both:
                send_x_one(block, to_row, which).wait_recv()
                gain(mine[which], (x, block, to_row, low), x_one[which][block, to_row])
            send_y_two(block, which).start()
            for layer in both:
                send_y_one(layer, block, which).wait_recv()
                gain(mine[which], (layer, block, row, high), y_one[which][layer, block])
            send_x_two(block, which).start()

    def stage_second(index):
        block = nearest(z, nz - 1 - index, nz)
        origin = ((block < z) & (z == nz - 1)) | ((block > z) & (z == 0))
        for which in both:
            send_y_two(block, which).wait_recv()
            gain(mine[which], (x, block, row, low), y_two[which][block])
            send_x_two(block, which).wait_recv()
            gain(mine[which], (x, block, row, high), x_two[which][block])

            @pl.when(origin)
            def _():
                send_chain(block, which).start()

    start()
    lax.fori_loop(0, nz, begin, 0)
    each = -(-count // nz)

    for index in range(nz + 2):
        if index < nz:
            stage_core(index)
            for place in range(index * each, min(count, (index + 1) * each)):
                add(place)
        if 1 <= index < nz + 1:
            stage_first(index - 1)
        if index >= 2:
            stage_second(index - 2)

    def relay(turn, _):
        lower = z < nz // 2
        first = jnp.where(lower, nz - 1 - z, z)
        early = turn < first
        ahead = jnp.where(early, first - turn, nz - 1 - turn)
        rightward = lower == early
        block = jnp.where(rightward, z + ahead, z - ahead)

        @pl.when((z > 0) & (z < nz - 1))
        def _():
            for which in both:
                landed(chain[which].at[block], chain_recv.at[block, which])
                gain(mine[which], (x, block, row), chain[which][block])
                send_chain(block, which).start()

        return 0

    lax.fori_loop(0, nz - 1, relay, 0)
    for which in both:
        outs[which][...] = mine[which][x, z, row].astype(F32)

        @pl.when(z + 1 < nz)
        def _():
            landed(chain[which].at[z], chain_recv.at[z, which])
            outs[which][...] += chain[which][z].astype(F32)

        @pl.when(z > 0)
        def _():
            landed(chain[which].at[nz], chain_recv.at[nz, which])
            outs[which][...] += chain[which][nz].astype(F32)

    def drain(block, _):
        for which in both:
            for layer in both:
                for to_row in both:
                    give(layer, block, to_row, which).wait_send()
                send_y_one(layer, block, which).wait_send()
            for to_row in both:
                send_x_one(block, to_row, which).wait_send()
            send_y_two(block, which).wait_send()
            send_x_two(block, which).wait_send()

            @pl.when(block != z)
            def _():
                send_chain(block, which).wait_send()

        return 0

    lax.fori_loop(0, nz, drain, 0)
    finish()


def reduce_call(plan, collective_id, attention, terms):
    nx, nz, ns = plan.nx, plan.nz, plan.ns
    hbm = pl.BlockSpec(memory_space=pltpu.HBM)
    vmem = pl.BlockSpec(memory_space=pltpu.VMEM)
    grads = [part.reshape(nz, ns, -1, part.shape[1]) for layer in attention for part in layer]
    values = [part.reshape(ns, part.shape[0] // ns, D) for layer in terms for part in layer]
    sizes = [part.shape[2:] for part in grads[:2]]
    halves = [(rows // 2, width) for rows, width in sizes]
    return pl.pallas_call(
        functools.partial(reduce_kernel, plan),
        out_shape=[jax.ShapeDtypeStruct(size, F32) for size in sizes]
        + [jax.ShapeDtypeStruct((EXP_DEV,) + part.shape[1:], BF16) for part in values[:2]],
        in_specs=[hbm] * 8,
        out_specs=[vmem, vmem, hbm, hbm],
        scratch_shapes=[pltpu.VMEM((nx, nz, 2) + size, BF16) for size in sizes]
        + [pltpu.VMEM((nx, nz, 2) + size, BF16) for size in sizes]
        + [pltpu.VMEM((nz, 2) + size, BF16) for size in halves]
        + [pltpu.VMEM((nx, nz) + size, BF16) for size in halves]
        + [pltpu.VMEM((nz,) + size, BF16) for size in halves]
        + [pltpu.VMEM((nz,) + size, BF16) for size in halves]
        + [pltpu.VMEM((nz + 1,) + size, BF16) for size in sizes]
        + [
            DMA((nx, nz, 2, 2)),
            DMA((nx, nz, 2, 2)),
            DMA((nx, nz, 2, 2)),
            DMA((nz, 2, 2)),
            DMA((nz, 2, 2)),
            DMA((nx, nz, 2)),
            DMA((nx, nz, 2)),
            DMA((nz, 2)),
            DMA((nz, 2)),
            DMA((nz, 2)),
            DMA((nz, 2)),
            DMA((nz, 2)),
            DMA((nz + 1, 2)),
        ]
        + collect_scratch(plan, values),
        compiler_params=pltpu.CompilerParams(
            collective_id=collective_id, has_side_effects=True, vmem_limit_bytes=VMEM_LIMIT
        ),
    )(*grads, *values)


def rotate(values, cosine, sine_table):
    width_half = values.shape[-1] // 2
    first_part = values[..., :width_half]
    second_part = values[..., width_half:]
    return jnp.concatenate(
        [
            first_part * cosine - second_part * sine_table,
            second_part * cosine + first_part * sine_table,
        ],
        axis=-1,
    )


def norm_forward(hidden, gain_row):
    inverse = lax.rsqrt(jnp.mean(hidden * hidden, axis=-1, keepdims=True) + epsilon)
    return (hidden * inverse * gain_row, inverse)


def norm_backward(hidden, inverse, gain_row, grad_normed):
    scaled = grad_normed * gain_row
    gain_term = jnp.sum(grad_normed * hidden * inverse, axis=0)
    row_inner = jnp.mean(scaled * hidden, axis=-1, keepdims=True)
    return (inverse * scaled - hidden * inverse * inverse * inverse * row_inner, gain_term)


def slot_tables(plan, routes, gates):
    experts, nz = plan.experts, plan.nz
    named = routes[..., None] == jnp.arange(experts, dtype=jnp.int32)
    gate = jnp.sum(jnp.where(named, gates[..., None], 0.0), axis=2)
    named = jnp.any(named, axis=2)
    earlier = jnp.tril(jnp.ones((plan.tokens, plan.tokens), BF16), -1)
    rank = jnp.einsum("ut,mte->mue", earlier, named.astype(BF16), preferred_element_type=F32)
    table = jnp.stack([jnp.where(named, rank, -1.0), gate])
    table = table.reshape(2, plan.micro, plan.tokens, nz, EXP_DEV).transpose(3, 0, 1, 4, 2)
    table = lax.all_to_all(table, "expert", split_axis=0, concat_axis=0, tiled=True)
    rank, gate = table[:, 0], table[:, 1]
    first = jnp.arange(plan.micro, dtype=F32)[:, None, None] * plan.capacity
    place = jnp.where(rank >= 0, rank + first, -1.0).transpose(0, 2, 1, 3)
    hit = place[:, :, None] == jnp.arange(plan.slots, dtype=F32)[:, None, None]
    shape = (nz, EXP_DEV * plan.slots, plan.rows)
    one = hit.astype(BF16).reshape(shape)
    weighted = jnp.where(hit, gate.transpose(0, 2, 1, 3)[:, :, None], 0.0)
    weighted = weighted.astype(BF16).reshape(shape)
    return one, weighted


def shards(
    inputs,
    segments,
    routes,
    gate_weights,
    query_weight,
    key_value_weight,
    output_weight,
    norm_gains,
    expert_gate_up,
    expert_down,
    cotangent,
):
    section = lax.axis_index("section")
    shard_index = lax.axis_index("shard")
    tokens = inputs.shape[1]
    plan = Plan((lax.axis_size("section"), lax.axis_size("expert"), lax.axis_size("shard")), tokens)
    micro, rows, layers = plan.micro, plan.rows, plan.nx
    length = tokens * plan.ns

    def mine(value):
        return lax.dynamic_slice_in_dim(value, section * micro, micro, 0)

    paired = plan.nx == 2 and plan.ns == 4 and query_weight.shape[1] % 32 == 0
    gain_columns = jnp.pad(norm_gains[0].T, ((0, 0), (0, 126)))
    attention_weights = (
        jnp.concatenate([query_weight[0], key_value_weight[0], gain_columns], axis=1).astype(BF16),
        output_weight[0].astype(BF16),
    )
    expert_weights = (expert_gate_up[0].astype(BF16), expert_down[0].astype(BF16))
    if paired:
        weight_in, weight_o, wide_in, wide_down = gather_call(
            plan, 1, attention_weights, expert_weights
        )
    else:
        weight_in, weight_o = (
            lax.all_gather(part, ("section", "expert", "shard"), axis=0, tiled=True)
            for part in attention_weights
        )
        wide_in, wide_down = spread_call(plan, 1, *expert_weights)
    weight_in = weight_in.reshape(layers, D, -1)
    weight_o = weight_o.reshape(layers, WQ, D)
    gains = weight_in[:, :, WQ + 2 * WK : WQ + 2 * WK + 2].transpose(0, 2, 1).astype(F32)
    wide_in = wide_in.reshape(layers, D, 2 * FF)
    wide_down = wide_down.reshape(layers, FF, D)
    one, weighted = slot_tables(plan, mine(routes), mine(gate_weights))

    offset = shard_index * tokens
    position = (offset + jnp.arange(tokens, dtype=jnp.int32)).astype(F32)
    frequency = rope_base ** (-jnp.arange(HD // 2, dtype=F32) / (HD // 2))
    angles = position[:, None] * frequency[None, :]
    cosine = jnp.cos(angles)[:, None, :]
    sine_table = jnp.sin(angles)[:, None, :]
    segment_all = mine(segments)[:, 0]
    segment_own = lax.dynamic_slice_in_dim(segment_all, offset, tokens, 1)
    query_place = offset + jnp.arange(tokens, dtype=jnp.int32)
    key_place = jnp.arange(length, dtype=jnp.int32)
    allowed = (segment_own[:, :, None] == segment_all[:, None, :]) & (
        query_place[:, None] >= key_place[None, :]
    )
    allowed = jnp.tile(allowed, (1, GROUP, 1))[:, None]

    def stack_heads(values):
        return (
            values.reshape(micro, tokens, KV_HEADS, GROUP, HD)
            .transpose(0, 2, 3, 1, 4)
            .reshape(micro, KV_HEADS, GROUP * tokens, HD)
        )

    def unstack_heads(values):
        return (
            values.reshape(micro, KV_HEADS, GROUP, tokens, HD)
            .transpose(0, 3, 1, 2, 4)
            .reshape(micro, tokens, HEADS, HD)
        )

    def split_kv(all_kv):
        key_rows = all_kv[..., :WK].reshape(micro, length, KV_HEADS, HD)
        value_rows = all_kv[..., WK:].reshape(micro, length, KV_HEADS, HD)
        return key_rows, value_rows

    def score(stacked, key_rows):
        raw = jnp.einsum("mhqd,mkhd->mhqk", stacked, key_rows, preferred_element_type=F32)
        return jnp.where(allowed, raw * SCALE, -1e30)

    def attend_forward(layer, start):
        normed, inverse = norm_forward(start, gains[layer, 0])
        low = normed.astype(BF16)
        projected = jnp.dot(low, weight_in[layer], preferred_element_type=F32)
        queries, keys_values = projected[:, :WQ], projected[:, WQ : WQ + 2 * WK]
        queries_low = rotate(
            queries.reshape(micro, tokens, HEADS, HD), cosine, sine_table
        ).astype(BF16)
        key_rot = rotate(
            keys_values[:, :WK].reshape(micro, tokens, KV_HEADS, HD), cosine, sine_table
        ).reshape(rows, WK)
        local_kv = jnp.concatenate([key_rot, keys_values[:, WK:]], axis=1).astype(BF16)
        local_kv = local_kv.reshape(micro, tokens, 2 * WK)
        all_kv = jnp.stack(
            [lax.all_gather(local_kv[i], "shard", axis=0, tiled=True) for i in range(micro)]
        )
        stacked = stack_heads(queries_low)
        key_rows, value_rows = split_kv(all_kv)
        scores = score(stacked, key_rows)
        row_max = jnp.max(scores, axis=-1, keepdims=True)
        weights = jnp.exp(scores - row_max)
        row_sum = jnp.sum(weights, axis=-1, keepdims=True)
        probs = (weights / row_sum).astype(BF16)
        mixed = jnp.einsum("mhqk,mkhd->mhqd", probs, value_rows, preferred_element_type=F32)
        mixed_low = unstack_heads(mixed.astype(BF16)).reshape(rows, WQ)
        middle = start + jnp.dot(mixed_low, weight_o[layer], preferred_element_type=F32)
        return middle, (start, inverse, low, stacked, all_kv, row_max, row_sum, mixed_low)

    def attend_backward(layer, saved, grad_middle):
        start, inverse, low, stacked, all_kv, row_max, row_sum, mixed_low = saved
        branch = grad_middle.astype(BF16)
        out_term = jnp.einsum("tq,td->qd", mixed_low, branch, preferred_element_type=F32)
        out_term = out_term.astype(BF16)
        grad_mixed = jnp.einsum(
            "td,qd->tq", branch, weight_o[layer], preferred_element_type=F32
        ).astype(BF16)
        grad_stacked = stack_heads(grad_mixed)
        key_rows, value_rows = split_kv(all_kv)
        scores = score(stacked, key_rows)
        probs = jnp.exp(scores - row_max) / row_sum
        grad_probs = jnp.einsum(
            "mhqd,mkhd->mhqk", grad_stacked, value_rows, preferred_element_type=F32
        )
        inner = jnp.sum(grad_probs * probs, axis=-1, keepdims=True)
        grad_raw = (probs * (grad_probs - inner) * SCALE).astype(BF16)
        grad_queries = jnp.einsum(
            "mhqk,mkhd->mhqd", grad_raw, key_rows, preferred_element_type=F32
        )
        grad_keys = jnp.einsum("mhqk,mhqd->mkhd", grad_raw, stacked, preferred_element_type=F32)
        grad_values = jnp.einsum(
            "mhqk,mhqd->mkhd", probs.astype(BF16), grad_stacked, preferred_element_type=F32
        )
        partial = jnp.concatenate(
            [grad_keys.reshape(micro, length, WK), grad_values.reshape(micro, length, WK)], axis=2
        ).astype(BF16)
        grad_kv = jnp.concatenate(
            [
                lax.psum_scatter(partial[i], "shard", scatter_dimension=0, tiled=True)
                for i in range(micro)
            ]
        ).astype(F32)
        grad_q_low = (
            rotate(unstack_heads(grad_queries), cosine, -sine_table).reshape(rows, WQ).astype(BF16)
        )
        grad_k = rotate(
            grad_kv[:, :WK].reshape(micro, tokens, KV_HEADS, HD), cosine, -sine_table
        ).reshape(rows, WK)
        grad_kv_low = jnp.concatenate([grad_k, grad_kv[:, WK:]], axis=1).astype(BF16)
        both = jnp.concatenate([grad_q_low, grad_kv_low], axis=1)
        in_term = jnp.einsum("td,tq->dq", low, both, preferred_element_type=F32).astype(BF16)
        grad_normed = jnp.einsum(
            "tq,dq->td", both, weight_in[layer, :, : WQ + 2 * WK], preferred_element_type=F32
        )
        grad_from, gain_term = norm_backward(start, inverse, gains[layer, 0], grad_normed)
        return grad_middle + grad_from, (in_term, out_term, gain_term)

    def gathered(in_term, out_term, gain_term):
        columns = jnp.pad(gain_term.T, ((0, 0), (0, 126))).astype(BF16)
        return jnp.concatenate([in_term, columns], axis=1), out_term

    hidden = mine(inputs).reshape(rows, D).astype(F32)
    kept = []
    for layer in range(layers):
        if layer > 0:
            hidden = hidden.astype(BF16).astype(F32)
        middle, saved = attend_forward(layer, hidden)
        normed, inverse = norm_forward(middle, gains[layer, 1])
        hidden, sent, gate_up, hidden_low = moe_call(
            plan,
            False,
            2 + layer,
            normed.astype(BF16),
            one,
            weighted,
            wide_in[layer],
            wide_down[layer],
            middle,
        )
        kept.append((saved, middle, inverse, sent, gate_up, hidden_low))
    output = hidden.reshape(micro, tokens, D)

    grad = mine(cotangent).reshape(rows, D)
    attention_terms = [None] * layers
    expert_terms = [None] * layers
    for layer in reversed(range(layers)):
        saved, middle, inverse, sent, gate_up, hidden_low = kept[layer]
        grad_low = grad.astype(BF16)
        grad_out = grad_low.astype(F32)
        grad_moe, grad_sent, grad_both = moe_call(
            plan,
            True,
            2 + layers + layer,
            grad_low,
            weighted,
            one,
            wide_in[layer],
            wide_down[layer],
            gate_up,
        )
        in_term = jnp.einsum(
            "rd,rf->df",
            sent.reshape(-1, D),
            grad_both.reshape(-1, 2 * FF),
            preferred_element_type=F32,
        ).astype(BF16)
        down_term = jnp.einsum(
            "rf,rd->fd",
            hidden_low.reshape(-1, FF),
            grad_sent.reshape(-1, D),
            preferred_element_type=F32,
        ).astype(BF16)
        expert_terms[layer] = (in_term, down_term)
        grad_from, gain_two = norm_backward(middle, inverse, gains[layer, 1], grad_moe)
        grad, terms = attend_backward(layer, saved, grad_out + grad_from)
        attention_terms[layer] = gathered(
            terms[0], terms[1], jnp.stack([terms[2], gain_two])
        )
    input_grad = grad.reshape(micro, tokens, D)

    if paired:
        in_grad, output_weight_grad, gate_up_grad, down_grad = reduce_call(
            plan, 2 + 2 * layers, attention_terms, expert_terms
        )
    else:
        gate_up_grad, down_grad = collect_call(plan, 2 + 2 * layers, expert_terms)
        in_grad, output_weight_grad = (
            lax.psum_scatter(
                jnp.concatenate([terms[i] for terms in attention_terms]),
                ("section", "expert", "shard"),
                scatter_dimension=0,
                tiled=True,
            )
            for i in range(2)
        )
    query_grad, key_value_grad, gain_grad, output_weight_grad, gate_up_grad, down_grad = (
        part.astype(F32)[None]
        for part in (
            in_grad[:, :WQ],
            in_grad[:, WQ : WQ + 2 * WK],
            in_grad[:, WQ + 2 * WK : WQ + 2 * WK + 2].T,
            output_weight_grad,
            gate_up_grad,
            down_grad,
        )
    )
    return (
        output,
        input_grad,
        query_grad,
        key_value_grad,
        output_weight_grad,
        gain_grad,
        gate_up_grad,
        down_grad,
    )


def solution(mesh):
    placed = (
        P(None, ("expert", "shard"), None),
        P(None, "expert", None),
        P(None, ("expert", "shard"), None),
        P(None, ("expert", "shard"), None),
        P("section", ("expert", "shard"), None),
        P("section", ("expert", "shard"), None),
        P("section", ("expert", "shard"), None),
        P("section", None, ("expert", "shard")),
        P("section", "expert", "shard", None),
        P("section", "expert", "shard", None),
        P(None, ("expert", "shard"), None),
    )
    return jax.shard_map(
        shards,
        mesh=mesh,
        in_specs=placed,
        out_specs=(
            P("section", ("expert", "shard"), None),
            P("section", ("expert", "shard"), None),
            P("section", ("expert", "shard"), None),
            P("section", ("expert", "shard"), None),
            P("section", ("expert", "shard"), None),
            P("section", None, ("expert", "shard")),
            P("section", "expert", "shard", None),
            P("section", "expert", "shard", None),
        ),
        check_vma=False,
    )
```

```python
import functools

import jax
import jax.numpy as jnp
from jax import lax
from jax.experimental import pallas as pl
from jax.experimental.pallas import tpu as pltpu
from jax.sharding import PartitionSpec as P

D = 1536
HEADS = 12
KV_HEADS = 2
HD = 128
FF = 768
TOPK = 4
EXP_DEV = 4
MICRO = 4
GROUP = HEADS // KV_HEADS
PAD = 128
WQ = HEADS * HD
WK = KV_HEADS * HD
PROJ = WQ + 2 * WK
WIN = PROJ + PAD
SCALE = HD ** (-0.5)

epsilon = 1e-06
rope_base = 10000.0

MESH = pl.DeviceIdType.MESH
F32 = jnp.float32
BF16 = jnp.bfloat16
DMA = pltpu.SemaphoreType.DMA
VMEM_LIMIT = 60 * 2**20


class Plan:
    def __init__(self, mesh_shape, tokens):
        self.nx, self.nz, self.ns = mesh_shape
        self.tokens = tokens
        self.micro = MICRO // self.nx
        self.rows = self.micro * tokens
        self.ranks = self.nx * self.ns
        self.group = self.ranks // EXP_DEV
        self.halves = self.group // 2
        self.sources = self.ranks // self.halves
        self.experts = EXP_DEV * self.nz
        self.capacity = 5 * tokens * TOPK // (4 * self.experts)
        self.slots = -(-self.micro * self.capacity // 16) * 16
        self.blocks = self.nz // 2
        self.many = self.sources * self.slots


def me():
    return lax.axis_index("section"), lax.axis_index("expert"), lax.axis_index("shard")


def remote(src, dst, send, recv, device):
    return pltpu.make_async_remote_copy(
        src_ref=src,
        dst_ref=dst,
        send_sem=send,
        recv_sem=recv,
        device_id=device,
        device_id_type=MESH,
    )


def landed(ref, sem):
    pltpu.make_async_copy(ref, ref, sem).wait()


def greet_plane(plan, along=False):
    x, z, s = me()
    barrier = pltpu.get_barrier_semaphore()
    mine = x * plan.ns + s
    for step in range(1, plan.ranks):
        other = (mine + step) % plan.ranks
        pl.semaphore_signal(
            barrier, inc=1, device_id=(other // plan.ns, z, other % plan.ns), device_id_type=MESH
        )
    total = plan.ranks - 1
    if along:
        for step in range(1, plan.nz):
            pl.semaphore_signal(
                barrier, inc=1, device_id=(x, (z + step) % plan.nz, s), device_id_type=MESH
            )
        total += plan.nz - 1
    pl.semaphore_wait(barrier, total)


def nearest(place, index, count):
    left = place
    right = count - 1 - place
    short = jnp.minimum(left, right)
    odd = index % 2
    near = place + (1 - 2 * odd) * ((index + 1) // 2)
    far = jnp.where(left < right, index, count - 1 - index)
    return jnp.where(index <= 2 * short, near, far)


TILE = 256
CUTS = 3
CUT = D // CUTS


def moe_kernel(plan, layer, backward, *refs):
    if backward:
        (rows_in, put, take, w_in, w_down, gate_up, out, sent_save, grad_save) = refs[:9]
        scratch = refs[9:]
    else:
        (rows_in, put, take, w_in, w_down, base, out, sent_save, gate_up, hidden) = refs[:10]
        scratch = refs[10:]
    (
        line,
        sbuf,
        xbuf,
        ybuf,
        rbuf,
        pbuf,
        qbuf,
        win_v,
        wdown_v,
        gbuf,
        zbuf,
        line_recv,
        line_right,
        line_left,
        to_send,
        to_recv,
        back_send,
        back_recv,
        sum_send,
        sum_recv,
        local_sem,
        save_sem,
    ) = scratch
    x, z, s = me()
    nz, ns, slots, many = plan.nz, plan.ns, plan.slots, plan.many
    rank = x * ns + s
    own_expert = rank // plan.group
    own_turn = (rank % plan.group) // plan.halves
    own_half = rank % plan.halves
    part = ns // plan.halves
    own_source = x * part + s // plan.halves
    chunk = plan.tokens

    load_in = pltpu.make_async_copy(w_in.at[layer], win_v, local_sem.at[0])
    load_down = pltpu.make_async_copy(w_down.at[layer], wdown_v, local_sem.at[1])
    load_in.start()
    load_down.start()
    if backward:
        load_gate = pltpu.make_async_copy(gate_up, gbuf, local_sem.at[3])
        load_gate.start()
    greet_plane(plan, along=True)

    def along(block, piece, step, own):
        at = pl.ds(piece * chunk, chunk)
        src = rows_in.at[at] if own else line.at[block, at]
        sem = line_right if step > 0 else line_left
        return remote(
            src,
            line.at[block, at],
            sem.at[block, piece],
            line_recv.at[block, piece],
            (x, z + step, s),
        )

    def owner(block, expert):
        rank_to = expert * plan.group + (block % 2) * plan.halves + s % plan.halves
        return rank_to // ns, rank_to % ns

    def dispatch_copy(block, expert):
        to_x, to_s = owner(block, expert)
        here = (to_x == x) & (to_s == s)
        return here, remote(
            sbuf.at[block, expert],
            xbuf.at[block // 2, own_source],
            to_send.at[block, expert],
            to_recv.at[block // 2, own_source],
            (to_x, z, to_s),
        )

    def return_copy(block, half, source):
        to_x = source // part
        to_s = (source % part) * plan.halves + own_half
        here = (to_x == x) & (to_s == s)
        return here, remote(
            ybuf.at[block // 2, half, source],
            rbuf.at[block, half, own_expert],
            back_send.at[block // 2, half, source],
            back_recv.at[block, half, own_expert],
            (to_x, z, to_s),
        )

    def sum_copy(block, half):
        rightward = (block > z).astype(jnp.int32)
        to = z - 1 + 2 * rightward
        into = jnp.where((rightward == 1) & (block == to), nz, block)
        return remote(
            pbuf.at[block, half],
            qbuf.at[into, half],
            sum_send.at[block, half],
            sum_recv.at[into, half],
            (x, to, s),
        )

    for piece in range(plan.micro):

        @pl.when(z + 1 < nz)
        def _():
            along(z, piece, 1, True).start()

        @pl.when(z > 0)
        def _():
            along(z, piece, -1, True).start()

    own_copy = pltpu.make_async_copy(rows_in, line.at[z], local_sem.at[2])
    own_copy.start()
    own_copy.wait()

    def stage_put(index):
        block = nearest(z, index, nz)
        for piece in range(plan.micro):

            @pl.when(block < z)
            def _():
                along(block, piece, 1, False).wait_recv()

                @pl.when(z + 1 < nz)
                def _():
                    along(block, piece, 1, False).start()

            @pl.when(block > z)
            def _():
                along(block, piece, -1, False).wait_recv()

                @pl.when(z > 0)
                def _():
                    along(block, piece, -1, False).start()

        def lay(step, _):
            at = pl.ds(pl.multiple_of(step * TILE, TILE), TILE)
            laid = jnp.dot(put[block], line[block, :, at], preferred_element_type=F32)
            sbuf[block, :, :, at] = laid.astype(BF16).reshape(EXP_DEV, slots, TILE)
            return 0

        lax.fori_loop(0, D // TILE, lay, 0)
        for expert in range(EXP_DEV):
            here, copy = dispatch_copy(block, expert)

            @pl.when(here)
            def _():
                pltpu.make_async_copy(
                    sbuf.at[block, expert],
                    xbuf.at[block // 2, own_source],
                    to_recv.at[block // 2, own_source],
                ).start()

            @pl.when(jnp.logical_not(here))
            def _():
                copy.start()

    def stage_expert(index):
        block = nearest(z, index, nz)
        pair = block // 2
        for source in range(plan.sources):
            landed(xbuf.at[pair, source], to_recv.at[pair, source])
        pltpu.make_async_copy(xbuf.at[pair], sent_save.at[pair], save_sem.at[0, pair]).start()
        taken = xbuf[pair].reshape(many, D)

        def middle(step, _):
            at = pl.multiple_of(step * TILE, TILE)
            if backward:
                grad_hidden = lax.dot_general(
                    taken,
                    wdown_v[pl.ds(at, TILE), :],
                    (((1,), (1,)), ((), ())),
                    preferred_element_type=F32,
                )
                gate = gbuf[pair, :, pl.ds(at, TILE)].astype(F32)
                up = gbuf[pair, :, pl.ds(FF + at, TILE)].astype(F32)
                sig = 1.0 / (1.0 + jnp.exp(-gate))
                gs = gate * sig
                grad_gate = grad_hidden * up * (sig + gs * (1.0 - sig))
                gbuf[pair, :, pl.ds(at, TILE)] = grad_gate.astype(BF16)
                gbuf[pair, :, pl.ds(FF + at, TILE)] = (grad_hidden * gs).astype(BF16)
            else:
                gate = jnp.dot(taken, win_v[:, pl.ds(at, TILE)], preferred_element_type=F32)
                up = jnp.dot(taken, win_v[:, pl.ds(FF + at, TILE)], preferred_element_type=F32)
                gbuf[pair, :, pl.ds(at, TILE)] = gate.astype(BF16)
                gbuf[pair, :, pl.ds(FF + at, TILE)] = up.astype(BF16)
                zbuf[pair, :, pl.ds(at, TILE)] = (gate / (1.0 + jnp.exp(-gate)) * up).astype(BF16)
            return 0

        lax.fori_loop(0, FF // TILE, middle, 0)
        if backward:
            pltpu.make_async_copy(gbuf.at[pair], grad_save.at[pair], save_sem.at[1, pair]).start()
        else:
            pltpu.make_async_copy(gbuf.at[pair], gate_up.at[pair], save_sem.at[1, pair]).start()
            pltpu.make_async_copy(zbuf.at[pair], hidden.at[pair], save_sem.at[2, pair]).start()

        def last(step, _):
            half = step // (CUT // TILE)
            at = pl.multiple_of(step * TILE, TILE)
            inside = pl.multiple_of((step % (CUT // TILE)) * TILE, TILE)
            if backward:
                result = lax.dot_general(
                    gbuf[pair],
                    win_v[pl.ds(at, TILE), :],
                    (((1,), (1,)), ((), ())),
                    preferred_element_type=F32,
                )
            else:
                result = jnp.dot(
                    zbuf[pair], wdown_v[:, pl.ds(at, TILE)], preferred_element_type=F32
                )
            ybuf[pair, half, :, :, pl.ds(inside, TILE)] = result.astype(BF16).reshape(
                plan.sources, slots, TILE
            )

            return 0

        lax.fori_loop(0, D // TILE, last, 0)

    def give_back(index):
        block = nearest(z, index, nz)
        pair = block // 2
        for half in range(CUTS):
            for source in range(plan.sources):
                here, copy = return_copy(block, half, source)

                @pl.when(here)
                def _():
                    pltpu.make_async_copy(
                        ybuf.at[pair, half, source],
                        rbuf.at[block, half, own_expert],
                        back_recv.at[block, half, own_expert],
                    ).start()

                @pl.when(jnp.logical_not(here))
                def _():
                    copy.start()

    def stage_take(index):
        block = nearest(z, index, nz)
        origin = ((block < z) & (z == nz - 1)) | ((block > z) & (z == 0))
        for half in range(CUTS):
            for expert in range(EXP_DEV):
                landed(rbuf.at[block, half, expert], back_recv.at[block, half, expert])
            got = lax.dot_general(
                take[block],
                rbuf[block, half].reshape(EXP_DEV * slots, CUT),
                (((0,), (0,)), ((), ())),
                preferred_element_type=F32,
            )

            @pl.when(block == z)
            def _():
                at = pl.ds(half * CUT, CUT)
                if backward:
                    out[:, at] = got
                else:
                    out[:, at] = base[:, at] + got

            @pl.when(block != z)
            def _():
                pbuf[block, half] = got.astype(BF16)

            @pl.when(origin)
            def _():
                sum_copy(block, half).start()

    def relay(turn):
        lower = z < nz // 2
        first = jnp.where(lower, nz - 1 - z, z)
        early = turn < first
        ahead = jnp.where(early, first - turn, nz - 1 - turn)
        rightward = lower == early
        block = jnp.where(rightward, z + ahead, z - ahead)

        @pl.when((z > 0) & (z < nz - 1))
        def _():
            for half in range(CUTS):
                landed(qbuf.at[block, half], sum_recv.at[block, half])
                pbuf[block, half] = (
                    pbuf[block, half].astype(F32) + qbuf[block, half].astype(F32)
                ).astype(BF16)
                sum_copy(block, half).start()

    def own_turn_do(index, act):
        @pl.when(nearest(z, index, nz) % 2 == own_turn)
        def _():
            act(index)

    final = nz - 1
    stage_put(0)
    load_in.wait()
    load_down.wait()
    if backward:
        load_gate.wait()
    for index in range(1, nz):
        stage_put(index)
        own_turn_do(index - 1, stage_expert)
        if 1 < index < final:
            own_turn_do(index - 1, give_back)
    for index in range(1, nz - 2):
        stage_take(index)
    own_turn_do(final, stage_expert)
    own_turn_do(final, give_back)
    stage_take(final)
    own_turn_do(final - 1, give_back)
    own_turn_do(0, give_back)
    relay(0)
    stage_take(final - 1)
    stage_take(0)
    for turn in (2, 1) if nz == 4 else range(1, nz - 1):
        relay(turn)
    for half in range(CUTS):
        at = pl.ds(half * CUT, CUT)

        @pl.when(z + 1 < nz)
        def _():
            landed(qbuf.at[z, half], sum_recv.at[z, half])
            out[:, at] += qbuf[z, half].astype(F32)

        @pl.when(z > 0)
        def _():
            landed(qbuf.at[nz, half], sum_recv.at[nz, half])
            out[:, at] += qbuf[nz, half].astype(F32)

    def drain(block, _):
        for piece in range(plan.micro):

            @pl.when((block <= z) & (z + 1 < nz))
            def _():
                along(block, piece, 1, False).wait_send()

            @pl.when((block >= z) & (z > 0))
            def _():
                along(block, piece, -1, False).wait_send()

        for expert in range(EXP_DEV):
            here, copy = dispatch_copy(block, expert)

            @pl.when(jnp.logical_not(here))
            def _():
                copy.wait_send()

        @pl.when(block % 2 == own_turn)
        def _():
            for half in range(CUTS):
                for source in range(plan.sources):
                    here, copy = return_copy(block, half, source)

                    @pl.when(jnp.logical_not(here))
                    def _():
                        copy.wait_send()

        @pl.when(block != z)
        def _():
            for half in range(CUTS):
                sum_copy(block, half).wait_send()

        return 0

    lax.fori_loop(0, nz, drain, 0)
    for pair in range(plan.blocks):
        pltpu.make_async_copy(xbuf.at[pair], sent_save.at[pair], save_sem.at[0, pair]).wait()
        if backward:
            pltpu.make_async_copy(gbuf.at[pair], grad_save.at[pair], save_sem.at[1, pair]).wait()
        else:
            pltpu.make_async_copy(gbuf.at[pair], gate_up.at[pair], save_sem.at[1, pair]).wait()
            pltpu.make_async_copy(zbuf.at[pair], hidden.at[pair], save_sem.at[2, pair]).wait()


def moe_call(plan, layer, backward, collective_id, rows_in, put, take, w_in, w_down, last):
    nz, blocks, slots, many, sources = plan.nz, plan.blocks, plan.slots, plan.many, plan.sources
    vmem = pl.BlockSpec(memory_space=pltpu.VMEM)
    hbm = pl.BlockSpec(memory_space=pltpu.HBM)
    saved = (blocks, sources, slots, D)
    shape = jax.ShapeDtypeStruct
    outs = [shape((plan.rows, D), F32), shape(saved, BF16), shape((blocks, many, 2 * FF), BF16)]
    if not backward:
        outs.append(shape((blocks, many, FF), BF16))
    return pl.pallas_call(
        functools.partial(moe_kernel, plan, layer, backward),
        out_shape=outs,
        in_specs=[vmem, vmem, vmem, hbm, hbm, hbm if backward else vmem],
        out_specs=[vmem] + [hbm] * (len(outs) - 1),
        scratch_shapes=[
            pltpu.VMEM((nz, plan.rows, D), BF16),
            pltpu.VMEM((nz, EXP_DEV, slots, D), BF16),
            pltpu.VMEM(saved, BF16),
            pltpu.VMEM((blocks, CUTS, sources, slots, CUT), BF16),
            pltpu.VMEM((nz, CUTS, EXP_DEV, slots, CUT), BF16),
            pltpu.VMEM((nz, CUTS, plan.rows, CUT), BF16),
            pltpu.VMEM((nz + 1, CUTS, plan.rows, CUT), BF16),
            pltpu.VMEM((D, 2 * FF), BF16),
            pltpu.VMEM((FF, D), BF16),
            pltpu.VMEM((blocks, many, 2 * FF), BF16),
            pltpu.VMEM((blocks, many, FF), BF16),
            DMA((nz, plan.micro)),
            DMA((nz, plan.micro)),
            DMA((nz, plan.micro)),
            DMA((nz, EXP_DEV)),
            DMA((blocks, sources)),
            DMA((blocks, CUTS, sources)),
            DMA((nz, CUTS, EXP_DEV)),
            DMA((nz, CUTS)),
            DMA((nz + 1, CUTS)),
            DMA((4,)),
            DMA((3, blocks)),
        ],
        compiler_params=pltpu.CompilerParams(
            collective_id=collective_id, has_side_effects=True, vmem_limit_bytes=VMEM_LIMIT
        ),
        cost_estimate=pl.CostEstimate(
            flops=100_000_000_000, bytes_accessed=30_000_000, transcendentals=0
        ),
    )(rows_in, put, take, w_in, w_down, last)


def expert_spread(plan, ins, outs, send, recv, pass_send, pass_recv):
    x, z, s = me()
    nx, ns, group = plan.nx, plan.ns, plan.group
    rank = x * ns + s
    own_expert, own_part = rank // group, rank % group
    own = [(layer, k) for layer in range(nx) for k in range(ns // group)]

    def first(expert, which):
        to = expert * group + s % group
        return to == rank, remote(
            ins[which].at[expert],
            outs[which].at[x, s],
            send.at[expert, which],
            recv.at[x, s, which],
            (to // ns, z, to % ns),
        )

    def onward(layer, source, step, which):
        to = own_expert * group + (own_part + step) % group
        return remote(
            outs[which].at[layer, source],
            outs[which].at[layer, source],
            pass_send.at[layer, source, step - 1, which],
            pass_recv.at[layer, source, which],
            (to // ns, z, to % ns),
        )

    def start():
        for which in range(2):
            for expert in range(EXP_DEV):
                here, copy = first(expert, which)

                @pl.when(here)
                def _():
                    pltpu.make_async_copy(
                        ins[which].at[expert], outs[which].at[x, s], recv.at[x, s, which]
                    ).start()

                @pl.when(jnp.logical_not(here))
                def _():
                    copy.start()

    def pass_on():
        for layer, k in own:
            source = k * group + own_part
            for which in range(2):
                landed(outs[which].at[layer, source], recv.at[layer, source, which])
                for step in range(1, group):
                    onward(layer, source, step, which).start()

    def finish():
        for layer, k in own:
            for step in range(1, group):
                source = k * group + (own_part + step) % group
                for which in range(2):
                    landed(outs[which].at[layer, source], pass_recv.at[layer, source, which])
        for which in range(2):
            for expert in range(EXP_DEV):
                here, copy = first(expert, which)

                @pl.when(jnp.logical_not(here))
                def _():
                    copy.wait_send()

        for layer, k in own:
            source = k * group + own_part
            for which in range(2):
                for step in range(1, group):
                    onward(layer, source, step, which).wait_send()

    return start, pass_on, finish


def spread_scratch(plan):
    nx, ns, group = plan.nx, plan.ns, plan.group
    return [
        DMA((EXP_DEV, 2)),
        DMA((nx, ns, 2)),
        DMA((nx, ns, group - 1, 2)),
        DMA((nx, ns, 2)),
    ]


def spread_kernel(plan, *refs):
    greet_plane(plan)
    start, pass_on, finish = expert_spread(plan, refs[:2], refs[2:4], *refs[4:])
    start()
    pass_on()
    finish()


def spread_call(plan, collective_id, gate_up, down):
    hbm = pl.BlockSpec(memory_space=pltpu.HBM)
    vmem = pl.BlockSpec(memory_space=pltpu.VMEM)
    outs = [
        jax.ShapeDtypeStruct((plan.nx, plan.ns) + part.shape[1:], BF16) for part in (gate_up, down)
    ]
    return pl.pallas_call(
        functools.partial(spread_kernel, plan),
        out_shape=outs,
        in_specs=[vmem, vmem],
        out_specs=[hbm, hbm],
        scratch_shapes=spread_scratch(plan),
        compiler_params=pltpu.CompilerParams(
            collective_id=collective_id, has_side_effects=True, vmem_limit_bytes=VMEM_LIMIT
        ),
    )(gate_up, down)


def gather_kernel(plan, *refs):
    piece, wide_ins, out, wide_outs = refs[0], refs[1:3], refs[3], refs[4:6]
    line_recv, right, left, copy_sem, plane_recv, to_core, to_x, to_y = refs[6:14]
    x, z, s = me()
    nz = plan.nz
    over = (s + 2) % 4
    greet_plane(plan, along=True)
    start, pass_on, finish = expert_spread(plan, wide_ins, wide_outs, *refs[14:])
    size = piece.shape[0] // 2
    whole = pl.ds(0, 2 * size)
    parts = (pl.ds(0, size), pl.ds(size, size))
    core = (x, z, s + 1 - 2 * (s % 2))
    across_x = (1 - x, z, s)
    across_y = (x, z, over)

    def along(block, step, own):
        place = out.at[x, block, s]
        sem = right if step > 0 else left
        return remote(
            piece if own else place, place, sem.at[block], line_recv.at[block], (x, z + step, s)
        )

    def passed(layer, block, shard, rows, kind, sem, to, own=False):
        place = out.at[layer, block, shard, rows]
        return remote(
            piece if own else place,
            place,
            sem.at[layer, block, shard // 2],
            plane_recv.at[layer, block, shard, kind],
            to,
        )

    def arrived(layer, block, shard, rows, kind):
        landed(out.at[layer, block, shard, rows], plane_recv.at[layer, block, shard, kind])

    @pl.when(z + 1 < nz)
    def _():
        along(z, 1, True).start()

    @pl.when(z > 0)
    def _():
        along(z, -1, True).start()

    own = pltpu.make_async_copy(piece, out.at[x, z, s], copy_sem.at[0])
    own.start()
    start()

    def column_copies(block, own=False):
        ways = ((to_x, across_x), (to_y, across_y), (to_core, core))
        return [passed(x, block, s, whole, 0, sem, to, own) for sem, to in ways]

    def column(index):
        block = nearest(z, index, nz)

        @pl.when(block < z)
        def _():
            along(block, 1, False).wait_recv()

            @pl.when(z + 1 < nz)
            def _():
                along(block, 1, False).start()

        @pl.when(block > z)
        def _():
            along(block, -1, False).wait_recv()

            @pl.when(z > 0)
            def _():
                along(block, -1, False).start()

        @pl.when(block == z)
        def _():
            for copy in column_copies(block, True):
                copy.start()

        @pl.when(block != z)
        def _():
            for copy in column_copies(block):
                copy.start()

    def neighbour_copies(block):
        return [
            passed(1 - x, block, s, parts[0], 1, to_y, across_y),
            passed(1 - x, block, s, whole, 0, to_core, core),
            passed(x, block, over, parts[1], 2, to_x, across_x),
            passed(x, block, over, whole, 0, to_core, core),
        ]

    def neighbours(index):
        block = nearest(z, index, nz)
        copies = neighbour_copies(block)
        arrived(1 - x, block, s, whole, 0)
        copies[0].start()
        copies[1].start()
        arrived(x, block, over, whole, 0)
        copies[2].start()
        copies[3].start()

    def opposite(index):
        block = nearest(z, index, nz)
        arrived(1 - x, block, over, parts[0], 1)
        arrived(1 - x, block, over, parts[1], 2)
        passed(1 - x, block, over, whole, 0, to_core, core).start()

    def each(act):
        def body(index, _):
            act(index)
            return 0

        lax.fori_loop(0, nz, body, 0)

    each(column)
    each(neighbours)
    each(opposite)
    own.wait()
    pass_on()

    def drain(block, _):
        other = s + 1 - 2 * (s % 2)
        for layer in range(2):
            for row in range(2):
                arrived(layer, block, row * 2 + other % 2, whole, 0)

        @pl.when((block <= z) & (z + 1 < nz))
        def _():
            along(block, 1, False).wait_send()

        @pl.when((block >= z) & (z > 0))
        def _():
            along(block, -1, False).wait_send()

        for copy in column_copies(block) + neighbour_copies(block):
            copy.wait_send()
        passed(1 - x, block, over, whole, 0, to_core, core).wait_send()
        return 0

    lax.fori_loop(0, nz, drain, 0)
    finish()


def gather_call(plan, collective_id, attention, experts):
    hbm = pl.BlockSpec(memory_space=pltpu.HBM)
    vmem = pl.BlockSpec(memory_space=pltpu.VMEM)
    nx, nz, ns = plan.nx, plan.nz, plan.ns
    outs = [jax.ShapeDtypeStruct((nx, nz, ns) + attention.shape, BF16)]
    outs += [jax.ShapeDtypeStruct((nx, ns) + part.shape[1:], BF16) for part in experts]
    return pl.pallas_call(
        functools.partial(gather_kernel, plan),
        out_shape=outs,
        in_specs=[vmem] * 3,
        out_specs=[hbm] * 3,
        scratch_shapes=[
            DMA((nz,)),
            DMA((nz,)),
            DMA((nz,)),
            DMA((1,)),
            DMA((nx, nz, ns, 3)),
            DMA((nx, nz, 2)),
            DMA((nx, nz, 2)),
            DMA((nx, nz, 2)),
        ]
        + spread_scratch(plan),
        compiler_params=pltpu.CompilerParams(
            collective_id=collective_id, has_side_effects=True, vmem_limit_bytes=VMEM_LIMIT
        ),
    )(attention, *experts)


def expert_collect(plan, ins, outs, parts, stage, load, swap_send, swap_recv, send, recv):
    x, z, s = me()
    ns, group = plan.ns, plan.group
    rank = x * ns + s
    own_expert, own_part = rank // group, rank % group
    order = [(k, kind) for kind in range(len(ins)) for k in range(ns // group)]

    def swap(k, step, kind):
        part_to = (own_part + step) % group
        to = own_expert * group + part_to
        return remote(
            ins[kind].at[k * group + part_to],
            parts[kind].at[step - 1, k],
            swap_send.at[step - 1, k, kind],
            swap_recv.at[step - 1, k, kind],
            (to // ns, z, to % ns),
        )

    def own(k, kind):
        return pltpu.make_async_copy(
            ins[kind].at[k * group + own_part], stage[kind].at[k], load.at[k, kind]
        )

    def home(k, kind):
        layer, which = kind // 2, kind % 2
        here = (x == layer) & (s == k * group + own_part)
        return here, remote(
            stage[kind].at[k],
            outs[which].at[own_expert],
            send.at[k, kind],
            recv.at[own_expert, which],
            (layer, z, k * group + own_part),
        )

    def start():
        for k, kind in order:
            own(k, kind).start()
            for step in range(1, group):
                swap(k, step, kind).start()

    def add(place):
        k, kind = order[place]
        own(k, kind).wait()
        for step in range(1, group):
            swap(k, step, kind).wait_recv()
        total = stage[kind][k].astype(F32)
        for step in range(1, group):
            total += parts[kind][step - 1, k].astype(F32)
        stage[kind][k] = total.astype(BF16)
        here, copy = home(k, kind)

        @pl.when(here)
        def _():
            which = kind % 2
            pltpu.make_async_copy(
                stage[kind].at[k], outs[which].at[own_expert], recv.at[own_expert, which]
            ).start()

        @pl.when(jnp.logical_not(here))
        def _():
            copy.start()

    def finish():
        for which in range(2):
            for expert in range(EXP_DEV):
                landed(outs[which].at[expert], recv.at[expert, which])
        for k, kind in order:
            for step in range(1, group):
                swap(k, step, kind).wait_send()
            here, copy = home(k, kind)

            @pl.when(jnp.logical_not(here))
            def _():
                copy.wait_send()

    return len(order), start, add, finish


def collect_scratch(plan, values):
    group, each, kinds = plan.group, plan.ns // plan.group, len(values)
    return (
        [pltpu.VMEM((group - 1, each) + part.shape[1:], BF16) for part in values]
        + [pltpu.VMEM((each,) + part.shape[1:], BF16) for part in values]
        + [
            DMA((each, kinds)),
            DMA((group - 1, each, kinds)),
            DMA((group - 1, each, kinds)),
            DMA((each, kinds)),
            DMA((EXP_DEV, 2)),
        ]
    )


def collect_kernel(plan, *refs):
    kinds = 2 * plan.nx
    ins, outs = refs[:kinds], refs[kinds : kinds + 2]
    parts, stage = refs[kinds + 2 : 2 * kinds + 2], refs[2 * kinds + 2 : 3 * kinds + 2]
    greet_plane(plan)
    count, start, add, finish = expert_collect(
        plan, ins, outs, parts, stage, *refs[3 * kinds + 2 :]
    )
    start()
    for place in range(count):
        add(place)
    finish()


def collect_call(plan, collective_id, terms):
    ns = plan.ns
    hbm = pl.BlockSpec(memory_space=pltpu.HBM)
    values = [part.reshape(ns, part.shape[0] // ns, D) for layer in terms for part in layer]
    return pl.pallas_call(
        functools.partial(collect_kernel, plan),
        out_shape=[jax.ShapeDtypeStruct((EXP_DEV,) + part.shape[1:], BF16) for part in values[:2]],
        in_specs=[hbm] * len(values),
        out_specs=[hbm, hbm],
        scratch_shapes=collect_scratch(plan, values),
        compiler_params=pltpu.CompilerParams(
            collective_id=collective_id, has_side_effects=True, vmem_limit_bytes=VMEM_LIMIT
        ),
    )(*values)


ADDS = (0, 0, 0, 0, 8, 8, 8)
DEPTH = 1


def reduce_kernel(plan, *refs):
    grads, wide_ins, out, wide_outs = refs[0:2], refs[2:6], refs[6], refs[7:9]
    scratch = refs[9:]
    mine, given, x_one, y_one, y_two, x_two, chain = scratch[:7]
    (
        load_sem,
        core_send,
        core_recv,
        x_one_send,
        x_one_recv,
        y_one_send,
        y_one_recv,
        x_two_send,
        x_two_recv,
        y_two_send,
        y_two_recv,
        chain_send,
        chain_recv,
    ) = scratch[7:20]
    parts, stage = scratch[20:24], scratch[24:28]
    x, z, s = me()
    nz = plan.nz
    row, side = s // 2, s % 2
    core = (x, z, s + 1 - 2 * side)
    across_x = (1 - x, z, s)
    across_y = (x, z, (s + 2) % 4)
    size = grads[0].shape[2] // 2
    greet_plane(plan, along=True)
    count, start, add, finish = expert_collect(plan, wide_ins, wide_outs, parts, stage, *scratch[28:])
    both = range(2)
    low, high = pl.ds(0, size), pl.ds(size, size)

    def load(layer, block, to_row):
        return pltpu.make_async_copy(
            grads[layer].at[block, to_row * 2 + side],
            mine.at[layer, block, to_row],
            load_sem.at[layer, block, to_row],
        )

    def give(layer, block, to_row):
        return remote(
            grads[layer].at[block, to_row * 2 + 1 - side],
            given.at[layer, block, to_row],
            core_send.at[layer, block, to_row],
            core_recv.at[layer, block, to_row],
            core,
        )

    def send_x_one(block, to_row):
        return remote(
            mine.at[1 - x, block, to_row, low],
            x_one.at[block, to_row],
            x_one_send.at[block, to_row],
            x_one_recv.at[block, to_row],
            across_x,
        )

    def send_y_one(layer, block):
        return remote(
            mine.at[layer, block, 1 - row, high],
            y_one.at[layer, block],
            y_one_send.at[layer, block],
            y_one_recv.at[layer, block],
            across_y,
        )

    def send_y_two(block):
        return remote(
            mine.at[x, block, 1 - row, low],
            y_two.at[block],
            y_two_send.at[block],
            y_two_recv.at[block],
            across_y,
        )

    def send_x_two(block):
        return remote(
            mine.at[1 - x, block, row, high],
            x_two.at[block],
            x_two_send.at[block],
            x_two_recv.at[block],
            across_x,
        )

    def send_chain(block):
        rightward = (block > z).astype(jnp.int32)
        to = z - 1 + 2 * rightward
        into = jnp.where((rightward == 1) & (block == to), nz, block)
        return remote(
            mine.at[x, block, row],
            chain.at[into],
            chain_send.at[block],
            chain_recv.at[into],
            (x, to, s),
        )

    def gain(target, at, other):
        target[at] = (target[at].astype(F32) + other.astype(F32)).astype(BF16)

    def begin(index):
        block = nearest(z, nz - 1 - index, nz)
        for layer in both:
            for to_row in both:
                load(layer, block, to_row).start()
                give(layer, block, to_row).start()

    def stage_core(index):
        block = nearest(z, nz - 1 - index, nz)
        for layer in both:
            for to_row in both:
                load(layer, block, to_row).wait()
                give(layer, block, to_row).wait_recv()
                gain(mine, (layer, block, to_row), given[layer, block, to_row])
        for to_row in both:
            send_x_one(block, to_row).start()
        for layer in both:
            send_y_one(layer, block).start()

    def stage_first(index):
        block = nearest(z, nz - 1 - index, nz)
        for to_row in both:
            send_x_one(block, to_row).wait_recv()
            gain(mine, (x, block, to_row, low), x_one[block, to_row])
        send_y_two(block).start()
        for layer in both:
            send_y_one(layer, block).wait_recv()
            gain(mine, (layer, block, row, high), y_one[layer, block])
        send_x_two(block).start()

    def stage_second(index):
        block = nearest(z, nz - 1 - index, nz)
        origin = ((block < z) & (z == nz - 1)) | ((block > z) & (z == 0))
        send_y_two(block).wait_recv()
        gain(mine, (x, block, row, low), y_two[block])
        send_x_two(block).wait_recv()
        gain(mine, (x, block, row, high), x_two[block])

        @pl.when(origin)
        def _():
            send_chain(block).start()

    begin(0)
    begin(1)
    adds = 0
    for index in range(nz + 3):
        if index < nz:
            stage_core(index)
        if index + 2 < nz:
            begin(index + 2)
        if index == 0:
            start()
        if DEPTH <= index < nz + DEPTH:
            stage_first(index - DEPTH)
        if DEPTH + 1 <= index < nz + DEPTH + 1:
            stage_second(index - DEPTH - 1)
        while adds < count and adds < ADDS[index]:
            add(adds)
            adds += 1
    while adds < count:
        add(adds)
        adds += 1

    def relay(turn, _):
        lower = z < nz // 2
        first = jnp.where(lower, nz - 1 - z, z)
        early = turn < first
        ahead = jnp.where(early, first - turn, nz - 1 - turn)
        rightward = lower == early
        block = jnp.where(rightward, z + ahead, z - ahead)

        @pl.when((z > 0) & (z < nz - 1))
        def _():
            landed(chain.at[block], chain_recv.at[block])
            gain(mine, (x, block, row), chain[block])
            send_chain(block).start()

        return 0

    lax.fori_loop(0, nz - 1, relay, 0)
    out[...] = mine[x, z, row].astype(F32)

    @pl.when(z + 1 < nz)
    def _():
        landed(chain.at[z], chain_recv.at[z])
        out[...] += chain[z].astype(F32)

    @pl.when(z > 0)
    def _():
        landed(chain.at[nz], chain_recv.at[nz])
        out[...] += chain[nz].astype(F32)

    def drain(block, _):
        for layer in both:
            for to_row in both:
                give(layer, block, to_row).wait_send()
            send_y_one(layer, block).wait_send()
        for to_row in both:
            send_x_one(block, to_row).wait_send()
        send_y_two(block).wait_send()
        send_x_two(block).wait_send()

        @pl.when(block != z)
        def _():
            send_chain(block).wait_send()

        return 0

    lax.fori_loop(0, nz, drain, 0)
    finish()


def reduce_call(plan, collective_id, attention, terms):
    nx, nz, ns = plan.nx, plan.nz, plan.ns
    hbm = pl.BlockSpec(memory_space=pltpu.HBM)
    vmem = pl.BlockSpec(memory_space=pltpu.VMEM)
    grads = [part.reshape(nz, ns, -1, part.shape[1]) for part in attention]
    values = [part.reshape(ns, part.shape[0] // ns, D) for layer in terms for part in layer]
    size = grads[0].shape[2:]
    half = (size[0] // 2, size[1])
    return pl.pallas_call(
        functools.partial(reduce_kernel, plan),
        out_shape=[jax.ShapeDtypeStruct(size, F32)]
        + [jax.ShapeDtypeStruct((EXP_DEV,) + part.shape[1:], BF16) for part in values[:2]],
        in_specs=[hbm] * 6,
        out_specs=[vmem, hbm, hbm],
        scratch_shapes=[
            pltpu.VMEM((nx, nz, 2) + size, BF16),
            pltpu.VMEM((nx, nz, 2) + size, BF16),
            pltpu.VMEM((nz, 2) + half, BF16),
            pltpu.VMEM((nx, nz) + half, BF16),
            pltpu.VMEM((nz,) + half, BF16),
            pltpu.VMEM((nz,) + half, BF16),
            pltpu.VMEM((nz + 1,) + size, BF16),
            DMA((nx, nz, 2)),
            DMA((nx, nz, 2)),
            DMA((nx, nz, 2)),
            DMA((nz, 2)),
            DMA((nz, 2)),
            DMA((nx, nz)),
            DMA((nx, nz)),
            DMA((nz,)),
            DMA((nz,)),
            DMA((nz,)),
            DMA((nz,)),
            DMA((nz,)),
            DMA((nz + 1,)),
        ]
        + collect_scratch(plan, values),
        compiler_params=pltpu.CompilerParams(
            collective_id=collective_id, has_side_effects=True, vmem_limit_bytes=VMEM_LIMIT
        ),
    )(*grads, *values)


NARROW = (((1,), (1,)), ((), ()))
ACROSS = (((0,), (0,)), ((), ()))


def greet_shards(plan):
    x, z, s = me()
    barrier = pltpu.get_barrier_semaphore()
    for step in range(1, plan.ns):
        pl.semaphore_signal(
            barrier, inc=1, device_id=(x, z, (s + step) % plan.ns), device_id_type=MESH
        )
    pl.semaphore_wait(barrier, plan.ns - 1)


def turned(value, cosine, sine):
    return value * cosine + pltpu.roll(value, HD // 2, 1) * sine


def weights_of(queries, keys, allowed):
    raw = lax.dot_general(queries, keys, NARROW, preferred_element_type=F32)
    raw = jnp.where(allowed, raw * SCALE, -1e30)
    raw = jnp.exp(raw - jnp.max(raw, axis=1, keepdims=True))
    return raw / jnp.sum(raw, axis=1, keepdims=True)


def attend_kernel(plan, layer, *refs):
    (start, gains, cosine, sine, mask, weights) = refs[:6]
    (middle, normed, low, queries, kv, mixed) = refs[6:12]
    (win_v, wout_v, load_sem, send, recv) = refs[12:]
    x, z, s = me()
    tokens, rows, micro, ns = plan.tokens, plan.rows, plan.micro, plan.ns
    length = ns * tokens
    load_in = pltpu.make_async_copy(weights.at[layer, :, pl.ds(0, WIN)], win_v, load_sem.at[0])
    load_out = pltpu.make_async_copy(weights.at[layer, :, pl.ds(WIN, D)], wout_v, load_sem.at[1])
    load_in.start()
    load_out.start()
    greet_shards(plan)

    hidden = start[...].astype(F32)
    inverse = lax.rsqrt(jnp.mean(hidden * hidden, axis=1, keepdims=True) + epsilon)
    low[...] = (hidden * inverse * gains[0:1, :]).astype(BF16)
    load_in.wait()
    own = jnp.dot(low[...], win_v[:, WQ : WQ + 2 * WK], preferred_element_type=F32)
    for head in range(KV_HEADS):
        at = slice(head * HD, (head + 1) * HD)
        key = turned(own[:, at], cosine[...], sine[...]).astype(BF16)
        value = own[:, WK + head * HD : WK + (head + 1) * HD].astype(BF16)
        for m in range(micro):
            block = slice(m * tokens, (m + 1) * tokens)
            kv[s, m, :, at] = key[block]
            kv[s, m, :, WK + head * HD : WK + (head + 1) * HD] = value[block]

    def share(step, m):
        return remote(
            kv.at[s, m],
            kv.at[s, m],
            send.at[step - 1, m],
            recv.at[s, m],
            (x, z, (s + step) % ns),
        )

    for m in range(micro):
        for step in range(1, ns):
            share(step, m).start()

    def project(step, _):
        at = pl.multiple_of(step * 4 * HD, 4 * HD)
        part = jnp.dot(low[...], win_v[:, pl.ds(at, 4 * HD)], preferred_element_type=F32)
        for head in range(4):
            here = part[:, head * HD : (head + 1) * HD]
            queries[:, pl.ds(at + head * HD, HD)] = turned(here, cosine[...], sine[...]).astype(
                BF16
            )
        return 0

    lax.fori_loop(0, HEADS // 4, project, 0)

    def group(turn, _):
        m, pair = turn // KV_HEADS, turn % KV_HEADS

        @pl.when(pair == 0)
        def _():
            for step in range(1, ns):
                landed(kv.at[(s + step) % ns, m], recv.at[(s + step) % ns, m])

        span = pl.ds(pl.multiple_of(m * tokens, tokens), tokens)
        keys = kv[:, m, :, pl.ds(pl.multiple_of(pair * HD, HD), HD)].reshape(length, HD)
        values = kv[:, m, :, pl.ds(pl.multiple_of(WK + pair * HD, HD), HD)].reshape(length, HD)
        allowed = mask[m] > 0
        for i in range(GROUP):
            at = pl.ds(pl.multiple_of((pair * GROUP + i) * HD, HD), HD)
            probs = weights_of(queries[span, at], keys, allowed).astype(BF16)
            mixed[span, at] = jnp.dot(probs, values, preferred_element_type=F32).astype(BF16)
        return 0

    lax.fori_loop(0, micro * KV_HEADS, group, 0)
    load_out.wait()

    def back(step, _):
        at = pl.ds(pl.multiple_of(step * 512, 512), 512)
        middle[:, at] = start[:, at].astype(F32) + jnp.dot(
            mixed[...], wout_v[:, at], preferred_element_type=F32
        )
        return 0

    lax.fori_loop(0, D // 512, back, 0)
    after = middle[...]
    inverse = lax.rsqrt(jnp.mean(after * after, axis=1, keepdims=True) + epsilon)
    normed[...] = (after * inverse * gains[1:2, :]).astype(BF16)
    for m in range(micro):
        for step in range(1, ns):
            share(step, m).wait_send()


def attend_call(plan, layer, collective_id, start, gains, tables, weights):
    rows, ns, micro = plan.rows, plan.ns, plan.micro
    vmem = pl.BlockSpec(memory_space=pltpu.VMEM)
    hbm = pl.BlockSpec(memory_space=pltpu.HBM)
    shape = jax.ShapeDtypeStruct
    return pl.pallas_call(
        functools.partial(attend_kernel, plan, layer),
        out_shape=[
            shape((rows, D), F32),
            shape((rows, D), BF16),
            shape((rows, D), BF16),
            shape((rows, WQ), BF16),
            shape((ns, micro, plan.tokens, 2 * WK), BF16),
            shape((rows, WQ), BF16),
        ],
        in_specs=[vmem] * 5 + [hbm],
        out_specs=[vmem] * 6,
        scratch_shapes=[
            pltpu.VMEM((D, WIN), BF16),
            pltpu.VMEM((WQ, D), BF16),
            DMA((2,)),
            DMA((ns - 1, micro)),
            DMA((ns, micro)),
        ],
        compiler_params=pltpu.CompilerParams(
            collective_id=collective_id, has_side_effects=True, vmem_limit_bytes=VMEM_LIMIT
        ),
    )(start, gains, *tables, weights)


def return_kernel(plan, layer, *refs):
    (grad_out, grad_moe, middle, start, low, queries, kv, mixed) = refs[:8]
    (gains, cosine, sine, mask, weights) = refs[8:13]
    (grad_in, terms) = refs[13:15]
    (win_v, wout_v, branch, grad_mixed, both, part, got, in_v, out_v) = refs[15:24]
    (load_sem, save_in, save_out, send, recv) = refs[24:]
    x, z, s = me()
    tokens, rows, micro, ns = plan.tokens, plan.rows, plan.micro, plan.ns
    length = ns * tokens
    load_in = pltpu.make_async_copy(weights.at[layer, :, pl.ds(0, WIN)], win_v, load_sem.at[0])
    load_out = pltpu.make_async_copy(weights.at[layer, :, pl.ds(WIN, D)], wout_v, load_sem.at[1])
    load_out.start()
    load_in.start()
    greet_shards(plan)

    after = middle[...]
    inverse = lax.rsqrt(jnp.mean(after * after, axis=1, keepdims=True) + epsilon)
    scaled = grad_moe[...] * gains[1:2, :]
    inner = jnp.mean(scaled * after, axis=1, keepdims=True)
    total = grad_out[...].astype(F32) + inverse * scaled - after * (
        inverse * inverse * inverse * inner
    )
    grad_in[...] = total
    branch[...] = total.astype(BF16)
    gain_two = jnp.sum(grad_moe[...] * after * inverse, axis=0, keepdims=True)
    load_out.wait()

    def mix(step, _):
        at = pl.ds(pl.multiple_of(step * 512, 512), 512)
        grad_mixed[:, at] = lax.dot_general(
            branch[...], wout_v[at, :], NARROW, preferred_element_type=F32
        ).astype(BF16)
        return 0

    lax.fori_loop(0, WQ // 512, mix, 0)

    def share(step, m):
        to = (s + step) % ns
        return remote(
            part.at[to, m],
            got.at[s, m],
            send.at[step - 1, m],
            recv.at[s, m],
            (x, z, to),
        )

    def group(turn, _):
        m, pair = turn // KV_HEADS, turn % KV_HEADS
        span = pl.ds(pl.multiple_of(m * tokens, tokens), tokens)
        key_at = pl.ds(pl.multiple_of(pair * HD, HD), HD)
        value_at = pl.ds(pl.multiple_of(WK + pair * HD, HD), HD)
        keys = kv[:, m, :, key_at].reshape(length, HD)
        values = kv[:, m, :, value_at].reshape(length, HD)
        allowed = mask[m] > 0
        grad_keys = jnp.zeros((length, HD), F32)
        grad_values = jnp.zeros((length, HD), F32)
        for i in range(GROUP):
            at = pl.ds(pl.multiple_of((pair * GROUP + i) * HD, HD), HD)
            mine, given = queries[span, at], grad_mixed[span, at]
            probs = weights_of(mine, keys, allowed)
            grad_probs = lax.dot_general(given, values, NARROW, preferred_element_type=F32)
            inside = jnp.sum(grad_probs * probs, axis=1, keepdims=True)
            raw = (probs * (grad_probs - inside) * SCALE).astype(BF16)
            grad_query = jnp.dot(raw, keys, preferred_element_type=F32)
            both[span, at] = turned(grad_query, cosine[span], -sine[span]).astype(BF16)
            grad_keys += lax.dot_general(raw, mine, ACROSS, preferred_element_type=F32)
            grad_values += lax.dot_general(
                probs.astype(BF16), given, ACROSS, preferred_element_type=F32
            )
        part[:, m, :, key_at] = grad_keys.astype(BF16).reshape(ns, tokens, HD)
        part[:, m, :, value_at] = grad_values.astype(BF16).reshape(ns, tokens, HD)

        @pl.when(pair == KV_HEADS - 1)
        def _():
            for step in range(1, ns):
                share(step, m).start()

        return 0

    lax.fori_loop(0, micro * KV_HEADS, group, 0)

    def out_copy(step):
        at = pl.ds(step * 256, 256)
        return pltpu.make_async_copy(out_v.at[at], terms.at[at, pl.ds(WIN, D)], save_out.at[step])

    def in_copy(step):
        at = pl.ds(step * 256, 256)
        return pltpu.make_async_copy(in_v.at[at], terms.at[at, pl.ds(0, WIN)], save_in.at[step])

    def out_tile(step, _):
        at = pl.ds(pl.multiple_of(step * 256, 256), 256)
        out_v[at, :] = lax.dot_general(
            mixed[:, at], branch[...], ACROSS, preferred_element_type=F32
        ).astype(BF16)
        out_copy(step).start()
        return 0

    lax.fori_loop(0, WQ // 256, out_tile, 0)
    load_in.wait()
    for m in range(micro):
        for step in range(1, ns):
            landed(got.at[(s + step) % ns, m], recv.at[(s + step) % ns, m])
        span = slice(m * tokens, (m + 1) * tokens)
        total = part[s, m].astype(F32)
        for step in range(1, ns):
            total += got[(s + step) % ns, m].astype(F32)
        for head in range(KV_HEADS):
            at = slice(head * HD, (head + 1) * HD)
            both[span, WQ + head * HD : WQ + (head + 1) * HD] = turned(
                total[:, at], cosine[span], -sine[span]
            ).astype(BF16)
        both[span, WQ + WK :] = total[:, WK:].astype(BF16)

    def in_tile(step, _):
        at = pl.ds(pl.multiple_of(step * 256, 256), 256)
        in_v[at, : WQ + 2 * WK] = lax.dot_general(
            low[:, at], both[...], ACROSS, preferred_element_type=F32
        ).astype(BF16)
        return 0

    lax.fori_loop(0, D // 256, in_tile, 0)
    grad_normed = []
    for step in range(D // 512):
        at = slice(step * 512, (step + 1) * 512)
        grad_normed.append(
            lax.dot_general(
                both[...], win_v[at, : WQ + 2 * WK], NARROW, preferred_element_type=F32
            )
        )
    grad_normed = jnp.concatenate(grad_normed, axis=1)
    hidden = start[...].astype(F32)
    inverse = lax.rsqrt(jnp.mean(hidden * hidden, axis=1, keepdims=True) + epsilon)
    scaled = grad_normed * gains[0:1, :]
    inner = jnp.mean(scaled * hidden, axis=1, keepdims=True)
    grad_in[...] += inverse * scaled - hidden * (inverse * inverse * inverse * inner)
    gain_one = jnp.sum(grad_normed * hidden * inverse, axis=0, keepdims=True)
    place = lax.broadcasted_iota(jnp.int32, (128, D), 0)
    rows_of = jnp.where(place == 0, gain_one, jnp.where(place == 1, gain_two, 0.0))
    in_v[:, WQ + 2 * WK :] = rows_of.T.astype(BF16)
    for step in range(D // 256):
        in_copy(step).start()
    for step in range(D // 256):
        in_copy(step).wait()
        out_copy(step).wait()
    for m in range(micro):
        for step in range(1, ns):
            share(step, m).wait_send()


def return_call(plan, layer, collective_id, grads, saved, gains, tables, weights):
    rows, ns, micro, tokens = plan.rows, plan.ns, plan.micro, plan.tokens
    vmem = pl.BlockSpec(memory_space=pltpu.VMEM)
    hbm = pl.BlockSpec(memory_space=pltpu.HBM)
    shape = jax.ShapeDtypeStruct
    exchange = (ns, micro, tokens, 2 * WK)
    return pl.pallas_call(
        functools.partial(return_kernel, plan, layer),
        out_shape=[
            shape((rows, D), F32),
            shape((D, WIN + D), BF16),
        ],
        in_specs=[vmem] * 12 + [hbm],
        out_specs=[vmem, hbm],
        scratch_shapes=[
            pltpu.VMEM((D, WIN), BF16),
            pltpu.VMEM((WQ, D), BF16),
            pltpu.VMEM((rows, D), BF16),
            pltpu.VMEM((rows, WQ), BF16),
            pltpu.VMEM((rows, WQ + 2 * WK), BF16),
            pltpu.VMEM(exchange, BF16),
            pltpu.VMEM(exchange, BF16),
            pltpu.VMEM((D, WIN), BF16),
            pltpu.VMEM((WQ, D), BF16),
            DMA((2,)),
            DMA((D // 256,)),
            DMA((WQ // 256,)),
            DMA((ns - 1, micro)),
            DMA((ns, micro)),
        ],
        compiler_params=pltpu.CompilerParams(
            collective_id=collective_id, has_side_effects=True, vmem_limit_bytes=VMEM_LIMIT
        ),
    )(*grads, *saved, gains, *tables, weights)


def slot_tables(plan, routes, gates):
    experts, nz = plan.experts, plan.nz
    named = routes[..., None] == jnp.arange(experts, dtype=jnp.int32)
    gate = jnp.sum(jnp.where(named, gates[..., None], 0.0), axis=2)
    named = jnp.any(named, axis=2)
    earlier = jnp.tril(jnp.ones((plan.tokens, plan.tokens), BF16), -1)
    rank = jnp.einsum("ut,mte->mue", earlier, named.astype(BF16), preferred_element_type=F32)
    table = jnp.stack([jnp.where(named, rank, -1.0), gate])
    table = table.reshape(2, plan.micro, plan.tokens, nz, EXP_DEV).transpose(3, 0, 1, 4, 2)
    table = lax.all_to_all(table, "expert", split_axis=0, concat_axis=0, tiled=True)
    rank, gate = table[:, 0], table[:, 1]
    first = jnp.arange(plan.micro, dtype=F32)[:, None, None] * plan.capacity
    place = jnp.where(rank >= 0, rank + first, -1.0).transpose(0, 2, 1, 3)
    hit = place[:, :, None] == jnp.arange(plan.slots, dtype=F32)[:, None, None]
    shape = (nz, EXP_DEV * plan.slots, plan.rows)
    one = hit.astype(BF16).reshape(shape)
    weighted = jnp.where(hit, gate.transpose(0, 2, 1, 3)[:, :, None], 0.0)
    weighted = weighted.astype(BF16).reshape(shape)
    return one, weighted


def shards(
    inputs,
    segments,
    routes,
    gate_weights,
    query_weight,
    key_value_weight,
    output_weight,
    norm_gains,
    expert_gate_up,
    expert_down,
    cotangent,
):
    section = lax.axis_index("section")
    shard_index = lax.axis_index("shard")
    tokens = inputs.shape[1]
    plan = Plan((lax.axis_size("section"), lax.axis_size("expert"), lax.axis_size("shard")), tokens)
    micro, rows, layers = plan.micro, plan.rows, plan.nx
    length = tokens * plan.ns

    def mine(value):
        return lax.dynamic_slice_in_dim(value, section * micro, micro, 0)

    paired = plan.nx == 2 and plan.ns == 4 and query_weight.shape[1] % 32 == 0
    gain_columns = jnp.pad(norm_gains[0].T, ((0, 0), (0, PAD - 2)))
    attention_weights = jnp.concatenate(
        [query_weight[0], key_value_weight[0], gain_columns, output_weight[0]], axis=1
    ).astype(BF16)
    expert_weights = (expert_gate_up[0].astype(BF16), expert_down[0].astype(BF16))
    if paired:
        weights, wide_in, wide_down = gather_call(plan, 1, attention_weights, expert_weights)
    else:
        weights = lax.all_gather(
            attention_weights, ("section", "expert", "shard"), axis=0, tiled=True
        )
        wide_in, wide_down = spread_call(plan, 1, *expert_weights)
    weights = weights.reshape(layers, D, WIN + D)
    gains = weights[:, :, PROJ : PROJ + 2].transpose(0, 2, 1).astype(F32)
    wide_in = wide_in.reshape(layers, D, 2 * FF)
    wide_down = wide_down.reshape(layers, FF, D)
    one, weighted = slot_tables(plan, mine(routes), mine(gate_weights))

    offset = shard_index * tokens
    position = (offset + jnp.arange(tokens, dtype=jnp.int32)).astype(F32)
    frequency = rope_base ** (-jnp.arange(HD // 2, dtype=F32) / (HD // 2))
    angles = position[:, None] * frequency[None, :]
    cosine, sine = jnp.cos(angles), jnp.sin(angles)
    cosine = jnp.tile(jnp.concatenate([cosine, cosine], axis=1), (micro, 1))
    sine = jnp.tile(jnp.concatenate([-sine, sine], axis=1), (micro, 1))
    segment_all = mine(segments)[:, 0]
    segment_own = lax.dynamic_slice_in_dim(segment_all, offset, tokens, 1)
    query_place = offset + jnp.arange(tokens, dtype=jnp.int32)
    key_place = jnp.arange(length, dtype=jnp.int32)
    allowed = (segment_own[:, :, None] == segment_all[:, None, :]) & (
        query_place[:, None] >= key_place[None, :]
    )
    tables = (cosine, sine, allowed.astype(F32))

    hidden = mine(inputs).reshape(rows, D)
    kept = []
    for layer in range(layers):
        start = hidden.astype(BF16)
        middle, normed, low, queries, kv, mixed = attend_call(
            plan, layer, 2 + layer, start, gains[layer], tables, weights
        )
        hidden, sent, gate_up, hidden_low = moe_call(
            plan,
            layer,
            False,
            2 + layers + layer,
            normed,
            one,
            weighted,
            wide_in,
            wide_down,
            middle,
        )
        kept.append(((middle, start, low, queries, kv, mixed), sent, gate_up, hidden_low))
    output = hidden.reshape(micro, tokens, D)

    grad = mine(cotangent).reshape(rows, D)
    attention_terms = [None] * layers
    expert_terms = [None] * layers
    for layer in reversed(range(layers)):
        saved, sent, gate_up, hidden_low = kept[layer]
        grad_out = grad.astype(BF16)
        grad_moe, grad_sent, grad_both = moe_call(
            plan,
            layer,
            True,
            2 + 2 * layers + layer,
            grad_out,
            weighted,
            one,
            wide_in,
            wide_down,
            gate_up,
        )
        in_term = jnp.einsum(
            "rd,rf->df",
            sent.reshape(-1, D),
            grad_both.reshape(-1, 2 * FF),
            preferred_element_type=F32,
        ).astype(BF16)
        down_term = jnp.einsum(
            "rf,rd->fd",
            hidden_low.reshape(-1, FF),
            grad_sent.reshape(-1, D),
            preferred_element_type=F32,
        ).astype(BF16)
        expert_terms[layer] = (in_term, down_term)
        grad, attention_terms[layer] = return_call(
            plan,
            layer,
            2 + 3 * layers + layer,
            (grad_out, grad_moe),
            saved,
            gains[layer],
            tables,
            weights,
        )
    input_grad = grad.reshape(micro, tokens, D)

    if paired:
        term, gate_up_grad, down_grad = reduce_call(
            plan, 2 + 4 * layers, attention_terms, expert_terms
        )
    else:
        gate_up_grad, down_grad = collect_call(plan, 2 + 4 * layers, expert_terms)
        term = lax.psum_scatter(
            jnp.concatenate(attention_terms),
            ("section", "expert", "shard"),
            scatter_dimension=0,
            tiled=True,
        )
    query_grad, key_value_grad, gain_grad, output_weight_grad, gate_up_grad, down_grad = (
        part.astype(F32)[None]
        for part in (
            term[:, :WQ],
            term[:, WQ:PROJ],
            term[:, PROJ : PROJ + 2].T,
            term[:, WIN:],
            gate_up_grad,
            down_grad,
        )
    )
    return (
        output,
        input_grad,
        query_grad,
        key_value_grad,
        output_weight_grad,
        gain_grad,
        gate_up_grad,
        down_grad,
    )


def solution(mesh):
    placed = (
        P(None, ("expert", "shard"), None),
        P(None, "expert", None),
        P(None, ("expert", "shard"), None),
        P(None, ("expert", "shard"), None),
        P("section", ("expert", "shard"), None),
        P("section", ("expert", "shard"), None),
        P("section", ("expert", "shard"), None),
        P("section", None, ("expert", "shard")),
        P("section", "expert", "shard", None),
        P("section", "expert", "shard", None),
        P(None, ("expert", "shard"), None),
    )
    return jax.shard_map(
        shards,
        mesh=mesh,
        in_specs=placed,
        out_specs=(
            P("section", ("expert", "shard"), None),
            P("section", ("expert", "shard"), None),
            P("section", ("expert", "shard"), None),
            P("section", ("expert", "shard"), None),
            P("section", ("expert", "shard"), None),
            P("section", None, ("expert", "shard")),
            P("section", "expert", "shard", None),
            P("section", "expert", "shard", None),
        ),
        check_vma=False,
    )
```

```python
import functools
import math
from types import SimpleNamespace

import jax
import jax.numpy as jnp
from jax import lax
from jax.experimental import pallas as pl
from jax.experimental.pallas import tpu as pltpu
from jax.sharding import PartitionSpec as P

D = 1536
HEADS = 12
KV_HEADS = 2
HD = 128
FF = 768
TOPK = 4
EXP_DEV = 4
MICRO = 4
GROUP = HEADS // KV_HEADS
PAD = 128
WQ = HEADS * HD
WK = KV_HEADS * HD
PROJ = WQ + 2 * WK
WIN = PROJ + PAD
SCALE = HD ** (-0.5)

epsilon = 1e-06
rope_base = 10000.0

MESH = pl.DeviceIdType.MESH
F32 = jnp.float32
BF16 = jnp.bfloat16
DMA = pltpu.SemaphoreType.DMA
VMEM_LIMIT = 62 * 2**20


class Plan:
    def __init__(self, mesh_shape, tokens):
        self.nx, self.nz, self.ns = mesh_shape
        self.tokens = tokens
        self.micro = MICRO // self.nx
        self.rows = self.micro * tokens
        self.ranks = self.nx * self.ns
        self.group = self.ranks // EXP_DEV
        self.halves = self.group // 2
        self.sources = self.ranks // self.halves
        self.experts = EXP_DEV * self.nz
        self.capacity = 5 * tokens * TOPK // (4 * self.experts)
        self.slots = -(-self.micro * self.capacity // 16) * 16
        self.blocks = self.nz // 2
        self.many = self.sources * self.slots


def me():
    return lax.axis_index("section"), lax.axis_index("expert"), lax.axis_index("shard")


def remote(src, dst, send, recv, device):
    return pltpu.make_async_remote_copy(
        src_ref=src,
        dst_ref=dst,
        send_sem=send,
        recv_sem=recv,
        device_id=device,
        device_id_type=MESH,
    )


def landed(ref, sem):
    pltpu.make_async_copy(ref, ref, sem).wait()


def greet_plane(plan, along=False):
    x, z, s = me()
    barrier = pltpu.get_barrier_semaphore()
    mine = x * plan.ns + s
    for step in range(1, plan.ranks):
        other = (mine + step) % plan.ranks
        pl.semaphore_signal(
            barrier, inc=1, device_id=(other // plan.ns, z, other % plan.ns), device_id_type=MESH
        )
    total = plan.ranks - 1
    if along:
        for step in range(1, plan.nz):
            pl.semaphore_signal(
                barrier, inc=1, device_id=(x, (z + step) % plan.nz, s), device_id_type=MESH
            )
        total += plan.nz - 1
    pl.semaphore_wait(barrier, total)


def nearest(place, index, count):
    left = place
    right = count - 1 - place
    short = jnp.minimum(left, right)
    odd = index % 2
    near = place + (1 - 2 * odd) * ((index + 1) // 2)
    far = jnp.where(left < right, index, count - 1 - index)
    return jnp.where(index <= 2 * short, near, far)


NARROW = (((1,), (1,)), ((), ()))
ACROSS = (((0,), (0,)), ((), ()))
TILE = 256
CUTS = 3
CUT = D // CUTS


def moe_stages(plan, backward, r):
    x, z, s = me()
    nz, ns, slots = plan.nz, plan.ns, plan.slots
    rank = x * ns + s
    own_expert = rank // plan.group
    own_turn = (rank % plan.group) // plan.halves
    own_half = rank % plan.halves
    part = ns // plan.halves
    own_source = x * part + s // plan.halves
    chunk = plan.tokens
    own_copy = pltpu.make_async_copy(r.rows_in, r.line.at[z], r.own_sem.at[0])

    def along(block, piece, step, own):
        at = pl.ds(piece * chunk, chunk)
        src = r.rows_in.at[at] if own else r.line.at[block, at]
        sem = r.line_right if step > 0 else r.line_left
        return remote(
            src,
            r.line.at[block, at],
            sem.at[block, piece],
            r.line_recv.at[block, piece],
            (x, z + step, s),
        )

    def owner(block, expert):
        rank_to = expert * plan.group + (block % 2) * plan.halves + s % plan.halves
        return rank_to // ns, rank_to % ns

    def dispatch_copy(block, expert):
        to_x, to_s = owner(block, expert)
        here = (to_x == x) & (to_s == s)
        return here, remote(
            r.sbuf.at[block, expert],
            r.xbuf.at[block // 2, own_source],
            r.to_send.at[block, expert],
            r.to_recv.at[block // 2, own_source],
            (to_x, z, to_s),
        )

    def return_copy(block, cut, source):
        to_x = source // part
        to_s = (source % part) * plan.halves + own_half
        here = (to_x == x) & (to_s == s)
        return here, remote(
            r.ybuf.at[block // 2, cut, source],
            r.rbuf.at[block, cut, own_expert],
            r.back_send.at[block // 2, cut, source],
            r.back_recv.at[block, cut, own_expert],
            (to_x, z, to_s),
        )

    def sum_copy(block, cut):
        rightward = (block > z).astype(jnp.int32)
        to = z - 1 + 2 * rightward
        into = jnp.where((rightward == 1) & (block == to), nz, block)
        return remote(
            r.pbuf.at[block, cut],
            r.qbuf.at[into, cut],
            r.sum_send.at[block, cut],
            r.sum_recv.at[into, cut],
            (x, to, s),
        )

    def begin():
        for piece in range(plan.micro):

            @pl.when(z + 1 < nz)
            def _():
                along(z, piece, 1, True).start()

            @pl.when(z > 0)
            def _():
                along(z, piece, -1, True).start()

        own_copy.start()

    def fetch(index):
        block = nearest(z, index, nz)
        if index == 0:
            own_copy.wait()
        for piece in range(plan.micro):

            @pl.when(block < z)
            def _():
                along(block, piece, 1, False).wait_recv()

                @pl.when(z + 1 < nz)
                def _():
                    along(block, piece, 1, False).start()

            @pl.when(block > z)
            def _():
                along(block, piece, -1, False).wait_recv()

                @pl.when(z > 0)
                def _():
                    along(block, piece, -1, False).start()

    def put(index):
        block = nearest(z, index, nz)

        def lay(step, _):
            at = pl.ds(pl.multiple_of(step * TILE, TILE), TILE)
            laid = jnp.dot(r.put[block], r.line[block, :, at], preferred_element_type=F32)
            r.sbuf[block, :, :, at] = laid.astype(BF16).reshape(EXP_DEV, slots, TILE)
            return 0

        lax.fori_loop(0, D // TILE, lay, 0)
        for expert in range(EXP_DEV):
            here, copy = dispatch_copy(block, expert)

            @pl.when(here)
            def _():
                pltpu.make_async_copy(
                    r.sbuf.at[block, expert],
                    r.xbuf.at[block // 2, own_source],
                    r.to_recv.at[block // 2, own_source],
                ).start()

            @pl.when(jnp.logical_not(here))
            def _():
                copy.start()

    def compute(block, now):
        pair = block // 2
        for source in range(plan.sources):
            landed(r.xbuf.at[pair, source], r.to_recv.at[pair, source])
        few = plan.sources // 2
        span = few * slots

        def middle(step, _):
            rows = pl.ds(pl.multiple_of(step * span, 16), span)
            taken = r.xbuf[pair, pl.ds(step * few, few)].reshape(span, D)
            if backward:
                grad_hidden = lax.dot_general(
                    taken, r.wdown_v[...], NARROW, preferred_element_type=F32
                )
                gate = r.gbuf[pair, rows, :FF].astype(F32)
                up = r.gbuf[pair, rows, FF:].astype(F32)
                sig = 1.0 / (1.0 + jnp.exp(-gate))
                gs = gate * sig
                grad_gate = grad_hidden * up * (sig + gs * (1.0 - sig))
                r.gbuf[pair, rows, :FF] = grad_gate.astype(BF16)
                r.gbuf[pair, rows, FF:] = (grad_hidden * gs).astype(BF16)
            else:
                gate = jnp.dot(taken, r.win_v[:, :FF], preferred_element_type=F32)
                up = jnp.dot(taken, r.win_v[:, FF:], preferred_element_type=F32)
                r.gbuf[pair, rows, :FF] = gate.astype(BF16)
                r.gbuf[pair, rows, FF:] = up.astype(BF16)
                r.zbuf[pair, rows] = (gate / (1.0 + jnp.exp(-gate)) * up).astype(BF16)
            return 0

        lax.fori_loop(0, 2, middle, 0)

        def last(cut, _):
            at = pl.ds(pl.multiple_of(cut * CUT, CUT), CUT)
            if backward:
                result = lax.dot_general(
                    r.gbuf[pair], r.win_v[at, :], NARROW, preferred_element_type=F32
                )
            else:
                result = jnp.dot(r.zbuf[pair], r.wdown_v[:, at], preferred_element_type=F32)
            r.ybuf[pair, cut] = result.astype(BF16).reshape(plan.sources, slots, CUT)
            if now:
                return_cut(block, cut)
            return 0

        lax.fori_loop(0, CUTS, last, 0)

    def return_cut(block, cut):
        pair = block // 2
        for source in range(plan.sources):
            here, copy = return_copy(block, cut, source)

            @pl.when(here)
            def _():
                pltpu.make_async_copy(
                    r.ybuf.at[pair, cut, source],
                    r.rbuf.at[block, cut, own_expert],
                    r.back_recv.at[block, cut, own_expert],
                ).start()

            @pl.when(jnp.logical_not(here))
            def _():
                copy.start()

    def own_turn_do(index, act):
        block = nearest(z, index, nz)

        @pl.when(block % 2 == own_turn)
        def _():
            act(block)

    def give_back(block):
        for cut in range(CUTS):
            return_cut(block, cut)

    def take(index):
        block = nearest(z, index, nz)
        origin = ((block < z) & (z == nz - 1)) | ((block > z) & (z == 0))
        for cut in range(CUTS):
            for expert in range(EXP_DEV):
                landed(r.rbuf.at[block, cut, expert], r.back_recv.at[block, cut, expert])
            got = lax.dot_general(
                r.take[block],
                r.rbuf[block, cut].reshape(EXP_DEV * slots, CUT),
                (((0,), (0,)), ((), ())),
                preferred_element_type=F32,
            )

            @pl.when(block == z)
            def _():
                at = pl.ds(cut * CUT, CUT)
                if backward:
                    r.out[:, at] = got
                else:
                    r.out[:, at] += got

            @pl.when(block != z)
            def _():
                r.pbuf[block, cut] = got.astype(BF16)

            @pl.when(origin)
            def _():
                sum_copy(block, cut).start()

    def relay(turn):
        lower = z < nz // 2
        first = jnp.where(lower, nz - 1 - z, z)
        early = turn < first
        ahead = jnp.where(early, first - turn, nz - 1 - turn)
        rightward = lower == early
        block = jnp.where(rightward, z + ahead, z - ahead)

        @pl.when((z > 0) & (z < nz - 1))
        def _():
            for cut in range(CUTS):
                landed(r.qbuf.at[block, cut], r.sum_recv.at[block, cut])
                r.pbuf[block, cut] = (
                    r.pbuf[block, cut].astype(F32) + r.qbuf[block, cut].astype(F32)
                ).astype(BF16)
                sum_copy(block, cut).start()

    def finish():
        for cut in range(CUTS):
            at = pl.ds(cut * CUT, CUT)

            @pl.when(z + 1 < nz)
            def _():
                landed(r.qbuf.at[z, cut], r.sum_recv.at[z, cut])
                r.out[:, at] += r.qbuf[z, cut].astype(F32)

            @pl.when(z > 0)
            def _():
                landed(r.qbuf.at[nz, cut], r.sum_recv.at[nz, cut])
                r.out[:, at] += r.qbuf[nz, cut].astype(F32)

    def free_put(block):
        for piece in range(plan.micro):

            @pl.when((block <= z) & (z + 1 < nz))
            def _():
                along(block, piece, 1, False).wait_send()

            @pl.when((block >= z) & (z > 0))
            def _():
                along(block, piece, -1, False).wait_send()

        for expert in range(EXP_DEV):
            here, copy = dispatch_copy(block, expert)

            @pl.when(jnp.logical_not(here))
            def _():
                copy.wait_send()

    def free_back(block):
        for cut in range(CUTS):
            for source in range(plan.sources):
                here, copy = return_copy(block, cut, source)

                @pl.when(jnp.logical_not(here))
                def _():
                    copy.wait_send()

    def free_sum(block):
        @pl.when(block != z)
        def _():
            for cut in range(CUTS):
                sum_copy(block, cut).wait_send()

    def free_all():
        def free(block, _):
            free_put(block)

            @pl.when(block % 2 == own_turn)
            def _():
                free_back(block)

            free_sum(block)
            return 0

        lax.fori_loop(0, nz, free, 0)

    return SimpleNamespace(
        begin=begin,
        fetch=fetch,
        put=put,
        expert=lambda index, now=True: own_turn_do(index, lambda block: compute(block, now)),
        give_back=lambda index: own_turn_do(index, give_back),
        take=take,
        relay=relay,
        finish=finish,
        free_put=lambda index: free_put(nearest(z, index, nz)),
        free_back=lambda index: own_turn_do(index, free_back),
        free_sum=lambda index: free_sum(nearest(z, index, nz)),
        free_all=free_all,
    )


def late_relays(nz):
    return (2, 1) if nz == 4 else range(1, nz - 1)


def first_part(plan, stages, loaded):
    last = plan.nz - 1
    stages.fetch(0)
    stages.put(0)
    loaded()
    for index in range(1, plan.nz):
        stages.fetch(index)
        stages.put(index)
        stages.expert(index - 1, 1 < index < last)


def second_part(plan, stages, steps=()):
    last = plan.nz - 1
    steps = iter(steps)

    def another():
        next(steps, lambda: None)()

    for index in range(1, plan.nz - 2):
        stages.take(index)
    stages.expert(last)
    another()
    stages.take(last)
    stages.give_back(last - 1)
    stages.give_back(0)
    another()
    stages.relay(0)
    stages.take(last - 1)
    another()
    stages.take(0)


def weight_tiles(plan, given, hidden, grad_both, grad_rows, in_term, down_term, tile_v, sem):
    counts = (D // TILE, FF // TILE)

    def copy(tile):
        if isinstance(tile, int) and tile >= counts[0]:
            to = down_term.at[pl.ds((tile - counts[0]) * TILE, TILE)]
        else:
            to = in_term.at[pl.ds(pl.multiple_of(tile * TILE, TILE), TILE)]
        return pltpu.make_async_copy(tile_v.at[tile % 2], to, sem.at[tile % 2])

    def summed(left, right):
        total = lax.dot_general(left(0), right(0), ACROSS, preferred_element_type=F32)
        for pair in range(1, plan.blocks):
            total += lax.dot_general(left(pair), right(pair), ACROSS, preferred_element_type=F32)
        return total.astype(BF16)

    def rows_of(ref, pair, at):
        return ref[pair, :, :, at].reshape(plan.many, -1)

    def in_tile(tile, _):
        @pl.when(tile >= 2)
        def _():
            copy(tile % 2).wait()

        at = pl.ds(pl.multiple_of(tile * TILE, TILE), TILE)
        tile_v[tile % 2] = summed(lambda p: rows_of(given, p, at), lambda p: grad_both[p])
        copy(tile).start()
        return 0

    def first():
        lax.fori_loop(0, counts[0], in_tile, 0)

    def second():
        for step in range(counts[1]):
            tile = counts[0] + step
            copy(tile % 2).wait()
            at = slice(step * TILE, (step + 1) * TILE)
            tile_v[tile % 2] = summed(
                lambda p: hidden[p, :, at], lambda p: grad_rows[p].reshape(plan.many, D)
            )
            copy(tile).start()

    def finish():
        for tile in range(sum(counts) - 2, sum(counts)):
            copy(tile).wait()

    return first, second, finish


PASS_BUFFERS = ("line", "xbuf", "rbuf", "qbuf")
PASS_SEMAPHORES = (
    "own_sem",
    "line_recv",
    "line_right",
    "line_left",
    "to_send",
    "to_recv",
    "back_send",
    "back_recv",
    "sum_send",
    "sum_recv",
)
SHARED_BUFFERS = ("sbuf", "ybuf", "pbuf", "win_v", "wdown_v", "gbuf", "zbuf")


def pass_scratch(plan):
    nz, blocks, slots, sources, rows = plan.nz, plan.blocks, plan.slots, plan.sources, plan.rows
    return [
        pltpu.VMEM((nz, rows, D), BF16),
        pltpu.VMEM((blocks, sources, slots, D), BF16),
        pltpu.VMEM((nz, CUTS, EXP_DEV, slots, CUT), BF16),
        pltpu.VMEM((nz + 1, CUTS, rows, CUT), BF16),
        DMA((1,)),
        DMA((nz, plan.micro)),
        DMA((nz, plan.micro)),
        DMA((nz, plan.micro)),
        DMA((nz, EXP_DEV)),
        DMA((blocks, sources)),
        DMA((blocks, CUTS, sources)),
        DMA((nz, CUTS, EXP_DEV)),
        DMA((nz, CUTS)),
        DMA((nz + 1, CUTS)),
    ]


def shared_scratch(plan):
    nz, blocks, slots, many = plan.nz, plan.blocks, plan.slots, plan.many
    return [
        pltpu.VMEM((nz, EXP_DEV, slots, D), BF16),
        pltpu.VMEM((blocks, CUTS, plan.sources, slots, CUT), BF16),
        pltpu.VMEM((nz, CUTS, plan.rows, CUT), BF16),
        pltpu.VMEM((D, 2 * FF), BF16),
        pltpu.VMEM((FF, D), BF16),
        pltpu.VMEM((blocks, many, 2 * FF), BF16),
        pltpu.VMEM((blocks, many, FF), BF16),
    ]


PASS_NAMES = PASS_BUFFERS + PASS_SEMAPHORES


def named(names, refs):
    return dict(zip(names, refs, strict=True))


def run_copies(copies):
    for copy in copies:
        copy.start()

    def wait():
        for copy in copies:
            copy.wait()

    return wait


def moe_kernel(plan, layer, *refs):
    rows_in, put, take, w_in, w_down, base, result, sent, gate_up, hidden = refs[:10]
    count = len(PASS_NAMES)
    r = SimpleNamespace(
        rows_in=rows_in,
        put=put,
        take=take,
        **named(PASS_NAMES, refs[10 : 10 + count]),
        **named(SHARED_BUFFERS, refs[10 + count : -3]),
    )
    out, load_sem, save_sem = refs[-3:]
    r.out = out
    loaded = run_copies(
        [
            pltpu.make_async_copy(w_in.at[layer], r.win_v, load_sem.at[0]),
            pltpu.make_async_copy(w_down.at[layer], r.wdown_v, load_sem.at[1]),
            pltpu.make_async_copy(base, out, load_sem.at[2]),
        ]
    )
    greet_plane(plan, along=True)
    stages = moe_stages(plan, False, r)
    stages.begin()
    first_part(plan, stages, loaded)
    second_part(plan, stages)
    saved = run_copies(
        [
            pltpu.make_async_copy(r.xbuf, sent, save_sem.at[0]),
            pltpu.make_async_copy(r.gbuf, gate_up, save_sem.at[1]),
            pltpu.make_async_copy(r.zbuf, hidden, save_sem.at[2]),
        ]
    )
    for turn in late_relays(plan.nz):
        stages.relay(turn)
    stages.finish()
    result[...] = out[...].astype(result.dtype)
    stages.free_all()
    saved()


def moe_back_kernel(plan, layer, *refs):
    rows_in, put, take, w_in, w_down, sent, gate_up, hidden, out, in_term, down_term = refs[:11]
    count = len(PASS_NAMES)
    r = SimpleNamespace(
        rows_in=rows_in,
        put=put,
        take=take,
        out=out,
        **named(PASS_NAMES, refs[11 : 11 + count]),
        **named(SHARED_BUFFERS, refs[11 + count : -4]),
    )
    given, tile_v, load_sem, tile_sem = refs[-4:]
    loaded = run_copies(
        [
            pltpu.make_async_copy(w_in.at[layer], r.win_v, load_sem.at[0]),
            pltpu.make_async_copy(w_down.at[layer], r.wdown_v, load_sem.at[1]),
            pltpu.make_async_copy(gate_up, r.gbuf, load_sem.at[2]),
            pltpu.make_async_copy(sent, given, load_sem.at[3]),
            pltpu.make_async_copy(hidden, r.zbuf, load_sem.at[4]),
        ]
    )
    greet_plane(plan, along=True)
    stages = moe_stages(plan, True, r)
    first, second, finish = weight_tiles(
        plan, given, r.zbuf, r.gbuf, r.xbuf, in_term, down_term, tile_v, tile_sem
    )
    stages.begin()
    first_part(plan, stages, loaded)
    second_part(plan, stages, (first, second))
    for turn in late_relays(plan.nz):
        stages.relay(turn)
    stages.finish()
    stages.free_all()
    finish()


def moe_both_kernel(plan, layer, *refs):
    rows_in, rows_back, one, weighted, w_in, w_down, base = refs[:7]
    out, out_back, in_term, down_term = refs[7:11]
    count = len(PASS_NAMES)
    shared = named(SHARED_BUFFERS, refs[11 + 2 * count : -2])
    ahead = SimpleNamespace(
        rows_in=rows_in,
        put=one,
        take=weighted,
        out=out,
        **named(PASS_NAMES, refs[11 : 11 + count]),
        **shared,
    )
    back = SimpleNamespace(
        rows_in=rows_back,
        put=weighted,
        take=one,
        out=out_back,
        **named(PASS_NAMES, refs[11 + count : 11 + 2 * count]),
        **shared,
    )
    load_sem, tile_sem = refs[-2:]
    loaded = run_copies(
        [
            pltpu.make_async_copy(w_in.at[layer], ahead.win_v, load_sem.at[0]),
            pltpu.make_async_copy(w_down.at[layer], ahead.wdown_v, load_sem.at[1]),
            pltpu.make_async_copy(base, out, load_sem.at[2]),
        ]
    )
    greet_plane(plan, along=True)
    forward = moe_stages(plan, False, ahead)
    backward = moe_stages(plan, True, back)
    first, second, finish = weight_tiles(
        plan,
        ahead.xbuf,
        back.zbuf,
        back.gbuf,
        back.xbuf,
        in_term,
        down_term,
        ahead.line,
        tile_sem,
    )
    nz, last = plan.nz, plan.nz - 1
    forward.begin()
    first_part(plan, forward, loaded)
    backward.begin()
    order = list(reversed(range(nz)))
    relays = list(late_relays(nz))

    def arrive():
        for index in range(3, nz):
            backward.fetch(index)

    second_part(
        plan,
        forward,
        (
            lambda: backward.fetch(1),
            lambda: backward.fetch(2),
            arrive,
        ),
    )
    backward.fetch(0)

    def put(index):
        forward.free_put(index)
        backward.put(index)

    def expert(index):
        forward.free_back(index)
        backward.expert(index)

    def take(index):
        forward.free_sum(index)
        backward.take(index)

    put(order[0])
    for turn in relays[: len(relays) // 2]:
        forward.relay(turn)
    put(order[1])
    expert(order[0])
    for turn in relays[len(relays) // 2 :]:
        forward.relay(turn)
    put(order[2])
    expert(order[1])
    forward.finish()
    take(order[0])
    for place in range(3, nz):
        put(order[place])
        expert(order[place - 1])
        take(order[place - 2])
    backward.relay(0)
    expert(order[-1])
    first()
    take(order[-2])
    for turn in relays:
        backward.relay(turn)
    second()
    take(order[-1])
    backward.finish()
    backward.free_all()
    finish()


def moe_specs(plan, collective_id):
    return dict(
        compiler_params=pltpu.CompilerParams(
            collective_id=collective_id, has_side_effects=True, vmem_limit_bytes=VMEM_LIMIT
        ),
    )


def saved_shapes(plan):
    return [
        jax.ShapeDtypeStruct((plan.blocks, plan.sources, plan.slots, D), BF16),
        jax.ShapeDtypeStruct((plan.blocks, plan.many, 2 * FF), BF16),
        jax.ShapeDtypeStruct((plan.blocks, plan.many, FF), BF16),
    ]


TERMS = [jax.ShapeDtypeStruct((D, 2 * FF), BF16), jax.ShapeDtypeStruct((FF, D), BF16)]


def moe_call(plan, layer, kind, collective_id, rows_in, put, take, w_in, w_down, base):
    vmem = pl.BlockSpec(memory_space=pltpu.VMEM)
    hbm = pl.BlockSpec(memory_space=pltpu.HBM)
    return pl.pallas_call(
        functools.partial(moe_kernel, plan, layer),
        out_shape=[jax.ShapeDtypeStruct((plan.rows, D), kind)] + saved_shapes(plan),
        in_specs=[vmem] * 3 + [hbm] * 3,
        out_specs=[vmem] + [hbm] * 3,
        scratch_shapes=pass_scratch(plan) + shared_scratch(plan) + [pltpu.VMEM((plan.rows, D), F32), DMA((3,)), DMA((3,))],
        **moe_specs(plan, collective_id),
    )(rows_in, put, take, w_in, w_down, base)


def moe_back_call(plan, layer, collective_id, rows_in, put, take, w_in, w_down, saved):
    vmem = pl.BlockSpec(memory_space=pltpu.VMEM)
    hbm = pl.BlockSpec(memory_space=pltpu.HBM)
    out, *terms = pl.pallas_call(
        functools.partial(moe_back_kernel, plan, layer),
        out_shape=[jax.ShapeDtypeStruct((plan.rows, D), F32)] + TERMS,
        in_specs=[vmem] * 3 + [hbm] * 5,
        out_specs=[vmem] + [hbm] * 2,
        scratch_shapes=pass_scratch(plan)
        + shared_scratch(plan)
        + [
            pltpu.VMEM((plan.blocks, plan.sources, plan.slots, D), BF16),
            pltpu.VMEM((2, TILE, D), BF16),
            DMA((5,)),
            DMA((2,)),
        ],
        **moe_specs(plan, collective_id),
    )(rows_in, put, take, w_in, w_down, *saved)
    return out, terms


def both_fit(plan):
    scratch = pass_scratch(plan) * 2 + shared_scratch(plan)
    words = sum(
        math.prod(part.shape) for part in scratch if getattr(part, "dtype", None) == BF16
    )
    return 2 * words + 10 * 2**20 < VMEM_LIMIT and plan.rows == TILE


def moe_both_call(plan, layer, collective_id, rows_in, rows_back, one, weighted, w_in, w_down, base):
    vmem = pl.BlockSpec(memory_space=pltpu.VMEM)
    hbm = pl.BlockSpec(memory_space=pltpu.HBM)
    out, out_back, *terms = pl.pallas_call(
        functools.partial(moe_both_kernel, plan, layer),
        out_shape=[jax.ShapeDtypeStruct((plan.rows, D), F32)] * 2 + TERMS,
        in_specs=[vmem, hbm, vmem, vmem] + [hbm] * 3,
        out_specs=[vmem] * 2 + [hbm] * 2,
        scratch_shapes=pass_scratch(plan) * 2
        + shared_scratch(plan)
        + [DMA((3,)), DMA((2,))],
        **moe_specs(plan, collective_id),
    )(rows_in, rows_back, one, weighted, w_in, w_down, base)
    return out, out_back, terms


def expert_spread(plan, ins, outs, send, recv, pass_send, pass_recv):
    x, z, s = me()
    nx, ns, group = plan.nx, plan.ns, plan.group
    rank = x * ns + s
    own_expert, own_part = rank // group, rank % group
    own = [(layer, k) for layer in range(nx) for k in range(ns // group)]

    def first(expert, which):
        to = expert * group + s % group
        return to == rank, remote(
            ins[which].at[expert],
            outs[which].at[x, s],
            send.at[expert, which],
            recv.at[x, s, which],
            (to // ns, z, to % ns),
        )

    def onward(layer, source, step, which):
        to = own_expert * group + (own_part + step) % group
        return remote(
            outs[which].at[layer, source],
            outs[which].at[layer, source],
            pass_send.at[layer, source, step - 1, which],
            pass_recv.at[layer, source, which],
            (to // ns, z, to % ns),
        )

    def start(expert, which):
        here, copy = first(expert, which)

        @pl.when(here)
        def _():
            pltpu.make_async_copy(
                ins[which].at[expert], outs[which].at[x, s], recv.at[x, s, which]
            ).start()

        @pl.when(jnp.logical_not(here))
        def _():
            copy.start()

    def pass_on():
        for layer, k in own:
            source = k * group + own_part
            for which in range(2):
                landed(outs[which].at[layer, source], recv.at[layer, source, which])
                for step in range(1, group):
                    onward(layer, source, step, which).start()

    def finish():
        for layer, k in own:
            for step in range(1, group):
                source = k * group + (own_part + step) % group
                for which in range(2):
                    landed(outs[which].at[layer, source], pass_recv.at[layer, source, which])
        for which in range(2):
            for expert in range(EXP_DEV):
                here, copy = first(expert, which)

                @pl.when(jnp.logical_not(here))
                def _():
                    copy.wait_send()

        for layer, k in own:
            source = k * group + own_part
            for which in range(2):
                for step in range(1, group):
                    onward(layer, source, step, which).wait_send()

    return start, pass_on, finish


def spread_scratch(plan):
    nx, ns, group = plan.nx, plan.ns, plan.group
    return [
        DMA((EXP_DEV, 2)),
        DMA((nx, ns, 2)),
        DMA((nx, ns, group - 1, 2)),
        DMA((nx, ns, 2)),
    ]


def spread_kernel(plan, *refs):
    greet_plane(plan)
    start, pass_on, finish = expert_spread(plan, refs[:2], refs[2:4], *refs[4:])
    for which in range(2):
        for expert in range(EXP_DEV):
            start(expert, which)
    pass_on()
    finish()


def spread_call(plan, collective_id, gate_up, down):
    hbm = pl.BlockSpec(memory_space=pltpu.HBM)
    vmem = pl.BlockSpec(memory_space=pltpu.VMEM)
    outs = [
        jax.ShapeDtypeStruct((plan.nx, plan.ns) + part.shape[1:], BF16) for part in (gate_up, down)
    ]
    return pl.pallas_call(
        functools.partial(spread_kernel, plan),
        out_shape=outs,
        in_specs=[vmem, vmem],
        out_specs=[hbm, hbm],
        scratch_shapes=spread_scratch(plan),
        compiler_params=pltpu.CompilerParams(
            collective_id=collective_id, has_side_effects=True, vmem_limit_bytes=VMEM_LIMIT
        ),
    )(gate_up, down)


def gather_kernel(plan, *refs):
    piece, table, wide_ins = refs[0], refs[1], refs[2:4]
    out, table_out, wide_outs = refs[4], refs[5], refs[6:8]
    (line_recv, right, left, copy_sem, plane_recv, to_core, to_x, to_y) = refs[8:16]
    (up_recv, up_right, up_left, table_send, table_recv) = refs[16:21]
    wide_v, low_v, load_sem = refs[21:23], refs[23:25], refs[25]
    x, z, s = me()
    nz = plan.nz
    row, side = s // 2, s % 2
    over = (s + 2) % 4
    loads = [
        pltpu.make_async_copy(wide_ins[which].at[expert], wide_v[which].at[expert], load_sem.at[which, expert])
        for which in range(2)
        for expert in range(EXP_DEV)
    ]
    for load in loads:
        load.start()
    greet_plane(plan, along=True)
    start, pass_on, finish = expert_spread(plan, low_v, wide_outs, *refs[26:])
    third = piece.shape[0] // 3
    parts = (
        (pl.ds(0, 2 * third), pl.ds(0, third), pl.ds(third, third)),
        (
            pl.ds(2 * third, third),
            pl.ds(2 * third, third // 2),
            pl.ds(2 * third + third // 2, third // 2),
        ),
    )
    core = (x, z, s + 1 - 2 * side)
    across_x = (1 - x, z, s)
    across_y = (x, z, over)

    def along(block, step, own):
        rows = parts[0][0]
        place = out.at[x, block, s, rows]
        sem = right if step > 0 else left
        return remote(
            piece.at[rows] if own else place,
            place,
            sem.at[block],
            line_recv.at[block],
            (x, z + step, s),
        )

    def upward(block, layer, to_row, step, own=False):
        rows = parts[1][0]
        place = out.at[layer, block, to_row * 2 + side, rows]
        sem = up_right if step > 0 else up_left
        return remote(
            piece.at[rows] if own else place,
            place,
            sem.at[block, layer, to_row],
            up_recv.at[block, layer, to_row],
            (x, z + step, s),
        )

    def passed(layer, block, shard, part, kind, sem, to, own=False):
        rows = parts[part][kind]
        place = out.at[layer, block, shard, rows]
        return remote(
            piece.at[rows] if own else place,
            place,
            sem.at[layer, block, shard // 2, part],
            plane_recv.at[layer, block, shard, part, kind],
            to,
        )

    def arrived(layer, block, shard, part, kind):
        landed(
            out.at[layer, block, shard, parts[part][kind]],
            plane_recv.at[layer, block, shard, part, kind],
        )

    def column_copies(block, part, own=False, ways=3):
        ways = ((to_x, across_x), (to_y, across_y), (to_core, core))[:ways]
        return [passed(x, block, s, part, 0, sem, to, own) for sem, to in ways]

    def neighbour_copies(block, part):
        return [
            passed(1 - x, block, s, part, 1, to_y, across_y),
            passed(1 - x, block, s, part, 0, to_core, core),
            passed(x, block, over, part, 2, to_x, across_x),
            passed(x, block, over, part, 0, to_core, core),
        ]

    def send_up(block, layer, to_row, own=False):
        @pl.when((block <= z) & (z + 1 < nz))
        def _():
            upward(block, layer, to_row, 1, own).start()

        @pl.when((block >= z) & (z > 0))
        def _():
            upward(block, layer, to_row, -1, own).start()

    def neighbours_of(block, part):
        copies = neighbour_copies(block, part)
        arrived(1 - x, block, s, part, 0)
        copies[0].start()
        copies[1].start()
        arrived(x, block, over, part, 0)
        copies[2].start()
        copies[3].start()

    def opposite_of(block, part):
        arrived(1 - x, block, over, part, 1)
        arrived(1 - x, block, over, part, 2)
        passed(1 - x, block, over, part, 0, to_core, core).start()

    @pl.when(z + 1 < nz)
    def _():
        along(z, 1, True).start()

    @pl.when(z > 0)
    def _():
        along(z, -1, True).start()

    send_up(z, x, row, True)
    own = pltpu.make_async_copy(piece, out.at[x, z, s], copy_sem.at[0])
    own.start()
    for part in (1, 0):
        for copy in column_copies(z, part, True):
            copy.start()

    def table_copy(step):
        to = (z + step) % nz
        return remote(
            table.at[to], table_out.at[z], table_send.at[step - 1], table_recv.at[z], (x, to, s)
        )

    for step in range(1, nz):
        table_copy(step).start()
    table_out[z] = table[z]
    neighbours_of(z, 1)
    send_up(z, 1 - x, row)
    send_up(z, x, 1 - row)
    opposite_of(z, 1)
    send_up(z, 1 - x, 1 - row)

    def column(index, _):
        block = nearest(z, index, nz)

        @pl.when(block < z)
        def _():
            along(block, 1, False).wait_recv()

            @pl.when(z + 1 < nz)
            def _():
                along(block, 1, False).start()

        @pl.when(block > z)
        def _():
            along(block, -1, False).wait_recv()

            @pl.when(z > 0)
            def _():
                along(block, -1, False).start()

        for copy in column_copies(block, 0):
            copy.start()
        for layer in range(2):
            for to_row in range(2):
                upward(block, layer, to_row, 1).wait_recv()
                send_up(block, layer, to_row)
                passed(layer, block, to_row * 2 + side, 1, 0, to_core, core).start()
        return 0

    def neighbours(index, _):
        neighbours_of(nearest(z, index, nz), 0)
        return 0

    def opposite(index, _):
        opposite_of(nearest(z, index, nz), 0)
        return 0

    for place, load in enumerate(loads):
        which, expert = place // EXP_DEV, place % EXP_DEV
        load.wait()
        low_v[which][expert] = wide_v[which][expert].astype(BF16)
        start(expert, which)
    lax.fori_loop(1, nz, column, 0)
    lax.fori_loop(0, nz, neighbours, 0)
    lax.fori_loop(0, nz, opposite, 0)
    own.wait()
    pass_on()
    for step in range(1, nz):
        block = (z + step) % nz
        landed(table_out.at[block], table_recv.at[block])
        table_copy(step).wait_send()

    def drain(block, _):
        other = s + 1 - 2 * side

        @pl.when((block <= z) & (z + 1 < nz))
        def _():
            along(block, 1, False).wait_send()

        @pl.when((block >= z) & (z > 0))
        def _():
            along(block, -1, False).wait_send()

        for layer in range(2):
            for to_row in range(2):
                for part in range(2):
                    arrived(layer, block, to_row * 2 + other % 2, part, 0)
                    passed(layer, block, to_row * 2 + side, part, 0, to_core, core).wait_send()

                @pl.when((block <= z) & (z + 1 < nz))
                def _():
                    upward(block, layer, to_row, 1).wait_send()

                @pl.when((block >= z) & (z > 0))
                def _():
                    upward(block, layer, to_row, -1).wait_send()

        def plane(part):
            for copy in column_copies(block, part, ways=2):
                copy.wait_send()
            passed(1 - x, block, s, part, 1, to_y, across_y).wait_send()
            passed(x, block, over, part, 2, to_x, across_x).wait_send()

        plane(0)

        @pl.when(block == z)
        def _():
            plane(1)

        return 0

    lax.fori_loop(0, nz, drain, 0)
    finish()


def gather_call(plan, collective_id, attention, table, experts):
    hbm = pl.BlockSpec(memory_space=pltpu.HBM)
    vmem = pl.BlockSpec(memory_space=pltpu.VMEM)
    nx, nz, ns = plan.nx, plan.nz, plan.ns
    outs = [
        jax.ShapeDtypeStruct((nx, nz, ns) + attention.shape, BF16),
        jax.ShapeDtypeStruct(table.shape, F32),
    ]
    outs += [jax.ShapeDtypeStruct((nx, ns) + part.shape[1:], BF16) for part in experts]
    return pl.pallas_call(
        functools.partial(gather_kernel, plan),
        out_shape=outs,
        in_specs=[vmem, vmem, hbm, hbm],
        out_specs=[hbm, vmem, hbm, hbm],
        scratch_shapes=[
            DMA((nz,)),
            DMA((nz,)),
            DMA((nz,)),
            DMA((1,)),
            DMA((nx, nz, ns, 2, 3)),
            DMA((nx, nz, 2, 2)),
            DMA((nx, nz, 2, 2)),
            DMA((nx, nz, 2, 2)),
            DMA((nz, nx, 2)),
            DMA((nz, nx, 2)),
            DMA((nz, nx, 2)),
            DMA((nz - 1,)),
            DMA((nz,)),
        ]
        + [pltpu.VMEM(part.shape, F32) for part in experts]
        + [pltpu.VMEM(part.shape, BF16) for part in experts]
        + [DMA((2, EXP_DEV))]
        + spread_scratch(plan),
        compiler_params=pltpu.CompilerParams(
            collective_id=collective_id, has_side_effects=True, vmem_limit_bytes=VMEM_LIMIT
        ),
    )(attention, table, *experts)


def expert_collect(plan, ins, outs, parts, stage, load, swap_send, swap_recv, send, recv):
    x, z, s = me()
    ns, group = plan.ns, plan.group
    rank = x * ns + s
    own_expert, own_part = rank // group, rank % group
    order = [(k, kind) for kind in range(len(ins)) for k in range(ns // group)]

    def swap(k, step, kind):
        part_to = (own_part + step) % group
        to = own_expert * group + part_to
        return remote(
            ins[kind].at[k * group + part_to],
            parts[kind].at[step - 1, k],
            swap_send.at[step - 1, k, kind],
            swap_recv.at[step - 1, k, kind],
            (to // ns, z, to % ns),
        )

    def own(k, kind):
        return pltpu.make_async_copy(
            ins[kind].at[k * group + own_part], stage[kind].at[k], load.at[k, kind]
        )

    def home(k, kind):
        layer, which = kind // 2, kind % 2
        here = (x == layer) & (s == k * group + own_part)
        return here, remote(
            stage[kind].at[k],
            outs[which].at[own_expert],
            send.at[k, kind],
            recv.at[own_expert, which],
            (layer, z, k * group + own_part),
        )

    def start():
        for k, kind in order:
            own(k, kind).start()
            for step in range(1, group):
                swap(k, step, kind).start()

    def add(place):
        k, kind = order[place]
        own(k, kind).wait()
        for step in range(1, group):
            swap(k, step, kind).wait_recv()
        total = stage[kind][k].astype(F32)
        for step in range(1, group):
            total += parts[kind][step - 1, k].astype(F32)
        stage[kind][k] = total.astype(BF16)
        here, copy = home(k, kind)

        @pl.when(here)
        def _():
            which = kind % 2
            pltpu.make_async_copy(
                stage[kind].at[k], outs[which].at[own_expert], recv.at[own_expert, which]
            ).start()

        @pl.when(jnp.logical_not(here))
        def _():
            copy.start()

    def finish():
        for which in range(2):
            for expert in range(EXP_DEV):
                landed(outs[which].at[expert], recv.at[expert, which])
        for k, kind in order:
            for step in range(1, group):
                swap(k, step, kind).wait_send()
            here, copy = home(k, kind)

            @pl.when(jnp.logical_not(here))
            def _():
                copy.wait_send()

    return len(order), start, add, finish


def collect_scratch(plan, values):
    group, each, kinds = plan.group, plan.ns // plan.group, len(values)
    return (
        [pltpu.VMEM((group - 1, each) + part.shape[1:], BF16) for part in values]
        + [pltpu.VMEM((each,) + part.shape[1:], BF16) for part in values]
        + [
            DMA((each, kinds)),
            DMA((group - 1, each, kinds)),
            DMA((group - 1, each, kinds)),
            DMA((each, kinds)),
            DMA((EXP_DEV, 2)),
        ]
    )


def collect_kernel(plan, *refs):
    kinds = 2 * plan.nx
    ins, outs = refs[:kinds], refs[kinds : kinds + 2]
    parts, stage = refs[kinds + 2 : 2 * kinds + 2], refs[2 * kinds + 2 : 3 * kinds + 2]
    greet_plane(plan)
    count, start, add, finish = expert_collect(
        plan, ins, outs, parts, stage, *refs[3 * kinds + 2 :]
    )
    start()
    for place in range(count):
        add(place)
    finish()


def collect_call(plan, collective_id, terms):
    ns = plan.ns
    hbm = pl.BlockSpec(memory_space=pltpu.HBM)
    values = [part.reshape(ns, part.shape[0] // ns, D) for layer in terms for part in layer]
    return pl.pallas_call(
        functools.partial(collect_kernel, plan),
        out_shape=[jax.ShapeDtypeStruct((EXP_DEV,) + part.shape[1:], BF16) for part in values[:2]],
        in_specs=[hbm] * len(values),
        out_specs=[hbm, hbm],
        scratch_shapes=collect_scratch(plan, values),
        compiler_params=pltpu.CompilerParams(
            collective_id=collective_id, has_side_effects=True, vmem_limit_bytes=VMEM_LIMIT
        ),
    )(*values)


ADDS = (0, 0, 0, 0, 8, 8, 8)
DEPTH = 1


def reduce_kernel(plan, *refs):
    grads, wide_ins, out, wide_outs = refs[0:2], refs[2:6], refs[6], refs[7:9]
    scratch = refs[9:]
    mine, given, x_one, y_one, y_two, x_two, chain = scratch[:7]
    (
        load_sem,
        core_send,
        core_recv,
        x_one_send,
        x_one_recv,
        y_one_send,
        y_one_recv,
        x_two_send,
        x_two_recv,
        y_two_send,
        y_two_recv,
        chain_send,
        chain_recv,
    ) = scratch[7:20]
    parts, stage = scratch[20:24], scratch[24:28]
    x, z, s = me()
    nz = plan.nz
    row, side = s // 2, s % 2
    core = (x, z, s + 1 - 2 * side)
    across_x = (1 - x, z, s)
    across_y = (x, z, (s + 2) % 4)
    size = grads[0].shape[2] // 2
    greet_plane(plan, along=True)
    count, start, add, finish = expert_collect(plan, wide_ins, wide_outs, parts, stage, *scratch[28:])
    both = range(2)
    low, high = pl.ds(0, size), pl.ds(size, size)

    def load(layer, block, to_row):
        return pltpu.make_async_copy(
            grads[layer].at[block, to_row * 2 + side],
            mine.at[layer, block, to_row],
            load_sem.at[layer, block, to_row],
        )

    def give(layer, block, to_row):
        return remote(
            grads[layer].at[block, to_row * 2 + 1 - side],
            given.at[layer, block, to_row],
            core_send.at[layer, block, to_row],
            core_recv.at[layer, block, to_row],
            core,
        )

    def send_x_one(block, to_row):
        return remote(
            mine.at[1 - x, block, to_row, low],
            x_one.at[block, to_row],
            x_one_send.at[block, to_row],
            x_one_recv.at[block, to_row],
            across_x,
        )

    def send_y_one(layer, block):
        return remote(
            mine.at[layer, block, 1 - row, high],
            y_one.at[layer, block],
            y_one_send.at[layer, block],
            y_one_recv.at[layer, block],
            across_y,
        )

    def send_y_two(block):
        return remote(
            mine.at[x, block, 1 - row, low],
            y_two.at[block],
            y_two_send.at[block],
            y_two_recv.at[block],
            across_y,
        )

    def send_x_two(block):
        return remote(
            mine.at[1 - x, block, row, high],
            x_two.at[block],
            x_two_send.at[block],
            x_two_recv.at[block],
            across_x,
        )

    def send_chain(block):
        rightward = (block > z).astype(jnp.int32)
        to = z - 1 + 2 * rightward
        into = jnp.where((rightward == 1) & (block == to), nz, block)
        return remote(
            mine.at[x, block, row],
            chain.at[into],
            chain_send.at[block],
            chain_recv.at[into],
            (x, to, s),
        )

    def gain(target, at, other):
        target[at] = (target[at].astype(F32) + other.astype(F32)).astype(BF16)

    def begin(index):
        block = nearest(z, nz - 1 - index, nz)
        for layer in both:
            for to_row in both:
                load(layer, block, to_row).start()
                give(layer, block, to_row).start()

    def stage_core(index):
        block = nearest(z, nz - 1 - index, nz)
        for layer in both:
            for to_row in both:
                load(layer, block, to_row).wait()
                give(layer, block, to_row).wait_recv()
                gain(mine, (layer, block, to_row), given[layer, block, to_row])
        for to_row in both:
            send_x_one(block, to_row).start()
        for layer in both:
            send_y_one(layer, block).start()

    def stage_first(index):
        block = nearest(z, nz - 1 - index, nz)
        for to_row in both:
            send_x_one(block, to_row).wait_recv()
            gain(mine, (x, block, to_row, low), x_one[block, to_row])
        send_y_two(block).start()
        for layer in both:
            send_y_one(layer, block).wait_recv()
            gain(mine, (layer, block, row, high), y_one[layer, block])
        send_x_two(block).start()

    def stage_second(index):
        block = nearest(z, nz - 1 - index, nz)
        origin = ((block < z) & (z == nz - 1)) | ((block > z) & (z == 0))
        send_y_two(block).wait_recv()
        gain(mine, (x, block, row, low), y_two[block])
        send_x_two(block).wait_recv()
        gain(mine, (x, block, row, high), x_two[block])

        @pl.when(origin)
        def _():
            send_chain(block).start()

    begin(0)
    begin(1)
    adds = 0
    for index in range(nz + 3):
        if index < nz:
            stage_core(index)
        if index + 2 < nz:
            begin(index + 2)
        if index == 0:
            start()
        if DEPTH <= index < nz + DEPTH:
            stage_first(index - DEPTH)
        if DEPTH + 1 <= index < nz + DEPTH + 1:
            stage_second(index - DEPTH - 1)
        while adds < count and adds < ADDS[index]:
            add(adds)
            adds += 1
    while adds < count:
        add(adds)
        adds += 1

    def relay(turn, _):
        lower = z < nz // 2
        first = jnp.where(lower, nz - 1 - z, z)
        early = turn < first
        ahead = jnp.where(early, first - turn, nz - 1 - turn)
        rightward = lower == early
        block = jnp.where(rightward, z + ahead, z - ahead)

        @pl.when((z > 0) & (z < nz - 1))
        def _():
            landed(chain.at[block], chain_recv.at[block])
            gain(mine, (x, block, row), chain[block])
            send_chain(block).start()

        return 0

    lax.fori_loop(0, nz - 1, relay, 0)
    out[...] = mine[x, z, row].astype(F32)

    @pl.when(z + 1 < nz)
    def _():
        landed(chain.at[z], chain_recv.at[z])
        out[...] += chain[z].astype(F32)

    @pl.when(z > 0)
    def _():
        landed(chain.at[nz], chain_recv.at[nz])
        out[...] += chain[nz].astype(F32)

    def drain(block, _):
        for layer in both:
            for to_row in both:
                give(layer, block, to_row).wait_send()
            send_y_one(layer, block).wait_send()
        for to_row in both:
            send_x_one(block, to_row).wait_send()
        send_y_two(block).wait_send()
        send_x_two(block).wait_send()

        @pl.when(block != z)
        def _():
            send_chain(block).wait_send()

        return 0

    lax.fori_loop(0, nz, drain, 0)
    finish()


def reduce_call(plan, collective_id, attention, terms):
    nx, nz, ns = plan.nx, plan.nz, plan.ns
    hbm = pl.BlockSpec(memory_space=pltpu.HBM)
    vmem = pl.BlockSpec(memory_space=pltpu.VMEM)
    grads = [part.reshape(nz, ns, -1, part.shape[1]) for part in attention]
    values = [part.reshape(ns, part.shape[0] // ns, D) for layer in terms for part in layer]
    size = grads[0].shape[2:]
    half = (size[0] // 2, size[1])
    return pl.pallas_call(
        functools.partial(reduce_kernel, plan),
        out_shape=[jax.ShapeDtypeStruct(size, F32)]
        + [jax.ShapeDtypeStruct((EXP_DEV,) + part.shape[1:], BF16) for part in values[:2]],
        in_specs=[hbm] * 6,
        out_specs=[vmem, hbm, hbm],
        scratch_shapes=[
            pltpu.VMEM((nx, nz, 2) + size, BF16),
            pltpu.VMEM((nx, nz, 2) + size, BF16),
            pltpu.VMEM((nz, 2) + half, BF16),
            pltpu.VMEM((nx, nz) + half, BF16),
            pltpu.VMEM((nz,) + half, BF16),
            pltpu.VMEM((nz,) + half, BF16),
            pltpu.VMEM((nz + 1,) + size, BF16),
            DMA((nx, nz, 2)),
            DMA((nx, nz, 2)),
            DMA((nx, nz, 2)),
            DMA((nz, 2)),
            DMA((nz, 2)),
            DMA((nx, nz)),
            DMA((nx, nz)),
            DMA((nz,)),
            DMA((nz,)),
            DMA((nz,)),
            DMA((nz,)),
            DMA((nz,)),
            DMA((nz + 1,)),
        ]
        + collect_scratch(plan, values),
        compiler_params=pltpu.CompilerParams(
            collective_id=collective_id, has_side_effects=True, vmem_limit_bytes=VMEM_LIMIT
        ),
    )(*grads, *values)


def greet_shards(plan):
    x, z, s = me()
    barrier = pltpu.get_barrier_semaphore()
    for step in range(1, plan.ns):
        pl.semaphore_signal(
            barrier, inc=1, device_id=(x, z, (s + step) % plan.ns), device_id_type=MESH
        )
    pl.semaphore_wait(barrier, plan.ns - 1)


def turned(value, cosine, sine):
    return value * cosine + pltpu.roll(value, HD // 2, 1) * sine


def weights_of(queries, keys, allowed):
    raw = lax.dot_general(queries, keys, NARROW, preferred_element_type=F32)
    raw = jnp.where(allowed, raw * SCALE, -1e30)
    raw = jnp.exp(raw - jnp.max(raw, axis=1, keepdims=True))
    return raw / jnp.sum(raw, axis=1, keepdims=True)


def attend_kernel(plan, layer, *refs):
    (start, gains, cosine, sine, mask, weights) = refs[:6]
    (middle, normed, low, queries, kv, mixed) = refs[6:12]
    (win_v, wout_v, load_sem, send, recv) = refs[12:]
    x, z, s = me()
    tokens, rows, micro, ns = plan.tokens, plan.rows, plan.micro, plan.ns
    length = ns * tokens
    load_in = pltpu.make_async_copy(weights.at[layer, :, pl.ds(0, WIN)], win_v, load_sem.at[0])
    load_out = pltpu.make_async_copy(weights.at[layer, :, pl.ds(WIN, D)], wout_v, load_sem.at[1])
    load_in.start()
    load_out.start()
    greet_shards(plan)

    hidden = start[...].astype(F32)
    inverse = lax.rsqrt(jnp.mean(hidden * hidden, axis=1, keepdims=True) + epsilon)
    low[...] = (hidden * inverse * gains[0:1, :]).astype(BF16)
    load_in.wait()
    own = jnp.dot(low[...], win_v[:, WQ : WQ + 2 * WK], preferred_element_type=F32)
    for head in range(KV_HEADS):
        at = slice(head * HD, (head + 1) * HD)
        key = turned(own[:, at], cosine[...], sine[...]).astype(BF16)
        value = own[:, WK + head * HD : WK + (head + 1) * HD].astype(BF16)
        for m in range(micro):
            block = slice(m * tokens, (m + 1) * tokens)
            kv[s, m, :, at] = key[block]
            kv[s, m, :, WK + head * HD : WK + (head + 1) * HD] = value[block]

    def share(step, m):
        return remote(
            kv.at[s, m],
            kv.at[s, m],
            send.at[step - 1, m],
            recv.at[s, m],
            (x, z, (s + step) % ns),
        )

    for m in range(micro):
        for step in range(1, ns):
            share(step, m).start()

    def project(step, _):
        at = pl.multiple_of(step * 4 * HD, 4 * HD)
        part = jnp.dot(low[...], win_v[:, pl.ds(at, 4 * HD)], preferred_element_type=F32)
        for head in range(4):
            here = part[:, head * HD : (head + 1) * HD]
            queries[:, pl.ds(at + head * HD, HD)] = turned(here, cosine[...], sine[...]).astype(
                BF16
            )
        return 0

    lax.fori_loop(0, HEADS // 4, project, 0)

    def group(turn, _):
        m, pair = turn // KV_HEADS, turn % KV_HEADS

        @pl.when(pair == 0)
        def _():
            for step in range(1, ns):
                landed(kv.at[(s + step) % ns, m], recv.at[(s + step) % ns, m])

        span = pl.ds(pl.multiple_of(m * tokens, tokens), tokens)
        keys = kv[:, m, :, pl.ds(pl.multiple_of(pair * HD, HD), HD)].reshape(length, HD)
        values = kv[:, m, :, pl.ds(pl.multiple_of(WK + pair * HD, HD), HD)].reshape(length, HD)
        allowed = mask[m] > 0
        for i in range(GROUP):
            at = pl.ds(pl.multiple_of((pair * GROUP + i) * HD, HD), HD)
            probs = weights_of(queries[span, at], keys, allowed).astype(BF16)
            mixed[span, at] = jnp.dot(probs, values, preferred_element_type=F32).astype(BF16)
        return 0

    lax.fori_loop(0, micro * KV_HEADS, group, 0)
    load_out.wait()

    def back(step, _):
        at = pl.ds(pl.multiple_of(step * 512, 512), 512)
        middle[:, at] = start[:, at].astype(F32) + jnp.dot(
            mixed[...], wout_v[:, at], preferred_element_type=F32
        )
        return 0

    lax.fori_loop(0, D // 512, back, 0)
    after = middle[...]
    inverse = lax.rsqrt(jnp.mean(after * after, axis=1, keepdims=True) + epsilon)
    normed[...] = (after * inverse * gains[1:2, :]).astype(BF16)
    for m in range(micro):
        for step in range(1, ns):
            share(step, m).wait_send()


def attend_call(plan, layer, collective_id, start, gains, tables, weights):
    rows, ns, micro = plan.rows, plan.ns, plan.micro
    vmem = pl.BlockSpec(memory_space=pltpu.VMEM)
    hbm = pl.BlockSpec(memory_space=pltpu.HBM)
    shape = jax.ShapeDtypeStruct
    return pl.pallas_call(
        functools.partial(attend_kernel, plan, layer),
        out_shape=[
            shape((rows, D), F32),
            shape((rows, D), BF16),
            shape((rows, D), BF16),
            shape((rows, WQ), BF16),
            shape((ns, micro, plan.tokens, 2 * WK), BF16),
            shape((rows, WQ), BF16),
        ],
        in_specs=[vmem] * 5 + [hbm],
        out_specs=[vmem] * 6,
        scratch_shapes=[
            pltpu.VMEM((D, WIN), BF16),
            pltpu.VMEM((WQ, D), BF16),
            DMA((2,)),
            DMA((ns - 1, micro)),
            DMA((ns, micro)),
        ],
        compiler_params=pltpu.CompilerParams(
            collective_id=collective_id, has_side_effects=True, vmem_limit_bytes=VMEM_LIMIT
        ),
    )(start, gains, *tables, weights)


def return_kernel(plan, layer, *refs):
    (grad_out, grad_moe, middle, start, low, queries, kv, mixed) = refs[:8]
    (gains, cosine, sine, mask, weights) = refs[8:13]
    (result, terms) = refs[13:15]
    (win_v, wout_v, branch, grad_mixed, both, part, got, in_v, out_v, grad_in) = refs[15:25]
    (load_sem, save_in, save_out, send, recv) = refs[25:]
    x, z, s = me()
    tokens, rows, micro, ns = plan.tokens, plan.rows, plan.micro, plan.ns
    length = ns * tokens
    load_in = pltpu.make_async_copy(weights.at[layer, :, pl.ds(0, WIN)], win_v, load_sem.at[0])
    load_out = pltpu.make_async_copy(weights.at[layer, :, pl.ds(WIN, D)], wout_v, load_sem.at[1])
    load_out.start()
    load_in.start()
    greet_shards(plan)

    after = middle[...]
    inverse = lax.rsqrt(jnp.mean(after * after, axis=1, keepdims=True) + epsilon)
    scaled = grad_moe[...] * gains[1:2, :]
    inner = jnp.mean(scaled * after, axis=1, keepdims=True)
    total = grad_out[...].astype(F32) + inverse * scaled - after * (
        inverse * inverse * inverse * inner
    )
    grad_in[...] = total
    branch[...] = total.astype(BF16)
    gain_two = jnp.sum(grad_moe[...] * after * inverse, axis=0, keepdims=True)
    load_out.wait()

    def mix(step, _):
        at = pl.ds(pl.multiple_of(step * 512, 512), 512)
        grad_mixed[:, at] = lax.dot_general(
            branch[...], wout_v[at, :], NARROW, preferred_element_type=F32
        ).astype(BF16)
        return 0

    lax.fori_loop(0, WQ // 512, mix, 0)

    def share(step, m):
        to = (s + step) % ns
        return remote(
            part.at[to, m],
            got.at[s, m],
            send.at[step - 1, m],
            recv.at[s, m],
            (x, z, to),
        )

    def group(turn, _):
        m, pair = turn // KV_HEADS, turn % KV_HEADS
        span = pl.ds(pl.multiple_of(m * tokens, tokens), tokens)
        key_at = pl.ds(pl.multiple_of(pair * HD, HD), HD)
        value_at = pl.ds(pl.multiple_of(WK + pair * HD, HD), HD)
        keys = kv[:, m, :, key_at].reshape(length, HD)
        values = kv[:, m, :, value_at].reshape(length, HD)
        allowed = mask[m] > 0
        grad_keys = jnp.zeros((length, HD), F32)
        grad_values = jnp.zeros((length, HD), F32)
        for i in range(GROUP):
            at = pl.ds(pl.multiple_of((pair * GROUP + i) * HD, HD), HD)
            mine, given = queries[span, at], grad_mixed[span, at]
            probs = weights_of(mine, keys, allowed)
            grad_probs = lax.dot_general(given, values, NARROW, preferred_element_type=F32)
            inside = jnp.sum(grad_probs * probs, axis=1, keepdims=True)
            raw = (probs * (grad_probs - inside) * SCALE).astype(BF16)
            grad_query = jnp.dot(raw, keys, preferred_element_type=F32)
            both[span, at] = turned(grad_query, cosine[span], -sine[span]).astype(BF16)
            grad_keys += lax.dot_general(raw, mine, ACROSS, preferred_element_type=F32)
            grad_values += lax.dot_general(
                probs.astype(BF16), given, ACROSS, preferred_element_type=F32
            )
        part[:, m, :, key_at] = grad_keys.astype(BF16).reshape(ns, tokens, HD)
        part[:, m, :, value_at] = grad_values.astype(BF16).reshape(ns, tokens, HD)

        @pl.when(pair == KV_HEADS - 1)
        def _():
            for step in range(1, ns):
                share(step, m).start()

        return 0

    lax.fori_loop(0, micro * KV_HEADS, group, 0)

    def out_copy(step):
        at = pl.ds(step * 256, 256)
        return pltpu.make_async_copy(out_v.at[at], terms.at[at, pl.ds(WIN, D)], save_out.at[step])

    def in_copy(step):
        at = pl.ds(step * 256, 256)
        return pltpu.make_async_copy(in_v.at[at], terms.at[at, pl.ds(0, WIN)], save_in.at[step])

    def out_tile(step, _):
        at = pl.ds(pl.multiple_of(step * 256, 256), 256)
        out_v[at, :] = lax.dot_general(
            mixed[:, at], branch[...], ACROSS, preferred_element_type=F32
        ).astype(BF16)
        out_copy(step).start()
        return 0

    lax.fori_loop(0, WQ // 256, out_tile, 0)
    load_in.wait()
    for m in range(micro):
        for step in range(1, ns):
            landed(got.at[(s + step) % ns, m], recv.at[(s + step) % ns, m])
        span = slice(m * tokens, (m + 1) * tokens)
        total = part[s, m].astype(F32)
        for step in range(1, ns):
            total += got[(s + step) % ns, m].astype(F32)
        for head in range(KV_HEADS):
            at = slice(head * HD, (head + 1) * HD)
            both[span, WQ + head * HD : WQ + (head + 1) * HD] = turned(
                total[:, at], cosine[span], -sine[span]
            ).astype(BF16)
        both[span, WQ + WK :] = total[:, WK:].astype(BF16)

    def in_tile(step, _):
        at = pl.ds(pl.multiple_of(step * 256, 256), 256)
        in_v[at, : WQ + 2 * WK] = lax.dot_general(
            low[:, at], both[...], ACROSS, preferred_element_type=F32
        ).astype(BF16)
        return 0

    lax.fori_loop(0, D // 256, in_tile, 0)
    grad_normed = []
    for step in range(D // 512):
        at = slice(step * 512, (step + 1) * 512)
        grad_normed.append(
            lax.dot_general(
                both[...], win_v[at, : WQ + 2 * WK], NARROW, preferred_element_type=F32
            )
        )
    grad_normed = jnp.concatenate(grad_normed, axis=1)
    hidden = start[...].astype(F32)
    inverse = lax.rsqrt(jnp.mean(hidden * hidden, axis=1, keepdims=True) + epsilon)
    scaled = grad_normed * gains[0:1, :]
    inner = jnp.mean(scaled * hidden, axis=1, keepdims=True)
    grad_in[...] += inverse * scaled - hidden * (inverse * inverse * inverse * inner)
    result[...] = grad_in[...].astype(result.dtype)
    gain_one = jnp.sum(grad_normed * hidden * inverse, axis=0, keepdims=True)
    place = lax.broadcasted_iota(jnp.int32, (128, D), 0)
    rows_of = jnp.where(place == 0, gain_one, jnp.where(place == 1, gain_two, 0.0))
    in_v[:, WQ + 2 * WK :] = rows_of.T.astype(BF16)
    for step in range(D // 256):
        in_copy(step).start()
    for step in range(D // 256):
        in_copy(step).wait()
        out_copy(step).wait()
    for m in range(micro):
        for step in range(1, ns):
            share(step, m).wait_send()


def return_call(plan, layer, collective_id, grads, saved, gains, tables, weights):
    rows, ns, micro, tokens = plan.rows, plan.ns, plan.micro, plan.tokens
    vmem = pl.BlockSpec(memory_space=pltpu.VMEM)
    hbm = pl.BlockSpec(memory_space=pltpu.HBM)
    shape = jax.ShapeDtypeStruct
    exchange = (ns, micro, tokens, 2 * WK)
    return pl.pallas_call(
        functools.partial(return_kernel, plan, layer),
        out_shape=[
            shape((rows, D), BF16 if layer > 0 else F32),
            shape((D, WIN + D), BF16),
        ],
        in_specs=[vmem] * 12 + [hbm],
        out_specs=[vmem, hbm],
        scratch_shapes=[
            pltpu.VMEM((D, WIN), BF16),
            pltpu.VMEM((WQ, D), BF16),
            pltpu.VMEM((rows, D), BF16),
            pltpu.VMEM((rows, WQ), BF16),
            pltpu.VMEM((rows, WQ + 2 * WK), BF16),
            pltpu.VMEM(exchange, BF16),
            pltpu.VMEM(exchange, BF16),
            pltpu.VMEM((D, WIN), BF16),
            pltpu.VMEM((WQ, D), BF16),
            pltpu.VMEM((rows, D), F32),
            DMA((2,)),
            DMA((D // 256,)),
            DMA((WQ // 256,)),
            DMA((ns - 1, micro)),
            DMA((ns, micro)),
        ],
        compiler_params=pltpu.CompilerParams(
            collective_id=collective_id, has_side_effects=True, vmem_limit_bytes=VMEM_LIMIT
        ),
    )(*grads, *saved, gains, *tables, weights)


def slot_table(plan, routes, gates):
    experts, nz = plan.experts, plan.nz
    named = routes[..., None] == jnp.arange(experts, dtype=jnp.int32)
    gate = jnp.sum(jnp.where(named, gates[..., None], 0.0), axis=2)
    named = jnp.any(named, axis=2)
    earlier = jnp.tril(jnp.ones((plan.tokens, plan.tokens), BF16), -1)
    rank = jnp.einsum("ut,mte->mue", earlier, named.astype(BF16), preferred_element_type=F32)
    table = jnp.stack([jnp.where(named, rank, -1.0), gate])
    table = table.reshape(2, plan.micro, plan.tokens, nz, EXP_DEV).transpose(3, 0, 1, 4, 2)
    return table.reshape(nz, -1, plan.tokens)


def slot_places(plan, table):
    nz = plan.nz
    table = table.reshape(nz, 2, plan.micro, EXP_DEV, plan.tokens)
    rank, gate = table[:, 0], table[:, 1]
    first = jnp.arange(plan.micro, dtype=F32)[:, None, None] * plan.capacity
    place = jnp.where(rank >= 0, rank + first, -1.0).transpose(0, 2, 1, 3)
    hit = place[:, :, None] == jnp.arange(plan.slots, dtype=F32)[:, None, None]
    shape = (nz, EXP_DEV * plan.slots, plan.rows)
    one = hit.astype(BF16).reshape(shape)
    weighted = jnp.where(hit, gate.transpose(0, 2, 1, 3)[:, :, None], 0.0)
    weighted = weighted.astype(BF16).reshape(shape)
    return one, weighted


def shards(
    inputs,
    segments,
    routes,
    gate_weights,
    query_weight,
    key_value_weight,
    output_weight,
    norm_gains,
    expert_gate_up,
    expert_down,
    cotangent,
):
    section = lax.axis_index("section")
    shard_index = lax.axis_index("shard")
    tokens = inputs.shape[1]
    plan = Plan((lax.axis_size("section"), lax.axis_size("expert"), lax.axis_size("shard")), tokens)
    micro, rows, layers = plan.micro, plan.rows, plan.nx
    length = tokens * plan.ns

    def mine(value):
        return lax.dynamic_slice_in_dim(value, section * micro, micro, 0)

    paired = plan.nx == 2 and plan.ns == 4 and query_weight.shape[1] % 96 == 0
    gain_columns = jnp.pad(norm_gains[0].T, ((0, 0), (0, PAD - 2)))
    attention_weights = jnp.concatenate(
        [query_weight[0], key_value_weight[0], gain_columns, output_weight[0]], axis=1
    ).astype(BF16)
    table = slot_table(plan, mine(routes), mine(gate_weights))
    if paired:
        weights, table, wide_in, wide_down = gather_call(
            plan, 1, attention_weights, table, (expert_gate_up[0], expert_down[0])
        )
    else:
        weights = lax.all_gather(
            attention_weights, ("section", "expert", "shard"), axis=0, tiled=True
        )
        table = lax.all_to_all(table, "expert", split_axis=0, concat_axis=0, tiled=True)
        wide_in, wide_down = spread_call(
            plan, 1, expert_gate_up[0].astype(BF16), expert_down[0].astype(BF16)
        )
    weights = weights.reshape(layers, D, WIN + D)
    gains = weights[:, :, PROJ : PROJ + 2].transpose(0, 2, 1).astype(F32)
    wide_in = wide_in.reshape(layers, D, 2 * FF)
    wide_down = wide_down.reshape(layers, FF, D)
    one, weighted = slot_places(plan, table)

    offset = shard_index * tokens
    position = (offset + jnp.arange(tokens, dtype=jnp.int32)).astype(F32)
    frequency = rope_base ** (-jnp.arange(HD // 2, dtype=F32) / (HD // 2))
    angles = position[:, None] * frequency[None, :]
    cosine, sine = jnp.cos(angles), jnp.sin(angles)
    cosine = jnp.tile(jnp.concatenate([cosine, cosine], axis=1), (micro, 1))
    sine = jnp.tile(jnp.concatenate([-sine, sine], axis=1), (micro, 1))
    segment_all = mine(segments)[:, 0]
    segment_own = lax.dynamic_slice_in_dim(segment_all, offset, tokens, 1)
    query_place = offset + jnp.arange(tokens, dtype=jnp.int32)
    key_place = jnp.arange(length, dtype=jnp.int32)
    allowed = (segment_own[:, :, None] == segment_all[:, None, :]) & (
        query_place[:, None] >= key_place[None, :]
    )
    tables = (cosine, sine, allowed.astype(F32))

    hidden = mine(inputs).reshape(rows, D)
    grad = mine(cotangent).reshape(rows, D)
    kept, passed = [], []
    attention_terms = [None] * layers
    expert_terms = [None] * layers
    for layer in range(layers):
        start = hidden.astype(BF16)
        middle, normed, low, queries, kv, mixed = attend_call(
            plan, layer, 2 + layer, start, gains[layer], tables, weights
        )
        kept.append((middle, start, low, queries, kv, mixed))
        if layer == layers - 1 and both_fit(plan):
            hidden, grad_moe, expert_terms[layer] = moe_both_call(
                plan,
                layer,
                2 + layers + layer,
                normed,
                grad,
                one,
                weighted,
                wide_in,
                wide_down,
                middle,
            )
            passed.append(None)
        else:
            hidden, *saved = moe_call(
                plan,
                layer,
                F32 if layer == layers - 1 else BF16,
                2 + layers + layer,
                normed,
                one,
                weighted,
                wide_in,
                wide_down,
                middle,
            )
            passed.append(saved)
    output = hidden.reshape(micro, tokens, D)

    for layer in reversed(range(layers)):
        grad_out = grad.astype(BF16)
        if passed[layer] is not None:
            grad_moe, expert_terms[layer] = moe_back_call(
                plan,
                layer,
                2 + 2 * layers + layer,
                grad_out,
                weighted,
                one,
                wide_in,
                wide_down,
                passed[layer],
            )
        grad, attention_terms[layer] = return_call(
            plan,
            layer,
            2 + 3 * layers + layer,
            (grad_out, grad_moe),
            kept[layer],
            gains[layer],
            tables,
            weights,
        )
    input_grad = grad.reshape(micro, tokens, D)

    if paired:
        term, gate_up_grad, down_grad = reduce_call(
            plan, 2 + 4 * layers, attention_terms, expert_terms
        )
    else:
        gate_up_grad, down_grad = collect_call(plan, 2 + 4 * layers, expert_terms)
        term = lax.psum_scatter(
            jnp.concatenate(attention_terms),
            ("section", "expert", "shard"),
            scatter_dimension=0,
            tiled=True,
        )
    query_grad, key_value_grad, gain_grad, output_weight_grad, gate_up_grad, down_grad = (
        part.astype(F32)[None]
        for part in (
            term[:, :WQ],
            term[:, WQ:PROJ],
            term[:, PROJ : PROJ + 2].T,
            term[:, WIN:],
            gate_up_grad,
            down_grad,
        )
    )
    return (
        output,
        input_grad,
        query_grad,
        key_value_grad,
        output_weight_grad,
        gain_grad,
        gate_up_grad,
        down_grad,
    )


def solution(mesh):
    placed = (
        P(None, ("expert", "shard"), None),
        P(None, "expert", None),
        P(None, ("expert", "shard"), None),
        P(None, ("expert", "shard"), None),
        P("section", ("expert", "shard"), None),
        P("section", ("expert", "shard"), None),
        P("section", ("expert", "shard"), None),
        P("section", None, ("expert", "shard")),
        P("section", "expert", "shard", None),
        P("section", "expert", "shard", None),
        P(None, ("expert", "shard"), None),
    )
    return jax.shard_map(
        shards,
        mesh=mesh,
        in_specs=placed,
        out_specs=(
            P("section", ("expert", "shard"), None),
            P("section", ("expert", "shard"), None),
            P("section", ("expert", "shard"), None),
            P("section", ("expert", "shard"), None),
            P("section", ("expert", "shard"), None),
            P("section", None, ("expert", "shard")),
            P("section", "expert", "shard", None),
            P("section", "expert", "shard", None),
        ),
        check_vma=False,
    )
```

```python
import functools
import math
from types import SimpleNamespace

import jax
import jax.numpy as jnp
from jax import lax
from jax.experimental import pallas as pl
from jax.experimental.pallas import tpu as pltpu
from jax.sharding import PartitionSpec as P

D = 1536
HEADS = 12
KV_HEADS = 2
HD = 128
FF = 768
TOPK = 4
EXP_DEV = 4
MICRO = 4
GROUP = HEADS // KV_HEADS
PAD = 128
WQ = HEADS * HD
WK = KV_HEADS * HD
PROJ = WQ + 2 * WK
WIN = PROJ + PAD
SCALE = HD ** (-0.5)

epsilon = 1e-06
rope_base = 10000.0

MESH = pl.DeviceIdType.MESH
F32 = jnp.float32
BF16 = jnp.bfloat16
DMA = pltpu.SemaphoreType.DMA
VMEM_LIMIT = 62 * 2**20


class Plan:
    def __init__(self, mesh_shape, tokens):
        self.nx, self.nz, self.ns = mesh_shape
        self.tokens = tokens
        self.micro = MICRO // self.nx
        self.rows = self.micro * tokens
        self.ranks = self.nx * self.ns
        self.group = self.ranks // EXP_DEV
        self.halves = self.group // 2
        self.sources = self.ranks // self.halves
        self.experts = EXP_DEV * self.nz
        self.capacity = 5 * tokens * TOPK // (4 * self.experts)
        self.slots = -(-self.micro * self.capacity // 16) * 16
        self.blocks = self.nz // 2
        self.many = self.sources * self.slots


def me():
    return lax.axis_index("section"), lax.axis_index("expert"), lax.axis_index("shard")


def remote(src, dst, send, recv, device):
    return pltpu.make_async_remote_copy(
        src_ref=src,
        dst_ref=dst,
        send_sem=send,
        recv_sem=recv,
        device_id=device,
        device_id_type=MESH,
    )


def landed(ref, sem):
    pltpu.make_async_copy(ref, ref, sem).wait()


def greet_plane(plan, along=False):
    x, z, s = me()
    barrier = pltpu.get_barrier_semaphore()
    mine = x * plan.ns + s
    for step in range(1, plan.ranks):
        other = (mine + step) % plan.ranks
        pl.semaphore_signal(
            barrier, inc=1, device_id=(other // plan.ns, z, other % plan.ns), device_id_type=MESH
        )
    total = plan.ranks - 1
    if along:
        for step in range(1, plan.nz):
            pl.semaphore_signal(
                barrier, inc=1, device_id=(x, (z + step) % plan.nz, s), device_id_type=MESH
            )
        total += plan.nz - 1
    pl.semaphore_wait(barrier, total)


def nearest(place, index, count):
    left = place
    right = count - 1 - place
    short = jnp.minimum(left, right)
    odd = index % 2
    near = place + (1 - 2 * odd) * ((index + 1) // 2)
    far = jnp.where(left < right, index, count - 1 - index)
    return jnp.where(index <= 2 * short, near, far)


NARROW = (((1,), (1,)), ((), ()))
ACROSS = (((0,), (0,)), ((), ()))
TILE = 256
CUTS = 3
CUT = D // CUTS


def moe_stages(plan, backward, r):
    x, z, s = me()
    nz, ns, slots = plan.nz, plan.ns, plan.slots
    rank = x * ns + s
    own_expert = rank // plan.group
    own_turn = (rank % plan.group) // plan.halves
    own_half = rank % plan.halves
    part = ns // plan.halves
    own_source = x * part + s // plan.halves
    chunk = plan.tokens
    own_copy = pltpu.make_async_copy(r.rows_in, r.line.at[z], r.own_sem.at[0])

    def along(block, piece, step, own):
        at = pl.ds(piece * chunk, chunk)
        src = r.rows_in.at[at] if own else r.line.at[block, at]
        sem = r.line_right if step > 0 else r.line_left
        return remote(
            src,
            r.line.at[block, at],
            sem.at[block, piece],
            r.line_recv.at[block, piece],
            (x, z + step, s),
        )

    def owner(block, expert):
        rank_to = expert * plan.group + (block % 2) * plan.halves + s % plan.halves
        return rank_to // ns, rank_to % ns

    def dispatch_copy(block, expert):
        to_x, to_s = owner(block, expert)
        here = (to_x == x) & (to_s == s)
        return here, remote(
            r.sbuf.at[block, expert],
            r.xbuf.at[block // 2, own_source],
            r.to_send.at[block, expert],
            r.to_recv.at[block // 2, own_source],
            (to_x, z, to_s),
        )

    def return_copy(block, cut, source):
        to_x = source // part
        to_s = (source % part) * plan.halves + own_half
        here = (to_x == x) & (to_s == s)
        return here, remote(
            r.ybuf.at[block // 2, cut, source],
            r.rbuf.at[block, cut, own_expert],
            r.back_send.at[block // 2, cut, source],
            r.back_recv.at[block, cut, own_expert],
            (to_x, z, to_s),
        )

    def sum_copy(block, cut):
        rightward = (block > z).astype(jnp.int32)
        to = z - 1 + 2 * rightward
        into = jnp.where((rightward == 1) & (block == to), nz, block)
        return remote(
            r.pbuf.at[block, cut],
            r.qbuf.at[into, cut],
            r.sum_send.at[block, cut],
            r.sum_recv.at[into, cut],
            (x, to, s),
        )

    def begin():
        for piece in range(plan.micro):

            @pl.when(z + 1 < nz)
            def _():
                along(z, piece, 1, True).start()

            @pl.when(z > 0)
            def _():
                along(z, piece, -1, True).start()

        own_copy.start()

    def fetch(index):
        block = nearest(z, index, nz)
        if index == 0:
            own_copy.wait()
        for piece in range(plan.micro):

            @pl.when(block < z)
            def _():
                along(block, piece, 1, False).wait_recv()

                @pl.when(z + 1 < nz)
                def _():
                    along(block, piece, 1, False).start()

            @pl.when(block > z)
            def _():
                along(block, piece, -1, False).wait_recv()

                @pl.when(z > 0)
                def _():
                    along(block, piece, -1, False).start()

    def put(index):
        block = nearest(z, index, nz)

        def lay(step, _):
            at = pl.ds(pl.multiple_of(step * TILE, TILE), TILE)
            laid = jnp.dot(r.put[block], r.line[block, :, at], preferred_element_type=F32)
            r.sbuf[block, :, :, at] = laid.astype(BF16).reshape(EXP_DEV, slots, TILE)
            return 0

        lax.fori_loop(0, D // TILE, lay, 0)
        for expert in range(EXP_DEV):
            here, copy = dispatch_copy(block, expert)

            @pl.when(here)
            def _():
                pltpu.make_async_copy(
                    r.sbuf.at[block, expert],
                    r.xbuf.at[block // 2, own_source],
                    r.to_recv.at[block // 2, own_source],
                ).start()

            @pl.when(jnp.logical_not(here))
            def _():
                copy.start()

    def compute(block, now):
        pair = block // 2
        for source in range(plan.sources):
            landed(r.xbuf.at[pair, source], r.to_recv.at[pair, source])
        few = plan.sources // 2
        span = few * slots

        def middle(step, _):
            rows = pl.ds(pl.multiple_of(step * span, 16), span)
            taken = r.xbuf[pair, pl.ds(step * few, few)].reshape(span, D)
            if backward:
                grad_hidden = lax.dot_general(
                    taken, r.wdown_v[...], NARROW, preferred_element_type=F32
                )
                gate = r.gbuf[pair, rows, :FF].astype(F32)
                up = r.gbuf[pair, rows, FF:].astype(F32)
                sig = 1.0 / (1.0 + jnp.exp(-gate))
                gs = gate * sig
                grad_gate = grad_hidden * up * (sig + gs * (1.0 - sig))
                r.gbuf[pair, rows, :FF] = grad_gate.astype(BF16)
                r.gbuf[pair, rows, FF:] = (grad_hidden * gs).astype(BF16)
            else:
                gate = jnp.dot(taken, r.win_v[:, :FF], preferred_element_type=F32)
                up = jnp.dot(taken, r.win_v[:, FF:], preferred_element_type=F32)
                r.gbuf[pair, rows, :FF] = gate.astype(BF16)
                r.gbuf[pair, rows, FF:] = up.astype(BF16)
                r.zbuf[pair, rows] = (gate / (1.0 + jnp.exp(-gate)) * up).astype(BF16)
            return 0

        lax.fori_loop(0, 2, middle, 0)

        def last(cut, _):
            at = pl.ds(pl.multiple_of(cut * CUT, CUT), CUT)
            if backward:
                result = lax.dot_general(
                    r.gbuf[pair], r.win_v[at, :], NARROW, preferred_element_type=F32
                )
            else:
                result = jnp.dot(r.zbuf[pair], r.wdown_v[:, at], preferred_element_type=F32)
            r.ybuf[pair, cut] = result.astype(BF16).reshape(plan.sources, slots, CUT)
            if now:
                return_cut(block, cut)
            return 0

        lax.fori_loop(0, CUTS, last, 0)

    def return_cut(block, cut):
        pair = block // 2
        for source in range(plan.sources):
            here, copy = return_copy(block, cut, source)

            @pl.when(here)
            def _():
                pltpu.make_async_copy(
                    r.ybuf.at[pair, cut, source],
                    r.rbuf.at[block, cut, own_expert],
                    r.back_recv.at[block, cut, own_expert],
                ).start()

            @pl.when(jnp.logical_not(here))
            def _():
                copy.start()

    def own_turn_do(index, act):
        block = nearest(z, index, nz)

        @pl.when(block % 2 == own_turn)
        def _():
            act(block)

    def give_back(block):
        for cut in range(CUTS):
            return_cut(block, cut)

    def take(index):
        block = nearest(z, index, nz)
        origin = ((block < z) & (z == nz - 1)) | ((block > z) & (z == 0))
        for cut in range(CUTS):
            for expert in range(EXP_DEV):
                landed(r.rbuf.at[block, cut, expert], r.back_recv.at[block, cut, expert])
            got = lax.dot_general(
                r.take[block],
                r.rbuf[block, cut].reshape(EXP_DEV * slots, CUT),
                (((0,), (0,)), ((), ())),
                preferred_element_type=F32,
            )

            @pl.when(block == z)
            def _():
                at = pl.ds(cut * CUT, CUT)
                if backward:
                    r.out[:, at] = got
                else:
                    r.out[:, at] += got

            @pl.when(block != z)
            def _():
                r.pbuf[block, cut] = got.astype(BF16)

            @pl.when(origin)
            def _():
                sum_copy(block, cut).start()

    def relay(turn):
        lower = z < nz // 2
        first = jnp.where(lower, nz - 1 - z, z)
        early = turn < first
        ahead = jnp.where(early, first - turn, nz - 1 - turn)
        rightward = lower == early
        block = jnp.where(rightward, z + ahead, z - ahead)

        @pl.when((z > 0) & (z < nz - 1))
        def _():
            for cut in range(CUTS):
                landed(r.qbuf.at[block, cut], r.sum_recv.at[block, cut])
                r.pbuf[block, cut] = (
                    r.pbuf[block, cut].astype(F32) + r.qbuf[block, cut].astype(F32)
                ).astype(BF16)
                sum_copy(block, cut).start()

    def finish():
        for cut in range(CUTS):
            at = pl.ds(cut * CUT, CUT)

            @pl.when(z + 1 < nz)
            def _():
                landed(r.qbuf.at[z, cut], r.sum_recv.at[z, cut])
                r.out[:, at] += r.qbuf[z, cut].astype(F32)

            @pl.when(z > 0)
            def _():
                landed(r.qbuf.at[nz, cut], r.sum_recv.at[nz, cut])
                r.out[:, at] += r.qbuf[nz, cut].astype(F32)

    def free_put(block):
        for piece in range(plan.micro):

            @pl.when((block <= z) & (z + 1 < nz))
            def _():
                along(block, piece, 1, False).wait_send()

            @pl.when((block >= z) & (z > 0))
            def _():
                along(block, piece, -1, False).wait_send()

        for expert in range(EXP_DEV):
            here, copy = dispatch_copy(block, expert)

            @pl.when(jnp.logical_not(here))
            def _():
                copy.wait_send()

    def free_back(block):
        for cut in range(CUTS):
            for source in range(plan.sources):
                here, copy = return_copy(block, cut, source)

                @pl.when(jnp.logical_not(here))
                def _():
                    copy.wait_send()

    def free_sum(block):
        @pl.when(block != z)
        def _():
            for cut in range(CUTS):
                sum_copy(block, cut).wait_send()

    def free_all():
        def free(block, _):
            free_put(block)

            @pl.when(block % 2 == own_turn)
            def _():
                free_back(block)

            free_sum(block)
            return 0

        lax.fori_loop(0, nz, free, 0)

    return SimpleNamespace(
        begin=begin,
        fetch=fetch,
        put=put,
        expert=lambda index, now=True: own_turn_do(index, lambda block: compute(block, now)),
        give_back=lambda index: own_turn_do(index, give_back),
        take=take,
        relay=relay,
        finish=finish,
        free_put=lambda index: free_put(nearest(z, index, nz)),
        free_back=lambda index: own_turn_do(index, free_back),
        free_sum=lambda index: free_sum(nearest(z, index, nz)),
        free_all=free_all,
    )


def late_relays(nz):
    return (2, 1) if nz == 4 else range(1, nz - 1)


def first_part(plan, stages, loaded):
    last = plan.nz - 1
    stages.fetch(0)
    stages.put(0)
    loaded()
    for index in range(1, plan.nz):
        stages.fetch(index)
        stages.put(index)
        stages.expert(index - 1, 1 < index < last)


def second_part(plan, stages, steps=()):
    last = plan.nz - 1
    steps = iter(steps)

    def another():
        next(steps, lambda: None)()

    for index in range(1, plan.nz - 2):
        stages.take(index)
    stages.expert(last)
    another()
    stages.take(last)
    stages.give_back(last - 1)
    stages.give_back(0)
    another()
    stages.relay(0)
    stages.take(last - 1)
    another()
    stages.take(0)


def weight_tiles(plan, given, hidden, grad_both, grad_rows, in_term, down_term, tile_v, sem):
    counts = (D // TILE, FF // TILE)

    def copy(tile):
        if isinstance(tile, int) and tile >= counts[0]:
            to = down_term.at[pl.ds((tile - counts[0]) * TILE, TILE)]
        else:
            to = in_term.at[pl.ds(pl.multiple_of(tile * TILE, TILE), TILE)]
        return pltpu.make_async_copy(tile_v.at[tile % 2], to, sem.at[tile % 2])

    def summed(left, right):
        total = lax.dot_general(left(0), right(0), ACROSS, preferred_element_type=F32)
        for pair in range(1, plan.blocks):
            total += lax.dot_general(left(pair), right(pair), ACROSS, preferred_element_type=F32)
        return total.astype(BF16)

    def rows_of(ref, pair, at):
        return ref[pair, :, :, at].reshape(plan.many, -1)

    def in_tile(tile, _):
        @pl.when(tile >= 2)
        def _():
            copy(tile % 2).wait()

        at = pl.ds(pl.multiple_of(tile * TILE, TILE), TILE)
        tile_v[tile % 2] = summed(lambda p: rows_of(given, p, at), lambda p: grad_both[p])
        copy(tile).start()
        return 0

    def first():
        lax.fori_loop(0, counts[0], in_tile, 0)

    def second():
        for step in range(counts[1]):
            tile = counts[0] + step
            copy(tile % 2).wait()
            at = slice(step * TILE, (step + 1) * TILE)
            tile_v[tile % 2] = summed(
                lambda p: hidden[p, :, at], lambda p: grad_rows[p].reshape(plan.many, D)
            )
            copy(tile).start()

    def finish():
        for tile in range(sum(counts) - 2, sum(counts)):
            copy(tile).wait()

    return first, second, finish


PASS_BUFFERS = ("line", "xbuf", "rbuf", "qbuf")
PASS_SEMAPHORES = (
    "own_sem",
    "line_recv",
    "line_right",
    "line_left",
    "to_send",
    "to_recv",
    "back_send",
    "back_recv",
    "sum_send",
    "sum_recv",
)
SHARED_BUFFERS = ("sbuf", "ybuf", "pbuf", "win_v", "wdown_v", "gbuf", "zbuf")


def pass_scratch(plan):
    nz, blocks, slots, sources, rows = plan.nz, plan.blocks, plan.slots, plan.sources, plan.rows
    return [
        pltpu.VMEM((nz, rows, D), BF16),
        pltpu.VMEM((blocks, sources, slots, D), BF16),
        pltpu.VMEM((nz, CUTS, EXP_DEV, slots, CUT), BF16),
        pltpu.VMEM((nz + 1, CUTS, rows, CUT), BF16),
        DMA((1,)),
        DMA((nz, plan.micro)),
        DMA((nz, plan.micro)),
        DMA((nz, plan.micro)),
        DMA((nz, EXP_DEV)),
        DMA((blocks, sources)),
        DMA((blocks, CUTS, sources)),
        DMA((nz, CUTS, EXP_DEV)),
        DMA((nz, CUTS)),
        DMA((nz + 1, CUTS)),
    ]


def shared_scratch(plan):
    nz, blocks, slots, many = plan.nz, plan.blocks, plan.slots, plan.many
    return [
        pltpu.VMEM((nz, EXP_DEV, slots, D), BF16),
        pltpu.VMEM((blocks, CUTS, plan.sources, slots, CUT), BF16),
        pltpu.VMEM((nz, CUTS, plan.rows, CUT), BF16),
        pltpu.VMEM((D, 2 * FF), BF16),
        pltpu.VMEM((FF, D), BF16),
        pltpu.VMEM((blocks, many, 2 * FF), BF16),
        pltpu.VMEM((blocks, many, FF), BF16),
    ]


PASS_NAMES = PASS_BUFFERS + PASS_SEMAPHORES


def named(names, refs):
    return dict(zip(names, refs, strict=True))


def run_copies(copies):
    for copy in copies:
        copy.start()

    def wait():
        for copy in copies:
            copy.wait()

    return wait


def moe_kernel(plan, layer, *refs):
    rows_in, put, take, w_in, w_down, base, result, sent, gate_up, hidden = refs[:10]
    count = len(PASS_NAMES)
    r = SimpleNamespace(
        rows_in=rows_in,
        put=put,
        take=take,
        **named(PASS_NAMES, refs[10 : 10 + count]),
        **named(SHARED_BUFFERS, refs[10 + count : -3]),
    )
    out, load_sem, save_sem = refs[-3:]
    r.out = out
    loaded = run_copies(
        [
            pltpu.make_async_copy(w_in.at[layer], r.win_v, load_sem.at[0]),
            pltpu.make_async_copy(w_down.at[layer], r.wdown_v, load_sem.at[1]),
            pltpu.make_async_copy(base, out, load_sem.at[2]),
        ]
    )
    greet_plane(plan, along=True)
    stages = moe_stages(plan, False, r)
    stages.begin()
    first_part(plan, stages, loaded)
    second_part(plan, stages)
    saved = run_copies(
        [
            pltpu.make_async_copy(r.xbuf, sent, save_sem.at[0]),
            pltpu.make_async_copy(r.gbuf, gate_up, save_sem.at[1]),
            pltpu.make_async_copy(r.zbuf, hidden, save_sem.at[2]),
        ]
    )
    for turn in late_relays(plan.nz):
        stages.relay(turn)
    stages.finish()
    result[...] = out[...].astype(result.dtype)
    stages.free_all()
    saved()


def moe_back_kernel(plan, layer, *refs):
    rows_in, put, take, w_in, w_down, sent, gate_up, hidden, out, in_term, down_term = refs[:11]
    count = len(PASS_NAMES)
    r = SimpleNamespace(
        rows_in=rows_in,
        put=put,
        take=take,
        out=out,
        **named(PASS_NAMES, refs[11 : 11 + count]),
        **named(SHARED_BUFFERS, refs[11 + count : -4]),
    )
    given, tile_v, load_sem, tile_sem = refs[-4:]
    loaded = run_copies(
        [
            pltpu.make_async_copy(w_in.at[layer], r.win_v, load_sem.at[0]),
            pltpu.make_async_copy(w_down.at[layer], r.wdown_v, load_sem.at[1]),
            pltpu.make_async_copy(gate_up, r.gbuf, load_sem.at[2]),
            pltpu.make_async_copy(sent, given, load_sem.at[3]),
            pltpu.make_async_copy(hidden, r.zbuf, load_sem.at[4]),
        ]
    )
    greet_plane(plan, along=True)
    stages = moe_stages(plan, True, r)
    first, second, finish = weight_tiles(
        plan, given, r.zbuf, r.gbuf, r.xbuf, in_term, down_term, tile_v, tile_sem
    )
    stages.begin()
    first_part(plan, stages, loaded)
    second_part(plan, stages, (first, second))
    for turn in late_relays(plan.nz):
        stages.relay(turn)
    stages.finish()
    stages.free_all()
    finish()


def moe_both_kernel(plan, layer, *refs):
    rows_in, rows_back, one, weighted, w_in, w_down, base = refs[:7]
    out, out_back, in_term, down_term = refs[7:11]
    count = len(PASS_NAMES)
    shared = named(SHARED_BUFFERS, refs[11 + 2 * count : -2])
    ahead = SimpleNamespace(
        rows_in=rows_in,
        put=one,
        take=weighted,
        out=out,
        **named(PASS_NAMES, refs[11 : 11 + count]),
        **shared,
    )
    back = SimpleNamespace(
        rows_in=rows_back,
        put=weighted,
        take=one,
        out=out_back,
        **named(PASS_NAMES, refs[11 + count : 11 + 2 * count]),
        **shared,
    )
    load_sem, tile_sem = refs[-2:]
    loaded = run_copies(
        [
            pltpu.make_async_copy(w_in.at[layer], ahead.win_v, load_sem.at[0]),
            pltpu.make_async_copy(w_down.at[layer], ahead.wdown_v, load_sem.at[1]),
            pltpu.make_async_copy(base, out, load_sem.at[2]),
        ]
    )
    greet_plane(plan, along=True)
    forward = moe_stages(plan, False, ahead)
    backward = moe_stages(plan, True, back)
    first, second, finish = weight_tiles(
        plan,
        ahead.xbuf,
        back.zbuf,
        back.gbuf,
        back.xbuf,
        in_term,
        down_term,
        ahead.line,
        tile_sem,
    )
    nz, last = plan.nz, plan.nz - 1
    forward.begin()
    first_part(plan, forward, loaded)
    backward.begin()
    order = list(reversed(range(nz)))
    relays = list(late_relays(nz))

    def arrive():
        for index in range(3, nz):
            backward.fetch(index)

    second_part(
        plan,
        forward,
        (
            lambda: backward.fetch(1),
            lambda: backward.fetch(2),
            arrive,
        ),
    )
    backward.fetch(0)

    def put(index):
        forward.free_put(index)
        backward.put(index)

    def expert(index):
        forward.free_back(index)
        backward.expert(index)

    def take(index):
        forward.free_sum(index)
        backward.take(index)

    put(order[0])
    for turn in relays[: len(relays) // 2]:
        forward.relay(turn)
    put(order[1])
    expert(order[0])
    for turn in relays[len(relays) // 2 :]:
        forward.relay(turn)
    put(order[2])
    expert(order[1])
    forward.finish()
    take(order[0])
    for place in range(3, nz):
        put(order[place])
        expert(order[place - 1])
        take(order[place - 2])
    backward.relay(0)
    expert(order[-1])
    first()
    take(order[-2])
    for turn in relays:
        backward.relay(turn)
    second()
    take(order[-1])
    backward.finish()
    backward.free_all()
    finish()


def moe_specs(plan, collective_id):
    return dict(
        compiler_params=pltpu.CompilerParams(
            collective_id=collective_id, has_side_effects=True, vmem_limit_bytes=VMEM_LIMIT
        ),
    )


def saved_shapes(plan):
    return [
        jax.ShapeDtypeStruct((plan.blocks, plan.sources, plan.slots, D), BF16),
        jax.ShapeDtypeStruct((plan.blocks, plan.many, 2 * FF), BF16),
        jax.ShapeDtypeStruct((plan.blocks, plan.many, FF), BF16),
    ]


TERMS = [jax.ShapeDtypeStruct((D, 2 * FF), BF16), jax.ShapeDtypeStruct((FF, D), BF16)]


def moe_call(plan, layer, kind, collective_id, rows_in, put, take, w_in, w_down, base):
    vmem = pl.BlockSpec(memory_space=pltpu.VMEM)
    hbm = pl.BlockSpec(memory_space=pltpu.HBM)
    return pl.pallas_call(
        functools.partial(moe_kernel, plan, layer),
        out_shape=[jax.ShapeDtypeStruct((plan.rows, D), kind)] + saved_shapes(plan),
        in_specs=[vmem] * 3 + [hbm] * 3,
        out_specs=[vmem] + [hbm] * 3,
        scratch_shapes=pass_scratch(plan) + shared_scratch(plan) + [pltpu.VMEM((plan.rows, D), F32), DMA((3,)), DMA((3,))],
        **moe_specs(plan, collective_id),
    )(rows_in, put, take, w_in, w_down, base)


def moe_back_call(plan, layer, collective_id, rows_in, put, take, w_in, w_down, saved):
    vmem = pl.BlockSpec(memory_space=pltpu.VMEM)
    hbm = pl.BlockSpec(memory_space=pltpu.HBM)
    out, *terms = pl.pallas_call(
        functools.partial(moe_back_kernel, plan, layer),
        out_shape=[jax.ShapeDtypeStruct((plan.rows, D), F32)] + TERMS,
        in_specs=[vmem] * 3 + [hbm] * 5,
        out_specs=[vmem] + [hbm] * 2,
        scratch_shapes=pass_scratch(plan)
        + shared_scratch(plan)
        + [
            pltpu.VMEM((plan.blocks, plan.sources, plan.slots, D), BF16),
            pltpu.VMEM((2, TILE, D), BF16),
            DMA((5,)),
            DMA((2,)),
        ],
        **moe_specs(plan, collective_id),
    )(rows_in, put, take, w_in, w_down, *saved)
    return out, terms


def both_fit(plan):
    scratch = pass_scratch(plan) * 2 + shared_scratch(plan)
    words = sum(
        math.prod(part.shape) for part in scratch if getattr(part, "dtype", None) == BF16
    )
    return 2 * words + 10 * 2**20 < VMEM_LIMIT and plan.rows == TILE


def moe_both_call(plan, layer, collective_id, rows_in, rows_back, one, weighted, w_in, w_down, base):
    vmem = pl.BlockSpec(memory_space=pltpu.VMEM)
    hbm = pl.BlockSpec(memory_space=pltpu.HBM)
    out, out_back, *terms = pl.pallas_call(
        functools.partial(moe_both_kernel, plan, layer),
        out_shape=[jax.ShapeDtypeStruct((plan.rows, D), F32)] * 2 + TERMS,
        in_specs=[vmem, hbm, vmem, vmem] + [hbm] * 3,
        out_specs=[vmem] * 2 + [hbm] * 2,
        scratch_shapes=pass_scratch(plan) * 2
        + shared_scratch(plan)
        + [DMA((3,)), DMA((2,))],
        **moe_specs(plan, collective_id),
    )(rows_in, rows_back, one, weighted, w_in, w_down, base)
    return out, out_back, terms


def expert_spread(plan, ins, outs, send, recv, pass_send, pass_recv):
    x, z, s = me()
    nx, ns, group = plan.nx, plan.ns, plan.group
    rank = x * ns + s
    own_expert, own_part = rank // group, rank % group
    own = [(layer, k) for layer in range(nx) for k in range(ns // group)]

    def first(expert, which):
        to = expert * group + s % group
        return to == rank, remote(
            ins[which].at[expert],
            outs[which].at[x, s],
            send.at[expert, which],
            recv.at[x, s, which],
            (to // ns, z, to % ns),
        )

    def onward(layer, source, step, which):
        to = own_expert * group + (own_part + step) % group
        return remote(
            outs[which].at[layer, source],
            outs[which].at[layer, source],
            pass_send.at[layer, source, step - 1, which],
            pass_recv.at[layer, source, which],
            (to // ns, z, to % ns),
        )

    def start(expert, which):
        here, copy = first(expert, which)

        @pl.when(here)
        def _():
            pltpu.make_async_copy(
                ins[which].at[expert], outs[which].at[x, s], recv.at[x, s, which]
            ).start()

        @pl.when(jnp.logical_not(here))
        def _():
            copy.start()

    def pass_on():
        for layer, k in own:
            source = k * group + own_part
            for which in range(2):
                landed(outs[which].at[layer, source], recv.at[layer, source, which])
                for step in range(1, group):
                    onward(layer, source, step, which).start()

    def finish():
        for layer, k in own:
            for step in range(1, group):
                source = k * group + (own_part + step) % group
                for which in range(2):
                    landed(outs[which].at[layer, source], pass_recv.at[layer, source, which])
        for which in range(2):
            for expert in range(EXP_DEV):
                here, copy = first(expert, which)

                @pl.when(jnp.logical_not(here))
                def _():
                    copy.wait_send()

        for layer, k in own:
            source = k * group + own_part
            for which in range(2):
                for step in range(1, group):
                    onward(layer, source, step, which).wait_send()

    return start, pass_on, finish


def spread_scratch(plan):
    nx, ns, group = plan.nx, plan.ns, plan.group
    return [
        DMA((EXP_DEV, 2)),
        DMA((nx, ns, 2)),
        DMA((nx, ns, group - 1, 2)),
        DMA((nx, ns, 2)),
    ]


def spread_kernel(plan, *refs):
    greet_plane(plan)
    start, pass_on, finish = expert_spread(plan, refs[:2], refs[2:4], *refs[4:])
    for which in range(2):
        for expert in range(EXP_DEV):
            start(expert, which)
    pass_on()
    finish()


def spread_call(plan, collective_id, gate_up, down):
    hbm = pl.BlockSpec(memory_space=pltpu.HBM)
    vmem = pl.BlockSpec(memory_space=pltpu.VMEM)
    outs = [
        jax.ShapeDtypeStruct((plan.nx, plan.ns) + part.shape[1:], BF16) for part in (gate_up, down)
    ]
    return pl.pallas_call(
        functools.partial(spread_kernel, plan),
        out_shape=outs,
        in_specs=[vmem, vmem],
        out_specs=[hbm, hbm],
        scratch_shapes=spread_scratch(plan),
        compiler_params=pltpu.CompilerParams(
            collective_id=collective_id, has_side_effects=True, vmem_limit_bytes=VMEM_LIMIT
        ),
    )(gate_up, down)


def gather_kernel(plan, *refs):
    piece, table, wide_ins = refs[0], refs[1], refs[2:4]
    out, table_out, wide_outs = refs[4], refs[5], refs[6:8]
    (line_recv, right, left, copy_sem, plane_recv, to_core, to_x, to_y) = refs[8:16]
    (up_recv, up_right, up_left, table_send, table_recv) = refs[16:21]
    wide_v, low_v, load_sem = refs[21:23], refs[23:25], refs[25]
    x, z, s = me()
    nz = plan.nz
    row, side = s // 2, s % 2
    over = (s + 2) % 4
    loads = [
        pltpu.make_async_copy(wide_ins[which].at[expert], wide_v[which].at[expert], load_sem.at[which, expert])
        for which in range(2)
        for expert in range(EXP_DEV)
    ]
    for load in loads:
        load.start()
    greet_plane(plan, along=True)
    start, pass_on, finish = expert_spread(plan, low_v, wide_outs, *refs[26:])
    third = piece.shape[0] // 3
    parts = (
        (pl.ds(0, 2 * third), pl.ds(0, third), pl.ds(third, third)),
        (
            pl.ds(2 * third, third),
            pl.ds(2 * third, third // 2),
            pl.ds(2 * third + third // 2, third // 2),
        ),
    )
    core = (x, z, s + 1 - 2 * side)
    across_x = (1 - x, z, s)
    across_y = (x, z, over)

    def along(block, step, own):
        rows = parts[0][0]
        place = out.at[x, block, s, rows]
        sem = right if step > 0 else left
        return remote(
            piece.at[rows] if own else place,
            place,
            sem.at[block],
            line_recv.at[block],
            (x, z + step, s),
        )

    def upward(block, layer, to_row, step, own=False):
        rows = parts[1][0]
        place = out.at[layer, block, to_row * 2 + side, rows]
        sem = up_right if step > 0 else up_left
        return remote(
            piece.at[rows] if own else place,
            place,
            sem.at[block, layer, to_row],
            up_recv.at[block, layer, to_row],
            (x, z + step, s),
        )

    def passed(layer, block, shard, part, kind, sem, to, own=False):
        rows = parts[part][kind]
        place = out.at[layer, block, shard, rows]
        return remote(
            piece.at[rows] if own else place,
            place,
            sem.at[layer, block, shard // 2, part],
            plane_recv.at[layer, block, shard, part, kind],
            to,
        )

    def arrived(layer, block, shard, part, kind):
        landed(
            out.at[layer, block, shard, parts[part][kind]],
            plane_recv.at[layer, block, shard, part, kind],
        )

    def column_copies(block, part, own=False, ways=3):
        ways = ((to_x, across_x), (to_y, across_y), (to_core, core))[:ways]
        return [passed(x, block, s, part, 0, sem, to, own) for sem, to in ways]

    def neighbour_copies(block, part):
        return [
            passed(1 - x, block, s, part, 1, to_y, across_y),
            passed(1 - x, block, s, part, 0, to_core, core),
            passed(x, block, over, part, 2, to_x, across_x),
            passed(x, block, over, part, 0, to_core, core),
        ]

    def send_up(block, layer, to_row, own=False):
        @pl.when((block <= z) & (z + 1 < nz))
        def _():
            upward(block, layer, to_row, 1, own).start()

        @pl.when((block >= z) & (z > 0))
        def _():
            upward(block, layer, to_row, -1, own).start()

    def neighbours_of(block, part):
        copies = neighbour_copies(block, part)
        arrived(1 - x, block, s, part, 0)
        copies[0].start()
        copies[1].start()
        arrived(x, block, over, part, 0)
        copies[2].start()
        copies[3].start()

    def opposite_of(block, part):
        arrived(1 - x, block, over, part, 1)
        arrived(1 - x, block, over, part, 2)
        passed(1 - x, block, over, part, 0, to_core, core).start()

    @pl.when(z + 1 < nz)
    def _():
        along(z, 1, True).start()

    @pl.when(z > 0)
    def _():
        along(z, -1, True).start()

    send_up(z, x, row, True)
    own = pltpu.make_async_copy(piece, out.at[x, z, s], copy_sem.at[0])
    own.start()
    for part in (1, 0):
        for copy in column_copies(z, part, True):
            copy.start()

    def table_copy(step):
        to = (z + step) % nz
        return remote(
            table.at[to], table_out.at[z], table_send.at[step - 1], table_recv.at[z], (x, to, s)
        )

    for step in range(1, nz):
        table_copy(step).start()
    table_out[z] = table[z]
    neighbours_of(z, 1)
    send_up(z, 1 - x, row)
    send_up(z, x, 1 - row)
    opposite_of(z, 1)
    send_up(z, 1 - x, 1 - row)

    def column(index, _):
        block = nearest(z, index, nz)

        @pl.when(block < z)
        def _():
            along(block, 1, False).wait_recv()

            @pl.when(z + 1 < nz)
            def _():
                along(block, 1, False).start()

        @pl.when(block > z)
        def _():
            along(block, -1, False).wait_recv()

            @pl.when(z > 0)
            def _():
                along(block, -1, False).start()

        for copy in column_copies(block, 0):
            copy.start()
        for layer in range(2):
            for to_row in range(2):
                upward(block, layer, to_row, 1).wait_recv()
                send_up(block, layer, to_row)
                passed(layer, block, to_row * 2 + side, 1, 0, to_core, core).start()
        return 0

    def neighbours(index, _):
        neighbours_of(nearest(z, index, nz), 0)
        return 0

    def opposite(index, _):
        opposite_of(nearest(z, index, nz), 0)
        return 0

    for place, load in enumerate(loads):
        which, expert = place // EXP_DEV, place % EXP_DEV
        load.wait()
        low_v[which][expert] = wide_v[which][expert].astype(BF16)
        start(expert, which)
    lax.fori_loop(1, nz, column, 0)
    lax.fori_loop(0, nz, neighbours, 0)
    lax.fori_loop(0, nz, opposite, 0)
    own.wait()
    pass_on()
    for step in range(1, nz):
        block = (z + step) % nz
        landed(table_out.at[block], table_recv.at[block])
        table_copy(step).wait_send()

    def drain(block, _):
        other = s + 1 - 2 * side

        @pl.when((block <= z) & (z + 1 < nz))
        def _():
            along(block, 1, False).wait_send()

        @pl.when((block >= z) & (z > 0))
        def _():
            along(block, -1, False).wait_send()

        for layer in range(2):
            for to_row in range(2):
                for part in range(2):
                    arrived(layer, block, to_row * 2 + other % 2, part, 0)
                    passed(layer, block, to_row * 2 + side, part, 0, to_core, core).wait_send()

                @pl.when((block <= z) & (z + 1 < nz))
                def _():
                    upward(block, layer, to_row, 1).wait_send()

                @pl.when((block >= z) & (z > 0))
                def _():
                    upward(block, layer, to_row, -1).wait_send()

        def plane(part):
            for copy in column_copies(block, part, ways=2):
                copy.wait_send()
            passed(1 - x, block, s, part, 1, to_y, across_y).wait_send()
            passed(x, block, over, part, 2, to_x, across_x).wait_send()

        plane(0)

        @pl.when(block == z)
        def _():
            plane(1)

        return 0

    lax.fori_loop(0, nz, drain, 0)
    finish()


def gather_call(plan, collective_id, attention, table, experts):
    hbm = pl.BlockSpec(memory_space=pltpu.HBM)
    vmem = pl.BlockSpec(memory_space=pltpu.VMEM)
    nx, nz, ns = plan.nx, plan.nz, plan.ns
    outs = [
        jax.ShapeDtypeStruct((nx, nz, ns) + attention.shape, BF16),
        jax.ShapeDtypeStruct(table.shape, F32),
    ]
    outs += [jax.ShapeDtypeStruct((nx, ns) + part.shape[1:], BF16) for part in experts]
    return pl.pallas_call(
        functools.partial(gather_kernel, plan),
        out_shape=outs,
        in_specs=[vmem, vmem, hbm, hbm],
        out_specs=[hbm, vmem, hbm, hbm],
        scratch_shapes=[
            DMA((nz,)),
            DMA((nz,)),
            DMA((nz,)),
            DMA((1,)),
            DMA((nx, nz, ns, 2, 3)),
            DMA((nx, nz, 2, 2)),
            DMA((nx, nz, 2, 2)),
            DMA((nx, nz, 2, 2)),
            DMA((nz, nx, 2)),
            DMA((nz, nx, 2)),
            DMA((nz, nx, 2)),
            DMA((nz - 1,)),
            DMA((nz,)),
        ]
        + [pltpu.VMEM(part.shape, F32) for part in experts]
        + [pltpu.VMEM(part.shape, BF16) for part in experts]
        + [DMA((2, EXP_DEV))]
        + spread_scratch(plan),
        compiler_params=pltpu.CompilerParams(
            collective_id=collective_id, has_side_effects=True, vmem_limit_bytes=VMEM_LIMIT
        ),
    )(attention, table, *experts)


def expert_collect(plan, ins, outs, parts, stage, load, swap_send, swap_recv, send, recv):
    x, z, s = me()
    ns, group = plan.ns, plan.group
    rank = x * ns + s
    own_expert, own_part = rank // group, rank % group
    order = [(k, kind) for kind in range(len(ins)) for k in range(ns // group)]

    def swap(k, step, kind):
        part_to = (own_part + step) % group
        to = own_expert * group + part_to
        return remote(
            ins[kind].at[k * group + part_to],
            parts[kind].at[step - 1, k],
            swap_send.at[step - 1, k, kind],
            swap_recv.at[step - 1, k, kind],
            (to // ns, z, to % ns),
        )

    def own(k, kind):
        return pltpu.make_async_copy(
            ins[kind].at[k * group + own_part], stage[kind].at[k], load.at[k, kind]
        )

    def home(k, kind):
        layer, which = kind // 2, kind % 2
        here = (x == layer) & (s == k * group + own_part)
        return here, remote(
            stage[kind].at[k],
            outs[which].at[own_expert],
            send.at[k, kind],
            recv.at[own_expert, which],
            (layer, z, k * group + own_part),
        )

    def start():
        for k, kind in order:
            own(k, kind).start()
            for step in range(1, group):
                swap(k, step, kind).start()

    def add(place):
        k, kind = order[place]
        own(k, kind).wait()
        for step in range(1, group):
            swap(k, step, kind).wait_recv()
        total = stage[kind][k].astype(F32)
        for step in range(1, group):
            total += parts[kind][step - 1, k].astype(F32)
        stage[kind][k] = total.astype(BF16)
        here, copy = home(k, kind)

        @pl.when(here)
        def _():
            which = kind % 2
            pltpu.make_async_copy(
                stage[kind].at[k], outs[which].at[own_expert], recv.at[own_expert, which]
            ).start()

        @pl.when(jnp.logical_not(here))
        def _():
            copy.start()

    def finish():
        for which in range(2):
            for expert in range(EXP_DEV):
                landed(outs[which].at[expert], recv.at[expert, which])
        for k, kind in order:
            for step in range(1, group):
                swap(k, step, kind).wait_send()
            here, copy = home(k, kind)

            @pl.when(jnp.logical_not(here))
            def _():
                copy.wait_send()

    return len(order), start, add, finish


def collect_scratch(plan, values):
    group, each, kinds = plan.group, plan.ns // plan.group, len(values)
    return (
        [pltpu.VMEM((group - 1, each) + part.shape[1:], BF16) for part in values]
        + [pltpu.VMEM((each,) + part.shape[1:], BF16) for part in values]
        + [
            DMA((each, kinds)),
            DMA((group - 1, each, kinds)),
            DMA((group - 1, each, kinds)),
            DMA((each, kinds)),
            DMA((EXP_DEV, 2)),
        ]
    )


def collect_kernel(plan, *refs):
    kinds = 2 * plan.nx
    ins, outs = refs[:kinds], refs[kinds : kinds + 2]
    parts, stage = refs[kinds + 2 : 2 * kinds + 2], refs[2 * kinds + 2 : 3 * kinds + 2]
    greet_plane(plan)
    count, start, add, finish = expert_collect(
        plan, ins, outs, parts, stage, *refs[3 * kinds + 2 :]
    )
    start()
    for place in range(count):
        add(place)
    finish()


def collect_call(plan, collective_id, terms):
    ns = plan.ns
    hbm = pl.BlockSpec(memory_space=pltpu.HBM)
    values = [part.reshape(ns, part.shape[0] // ns, D) for layer in terms for part in layer]
    return pl.pallas_call(
        functools.partial(collect_kernel, plan),
        out_shape=[jax.ShapeDtypeStruct((EXP_DEV,) + part.shape[1:], BF16) for part in values[:2]],
        in_specs=[hbm] * len(values),
        out_specs=[hbm, hbm],
        scratch_shapes=collect_scratch(plan, values),
        compiler_params=pltpu.CompilerParams(
            collective_id=collective_id, has_side_effects=True, vmem_limit_bytes=VMEM_LIMIT
        ),
    )(*values)


ADDS = 5
OWN_UP = 4


def reduce_kernel(plan, *refs):
    grads, wide_ins, outs, wide_outs = refs[0:2], refs[2:6], refs[6:10], refs[10:12]
    scratch = refs[12:]
    (mine, given, x_one, y_one, y_two, x_two, chain) = scratch[:7]
    (up, x_up, y_up, y_up_two, x_up_two) = scratch[7:12]
    (
        load_sem,
        core_send,
        core_recv,
        x_one_send,
        x_one_recv,
        y_one_send,
        y_one_recv,
        x_two_send,
        x_two_recv,
        y_two_send,
        y_two_recv,
        chain_send,
        chain_recv,
        up_send,
        up_recv,
        plane_send,
        plane_recv,
    ) = scratch[12:29]
    parts, stage = scratch[29:33], scratch[33:37]
    x, z, s = me()
    nz = plan.nz
    row, side = s // 2, s % 2
    core = (x, z, s + 1 - 2 * side)
    across_x = (1 - x, z, s)
    across_y = (x, z, (s + 2) % 4)
    third = grads[0].shape[2] // 3
    greet_plane(plan, along=True)
    count, start, add, finish = expert_collect(
        plan, wide_ins, wide_outs, parts, stage, *scratch[37:]
    )
    both = range(2)
    most = pl.ds(0, 2 * third)
    low, high = pl.ds(0, third), pl.ds(third, third)
    rest = pl.ds(2 * third, third)
    rest_low = pl.ds(2 * third, third // 2)
    rest_high = pl.ds(2 * third + third // 2, third // 2)

    def load(layer, block, to_row):
        return pltpu.make_async_copy(
            grads[layer].at[block, to_row * 2 + side],
            mine.at[layer, block, to_row],
            load_sem.at[layer, block, to_row],
        )

    def give(layer, block, to_row):
        return remote(
            grads[layer].at[block, to_row * 2 + 1 - side],
            given.at[layer, block, to_row],
            core_send.at[layer, block, to_row],
            core_recv.at[layer, block, to_row],
            core,
        )

    def send_x_one(block, to_row):
        return remote(
            mine.at[1 - x, block, to_row, low],
            x_one.at[block, to_row],
            x_one_send.at[block, to_row],
            x_one_recv.at[block, to_row],
            across_x,
        )

    def send_y_one(layer, block):
        return remote(
            mine.at[layer, block, 1 - row, high],
            y_one.at[layer, block],
            y_one_send.at[layer, block],
            y_one_recv.at[layer, block],
            across_y,
        )

    def send_y_two(block):
        return remote(
            mine.at[x, block, 1 - row, low],
            y_two.at[block],
            y_two_send.at[block],
            y_two_recv.at[block],
            across_y,
        )

    def send_x_two(block):
        return remote(
            mine.at[1 - x, block, row, high],
            x_two.at[block],
            x_two_send.at[block],
            x_two_recv.at[block],
            across_x,
        )

    def onward(block):
        rightward = (block > z).astype(jnp.int32)
        to = z - 1 + 2 * rightward
        return to, jnp.where((rightward == 1) & (block == to), nz, block)

    def send_chain(block):
        to, into = onward(block)
        return remote(
            mine.at[x, block, row, most],
            chain.at[into],
            chain_send.at[block],
            chain_recv.at[into],
            (x, to, s),
        )

    def send_up(block, layer, to_row):
        to, into = onward(block)
        return remote(
            mine.at[layer, block, to_row, rest],
            up.at[into, layer, to_row],
            up_send.at[block, layer, to_row],
            up_recv.at[into, layer, to_row],
            (x, to, s),
        )

    def plane_copy(step, place):
        if step == 0:
            src, dst, to = mine.at[1 - x, z, place, rest_low], x_up.at[place], across_x
        elif step == 1:
            src, dst, to = mine.at[place, z, 1 - row, rest_high], y_up.at[place], across_y
        elif step == 2:
            src, dst, to = mine.at[x, z, 1 - row, rest_low], y_up_two.at[0], across_y
        else:
            src, dst, to = mine.at[1 - x, z, row, rest_high], x_up_two.at[0], across_x
        return remote(src, dst, plane_send.at[step, place], plane_recv.at[step, place], to)

    def gain(at, other):
        mine[at] = (mine[at].astype(F32) + other.astype(F32)).astype(BF16)

    def begin(index):
        block = nearest(z, nz - 1 - index, nz)
        for layer in both:
            for to_row in both:
                load(layer, block, to_row).start()
                give(layer, block, to_row).start()

    def is_origin(block):
        return ((block < z) & (z == nz - 1)) | ((block > z) & (z == 0))

    def stage_core(index):
        block = nearest(z, nz - 1 - index, nz)
        for layer in both:
            for to_row in both:
                load(layer, block, to_row).wait()
                give(layer, block, to_row).wait_recv()
                gain((layer, block, to_row), given[layer, block, to_row])
        for to_row in both:
            send_x_one(block, to_row).start()
        for layer in both:
            send_y_one(layer, block).start()

        @pl.when(is_origin(block))
        def _():
            for layer in both:
                for to_row in both:
                    send_up(block, layer, to_row).start()

    def relay_up(index):
        block = nearest(z, nz - 1 - index, nz)

        @pl.when((z > 0) & (z < nz - 1))
        def _():
            for layer in both:
                for to_row in both:
                    landed(up.at[block, layer, to_row], up_recv.at[block, layer, to_row])
                    gain((layer, block, to_row, rest), up[block, layer, to_row])
                    send_up(block, layer, to_row).start()

    def own_up():
        for layer in both:
            for to_row in both:

                @pl.when(z + 1 < nz)
                def _():
                    landed(up.at[z, layer, to_row], up_recv.at[z, layer, to_row])
                    gain((layer, z, to_row, rest), up[z, layer, to_row])

                @pl.when(z > 0)
                def _():
                    landed(up.at[nz, layer, to_row], up_recv.at[nz, layer, to_row])
                    gain((layer, z, to_row, rest), up[nz, layer, to_row])

        for place in both:
            plane_copy(0, place).start()
            plane_copy(1, place).start()

    def up_first():
        for place in both:
            plane_copy(0, place).wait_recv()
            gain((x, z, place, rest_low), x_up[place])
            plane_copy(1, place).wait_recv()
            gain((place, z, row, rest_high), y_up[place])
        plane_copy(2, 0).start()
        plane_copy(3, 0).start()

    def up_second():
        plane_copy(2, 0).wait_recv()
        gain((x, z, row, rest_low), y_up_two[0])
        plane_copy(3, 0).wait_recv()
        gain((x, z, row, rest_high), x_up_two[0])

    def stage_first(index):
        block = nearest(z, nz - 1 - index, nz)
        for to_row in both:
            send_x_one(block, to_row).wait_recv()
            gain((x, block, to_row, low), x_one[block, to_row])
        send_y_two(block).start()
        for layer in both:
            send_y_one(layer, block).wait_recv()
            gain((layer, block, row, high), y_one[layer, block])
        send_x_two(block).start()

    def stage_second(index):
        block = nearest(z, nz - 1 - index, nz)
        send_y_two(block).wait_recv()
        gain((x, block, row, low), y_two[block])
        send_x_two(block).wait_recv()
        gain((x, block, row, high), x_two[block])

        @pl.when(is_origin(block))
        def _():
            send_chain(block).start()

    begin(0)
    begin(1)
    adds = 0
    for index in range(nz + 3):
        if index < nz:
            stage_core(index)
        if index + 2 < nz:
            begin(index + 2)
        if index == 0:
            start()
        if 1 <= index < nz + 1:
            stage_first(index - 1)
        if 1 <= index < nz:
            relay_up(index - 1)
        if 2 <= index < nz + 2:
            stage_second(index - 2)
        if index == OWN_UP:
            own_up()
        if index == OWN_UP + 1:
            up_first()
        while adds < count and index >= ADDS:
            add(adds)
            adds += 1
    up_second()

    def relay(turn, _):
        lower = z < nz // 2
        first = jnp.where(lower, nz - 1 - z, z)
        early = turn < first
        ahead = jnp.where(early, first - turn, nz - 1 - turn)
        rightward = lower == early
        block = jnp.where(rightward, z + ahead, z - ahead)

        @pl.when((z > 0) & (z < nz - 1))
        def _():
            landed(chain.at[block], chain_recv.at[block])
            gain((x, block, row, most), chain[block])
            send_chain(block).start()

        return 0

    lax.fori_loop(0, nz - 1, relay, 0)
    columns = (slice(0, WQ), slice(WQ, PROJ), slice(PROJ, WIN), slice(WIN, WIN + D))
    for out, at in zip(outs, columns):
        out[...] = mine[x, z, row, :, at].astype(F32)
    for place, there in ((z, z + 1 < nz), (nz, z > 0)):

        @pl.when(there)
        def _():
            landed(chain.at[place], chain_recv.at[place])
            for out, at in zip(outs, columns):
                out[: 2 * third] += chain[place, :, at].astype(F32)

    def drain(block, _):
        for layer in both:
            for to_row in both:
                give(layer, block, to_row).wait_send()

                @pl.when(block != z)
                def _():
                    send_up(block, layer, to_row).wait_send()

            send_y_one(layer, block).wait_send()
        for to_row in both:
            send_x_one(block, to_row).wait_send()
        send_y_two(block).wait_send()
        send_x_two(block).wait_send()

        @pl.when(block != z)
        def _():
            send_chain(block).wait_send()

        return 0

    lax.fori_loop(0, nz, drain, 0)
    for step, place in ((0, 0), (0, 1), (1, 0), (1, 1), (2, 0), (3, 0)):
        plane_copy(step, place).wait_send()
    finish()


def reduce_call(plan, collective_id, attention, terms):
    nx, nz, ns = plan.nx, plan.nz, plan.ns
    hbm = pl.BlockSpec(memory_space=pltpu.HBM)
    vmem = pl.BlockSpec(memory_space=pltpu.VMEM)
    grads = [part.reshape(nz, ns, -1, part.shape[1]) for part in attention]
    values = [part.reshape(ns, part.shape[0] // ns, D) for layer in terms for part in layer]
    held = [(EXP_DEV,) + part.shape[1:] for part in values[:2]]
    rows, width = grads[0].shape[2:]
    third = rows // 3
    return pl.pallas_call(
        functools.partial(reduce_kernel, plan),
        out_shape=[jax.ShapeDtypeStruct((rows, part), F32) for part in (WQ, 2 * WK, PAD, D)]
        + [jax.ShapeDtypeStruct(shape, BF16) for shape in held],
        in_specs=[hbm] * 6,
        out_specs=[vmem] * 4 + [hbm] * 2,
        scratch_shapes=[
            pltpu.VMEM((nx, nz, 2, rows, width), BF16),
            pltpu.VMEM((nx, nz, 2, rows, width), BF16),
            pltpu.VMEM((nz, 2, third, width), BF16),
            pltpu.VMEM((nx, nz, third, width), BF16),
            pltpu.VMEM((nz, third, width), BF16),
            pltpu.VMEM((nz, third, width), BF16),
            pltpu.VMEM((nz + 1, 2 * third, width), BF16),
            pltpu.VMEM((nz + 1, nx, 2, third, width), BF16),
            pltpu.VMEM((2, third // 2, width), BF16),
            pltpu.VMEM((2, third // 2, width), BF16),
            pltpu.VMEM((1, third // 2, width), BF16),
            pltpu.VMEM((1, third // 2, width), BF16),
            DMA((nx, nz, 2)),
            DMA((nx, nz, 2)),
            DMA((nx, nz, 2)),
            DMA((nz, 2)),
            DMA((nz, 2)),
            DMA((nx, nz)),
            DMA((nx, nz)),
            DMA((nz,)),
            DMA((nz,)),
            DMA((nz,)),
            DMA((nz,)),
            DMA((nz,)),
            DMA((nz + 1,)),
            DMA((nz, nx, 2)),
            DMA((nz + 1, nx, 2)),
            DMA((4, 2)),
            DMA((4, 2)),
        ]
        + collect_scratch(plan, values),
        compiler_params=pltpu.CompilerParams(
            collective_id=collective_id, has_side_effects=True, vmem_limit_bytes=VMEM_LIMIT
        ),
    )(*grads, *values)


def greet_shards(plan):
    x, z, s = me()
    barrier = pltpu.get_barrier_semaphore()
    for step in range(1, plan.ns):
        pl.semaphore_signal(
            barrier, inc=1, device_id=(x, z, (s + step) % plan.ns), device_id_type=MESH
        )
    pl.semaphore_wait(barrier, plan.ns - 1)


def turned(value, cosine, sine):
    return value * cosine + pltpu.roll(value, HD // 2, 1) * sine


def weights_of(queries, keys, allowed):
    raw = lax.dot_general(queries, keys, NARROW, preferred_element_type=F32)
    raw = jnp.where(allowed, raw * SCALE, -1e30)
    raw = jnp.exp(raw - jnp.max(raw, axis=1, keepdims=True))
    return raw / jnp.sum(raw, axis=1, keepdims=True)


def attend_kernel(plan, layer, *refs):
    (start, gains, cosine, sine, mask, weights) = refs[:6]
    (middle, normed, low, queries, kv, mixed) = refs[6:12]
    (win_v, wout_v, load_sem, send, recv) = refs[12:]
    x, z, s = me()
    tokens, rows, micro, ns = plan.tokens, plan.rows, plan.micro, plan.ns
    length = ns * tokens
    load_in = pltpu.make_async_copy(weights.at[layer, :, pl.ds(0, WIN)], win_v, load_sem.at[0])
    load_out = pltpu.make_async_copy(weights.at[layer, :, pl.ds(WIN, D)], wout_v, load_sem.at[1])
    load_in.start()
    load_out.start()
    greet_shards(plan)

    hidden = start[...].astype(F32)
    inverse = lax.rsqrt(jnp.mean(hidden * hidden, axis=1, keepdims=True) + epsilon)
    low[...] = (hidden * inverse * gains[0:1, :]).astype(BF16)
    load_in.wait()
    own = jnp.dot(low[...], win_v[:, WQ : WQ + 2 * WK], preferred_element_type=F32)
    for head in range(KV_HEADS):
        at = slice(head * HD, (head + 1) * HD)
        key = turned(own[:, at], cosine[...], sine[...]).astype(BF16)
        value = own[:, WK + head * HD : WK + (head + 1) * HD].astype(BF16)
        for m in range(micro):
            block = slice(m * tokens, (m + 1) * tokens)
            kv[s, m, :, at] = key[block]
            kv[s, m, :, WK + head * HD : WK + (head + 1) * HD] = value[block]

    def share(step, m):
        return remote(
            kv.at[s, m],
            kv.at[s, m],
            send.at[step - 1, m],
            recv.at[s, m],
            (x, z, (s + step) % ns),
        )

    for m in range(micro):
        for step in range(1, ns):
            share(step, m).start()

    def project(step, _):
        at = pl.multiple_of(step * 4 * HD, 4 * HD)
        part = jnp.dot(low[...], win_v[:, pl.ds(at, 4 * HD)], preferred_element_type=F32)
        for head in range(4):
            here = part[:, head * HD : (head + 1) * HD]
            queries[:, pl.ds(at + head * HD, HD)] = turned(here, cosine[...], sine[...]).astype(
                BF16
            )
        return 0

    lax.fori_loop(0, HEADS // 4, project, 0)

    def group(turn, _):
        m, pair = turn // KV_HEADS, turn % KV_HEADS

        @pl.when(pair == 0)
        def _():
            for step in range(1, ns):
                landed(kv.at[(s + step) % ns, m], recv.at[(s + step) % ns, m])

        span = pl.ds(pl.multiple_of(m * tokens, tokens), tokens)
        keys = kv[:, m, :, pl.ds(pl.multiple_of(pair * HD, HD), HD)].reshape(length, HD)
        values = kv[:, m, :, pl.ds(pl.multiple_of(WK + pair * HD, HD), HD)].reshape(length, HD)
        allowed = mask[m] > 0
        for i in range(GROUP):
            at = pl.ds(pl.multiple_of((pair * GROUP + i) * HD, HD), HD)
            probs = weights_of(queries[span, at], keys, allowed).astype(BF16)
            mixed[span, at] = jnp.dot(probs, values, preferred_element_type=F32).astype(BF16)
        return 0

    lax.fori_loop(0, micro * KV_HEADS, group, 0)
    load_out.wait()

    def back(step, _):
        at = pl.ds(pl.multiple_of(step * 512, 512), 512)
        middle[:, at] = start[:, at].astype(F32) + jnp.dot(
            mixed[...], wout_v[:, at], preferred_element_type=F32
        )
        return 0

    lax.fori_loop(0, D // 512, back, 0)
    after = middle[...]
    inverse = lax.rsqrt(jnp.mean(after * after, axis=1, keepdims=True) + epsilon)
    normed[...] = (after * inverse * gains[1:2, :]).astype(BF16)
    for m in range(micro):
        for step in range(1, ns):
            share(step, m).wait_send()


def attend_call(plan, layer, collective_id, start, gains, tables, weights):
    rows, ns, micro = plan.rows, plan.ns, plan.micro
    vmem = pl.BlockSpec(memory_space=pltpu.VMEM)
    hbm = pl.BlockSpec(memory_space=pltpu.HBM)
    shape = jax.ShapeDtypeStruct
    return pl.pallas_call(
        functools.partial(attend_kernel, plan, layer),
        out_shape=[
            shape((rows, D), F32),
            shape((rows, D), BF16),
            shape((rows, D), BF16),
            shape((rows, WQ), BF16),
            shape((ns, micro, plan.tokens, 2 * WK), BF16),
            shape((rows, WQ), BF16),
        ],
        in_specs=[vmem] * 5 + [hbm],
        out_specs=[vmem] * 6,
        scratch_shapes=[
            pltpu.VMEM((D, WIN), BF16),
            pltpu.VMEM((WQ, D), BF16),
            DMA((2,)),
            DMA((ns - 1, micro)),
            DMA((ns, micro)),
        ],
        compiler_params=pltpu.CompilerParams(
            collective_id=collective_id, has_side_effects=True, vmem_limit_bytes=VMEM_LIMIT
        ),
    )(start, gains, *tables, weights)


def return_kernel(plan, layer, *refs):
    (grad_out, grad_moe, middle, start, low, queries, kv, mixed) = refs[:8]
    (gains, cosine, sine, mask, weights) = refs[8:13]
    (result, terms) = refs[13:15]
    (win_v, wout_v, branch, grad_mixed, both, part, got, in_v, out_v, grad_in) = refs[15:25]
    (load_sem, save_in, save_out, send, recv) = refs[25:]
    x, z, s = me()
    tokens, rows, micro, ns = plan.tokens, plan.rows, plan.micro, plan.ns
    length = ns * tokens
    load_in = pltpu.make_async_copy(weights.at[layer, :, pl.ds(0, WIN)], win_v, load_sem.at[0])
    load_out = pltpu.make_async_copy(weights.at[layer, :, pl.ds(WIN, D)], wout_v, load_sem.at[1])
    load_out.start()
    load_in.start()
    greet_shards(plan)

    after = middle[...]
    inverse = lax.rsqrt(jnp.mean(after * after, axis=1, keepdims=True) + epsilon)
    scaled = grad_moe[...] * gains[1:2, :]
    inner = jnp.mean(scaled * after, axis=1, keepdims=True)
    total = grad_out[...].astype(F32) + inverse * scaled - after * (
        inverse * inverse * inverse * inner
    )
    grad_in[...] = total
    branch[...] = total.astype(BF16)
    gain_two = jnp.sum(grad_moe[...] * after * inverse, axis=0, keepdims=True)
    load_out.wait()

    def mix(step, _):
        at = pl.ds(pl.multiple_of(step * 512, 512), 512)
        grad_mixed[:, at] = lax.dot_general(
            branch[...], wout_v[at, :], NARROW, preferred_element_type=F32
        ).astype(BF16)
        return 0

    lax.fori_loop(0, WQ // 512, mix, 0)

    def share(step, m):
        to = (s + step) % ns
        return remote(
            part.at[to, m],
            got.at[s, m],
            send.at[step - 1, m],
            recv.at[s, m],
            (x, z, to),
        )

    def group(turn, _):
        m, pair = turn // KV_HEADS, turn % KV_HEADS
        span = pl.ds(pl.multiple_of(m * tokens, tokens), tokens)
        key_at = pl.ds(pl.multiple_of(pair * HD, HD), HD)
        value_at = pl.ds(pl.multiple_of(WK + pair * HD, HD), HD)
        keys = kv[:, m, :, key_at].reshape(length, HD)
        values = kv[:, m, :, value_at].reshape(length, HD)
        allowed = mask[m] > 0
        grad_keys = jnp.zeros((length, HD), F32)
        grad_values = jnp.zeros((length, HD), F32)
        for i in range(GROUP):
            at = pl.ds(pl.multiple_of((pair * GROUP + i) * HD, HD), HD)
            mine, given = queries[span, at], grad_mixed[span, at]
            probs = weights_of(mine, keys, allowed)
            grad_probs = lax.dot_general(given, values, NARROW, preferred_element_type=F32)
            inside = jnp.sum(grad_probs * probs, axis=1, keepdims=True)
            raw = (probs * (grad_probs - inside) * SCALE).astype(BF16)
            grad_query = jnp.dot(raw, keys, preferred_element_type=F32)
            both[span, at] = turned(grad_query, cosine[span], -sine[span]).astype(BF16)
            grad_keys += lax.dot_general(raw, mine, ACROSS, preferred_element_type=F32)
            grad_values += lax.dot_general(
                probs.astype(BF16), given, ACROSS, preferred_element_type=F32
            )
        part[:, m, :, key_at] = grad_keys.astype(BF16).reshape(ns, tokens, HD)
        part[:, m, :, value_at] = grad_values.astype(BF16).reshape(ns, tokens, HD)

        @pl.when(pair == KV_HEADS - 1)
        def _():
            for step in range(1, ns):
                share(step, m).start()

        return 0

    lax.fori_loop(0, micro * KV_HEADS, group, 0)

    def out_copy(step):
        at = pl.ds(step * 256, 256)
        return pltpu.make_async_copy(out_v.at[at], terms.at[at, pl.ds(WIN, D)], save_out.at[step])

    def in_copy(step):
        at = pl.ds(step * 256, 256)
        return pltpu.make_async_copy(in_v.at[at], terms.at[at, pl.ds(0, WIN)], save_in.at[step])

    def out_tile(step, _):
        at = pl.ds(pl.multiple_of(step * 256, 256), 256)
        out_v[at, :] = lax.dot_general(
            mixed[:, at], branch[...], ACROSS, preferred_element_type=F32
        ).astype(BF16)
        out_copy(step).start()
        return 0

    lax.fori_loop(0, WQ // 256, out_tile, 0)
    load_in.wait()
    for m in range(micro):
        for step in range(1, ns):
            landed(got.at[(s + step) % ns, m], recv.at[(s + step) % ns, m])
        span = slice(m * tokens, (m + 1) * tokens)
        total = part[s, m].astype(F32)
        for step in range(1, ns):
            total += got[(s + step) % ns, m].astype(F32)
        for head in range(KV_HEADS):
            at = slice(head * HD, (head + 1) * HD)
            both[span, WQ + head * HD : WQ + (head + 1) * HD] = turned(
                total[:, at], cosine[span], -sine[span]
            ).astype(BF16)
        both[span, WQ + WK :] = total[:, WK:].astype(BF16)

    def in_tile(step, _):
        at = pl.ds(pl.multiple_of(step * 256, 256), 256)
        in_v[at, : WQ + 2 * WK] = lax.dot_general(
            low[:, at], both[...], ACROSS, preferred_element_type=F32
        ).astype(BF16)
        return 0

    lax.fori_loop(0, D // 256, in_tile, 0)
    grad_normed = []
    for step in range(D // 512):
        at = slice(step * 512, (step + 1) * 512)
        grad_normed.append(
            lax.dot_general(
                both[...], win_v[at, : WQ + 2 * WK], NARROW, preferred_element_type=F32
            )
        )
    grad_normed = jnp.concatenate(grad_normed, axis=1)
    hidden = start[...].astype(F32)
    inverse = lax.rsqrt(jnp.mean(hidden * hidden, axis=1, keepdims=True) + epsilon)
    scaled = grad_normed * gains[0:1, :]
    inner = jnp.mean(scaled * hidden, axis=1, keepdims=True)
    grad_in[...] += inverse * scaled - hidden * (inverse * inverse * inverse * inner)
    result[...] = grad_in[...].astype(result.dtype)
    gain_one = jnp.sum(grad_normed * hidden * inverse, axis=0, keepdims=True)
    place = lax.broadcasted_iota(jnp.int32, (128, D), 0)
    rows_of = jnp.where(place == 0, gain_one, jnp.where(place == 1, gain_two, 0.0))
    in_v[:, WQ + 2 * WK :] = rows_of.T.astype(BF16)
    for step in range(D // 256):
        in_copy(step).start()
    for step in range(D // 256):
        in_copy(step).wait()
        out_copy(step).wait()
    for m in range(micro):
        for step in range(1, ns):
            share(step, m).wait_send()


def return_call(plan, layer, collective_id, grads, saved, gains, tables, weights):
    rows, ns, micro, tokens = plan.rows, plan.ns, plan.micro, plan.tokens
    vmem = pl.BlockSpec(memory_space=pltpu.VMEM)
    hbm = pl.BlockSpec(memory_space=pltpu.HBM)
    shape = jax.ShapeDtypeStruct
    exchange = (ns, micro, tokens, 2 * WK)
    return pl.pallas_call(
        functools.partial(return_kernel, plan, layer),
        out_shape=[
            shape((rows, D), BF16 if layer > 0 else F32),
            shape((D, WIN + D), BF16),
        ],
        in_specs=[vmem] * 12 + [hbm],
        out_specs=[vmem, hbm],
        scratch_shapes=[
            pltpu.VMEM((D, WIN), BF16),
            pltpu.VMEM((WQ, D), BF16),
            pltpu.VMEM((rows, D), BF16),
            pltpu.VMEM((rows, WQ), BF16),
            pltpu.VMEM((rows, WQ + 2 * WK), BF16),
            pltpu.VMEM(exchange, BF16),
            pltpu.VMEM(exchange, BF16),
            pltpu.VMEM((D, WIN), BF16),
            pltpu.VMEM((WQ, D), BF16),
            pltpu.VMEM((rows, D), F32),
            DMA((2,)),
            DMA((D // 256,)),
            DMA((WQ // 256,)),
            DMA((ns - 1, micro)),
            DMA((ns, micro)),
        ],
        compiler_params=pltpu.CompilerParams(
            collective_id=collective_id, has_side_effects=True, vmem_limit_bytes=VMEM_LIMIT
        ),
    )(*grads, *saved, gains, *tables, weights)


def slot_table(plan, routes, gates):
    experts, nz = plan.experts, plan.nz
    named = routes[..., None] == jnp.arange(experts, dtype=jnp.int32)
    gate = jnp.sum(jnp.where(named, gates[..., None], 0.0), axis=2)
    named = jnp.any(named, axis=2)
    earlier = jnp.tril(jnp.ones((plan.tokens, plan.tokens), BF16), -1)
    rank = jnp.einsum("ut,mte->mue", earlier, named.astype(BF16), preferred_element_type=F32)
    table = jnp.stack([jnp.where(named, rank, -1.0), gate])
    table = table.reshape(2, plan.micro, plan.tokens, nz, EXP_DEV).transpose(3, 0, 1, 4, 2)
    return table.reshape(nz, -1, plan.tokens)


def slot_places(plan, table):
    nz = plan.nz
    table = table.reshape(nz, 2, plan.micro, EXP_DEV, plan.tokens)
    rank, gate = table[:, 0], table[:, 1]
    first = jnp.arange(plan.micro, dtype=F32)[:, None, None] * plan.capacity
    place = jnp.where(rank >= 0, rank + first, -1.0).transpose(0, 2, 1, 3)
    hit = place[:, :, None] == jnp.arange(plan.slots, dtype=F32)[:, None, None]
    shape = (nz, EXP_DEV * plan.slots, plan.rows)
    one = hit.astype(BF16).reshape(shape)
    weighted = jnp.where(hit, gate.transpose(0, 2, 1, 3)[:, :, None], 0.0)
    weighted = weighted.astype(BF16).reshape(shape)
    return one, weighted


def shards(
    inputs,
    segments,
    routes,
    gate_weights,
    query_weight,
    key_value_weight,
    output_weight,
    norm_gains,
    expert_gate_up,
    expert_down,
    cotangent,
):
    section = lax.axis_index("section")
    shard_index = lax.axis_index("shard")
    tokens = inputs.shape[1]
    plan = Plan((lax.axis_size("section"), lax.axis_size("expert"), lax.axis_size("shard")), tokens)
    micro, rows, layers = plan.micro, plan.rows, plan.nx
    length = tokens * plan.ns

    def mine(value):
        return lax.dynamic_slice_in_dim(value, section * micro, micro, 0)

    paired = plan.nx == 2 and plan.ns == 4 and query_weight.shape[1] % 96 == 0
    gain_columns = jnp.pad(norm_gains[0].T, ((0, 0), (0, PAD - 2)))
    attention_weights = jnp.concatenate(
        [query_weight[0], key_value_weight[0], gain_columns, output_weight[0]], axis=1
    ).astype(BF16)
    table = slot_table(plan, mine(routes), mine(gate_weights))
    if paired:
        weights, table, wide_in, wide_down = gather_call(
            plan, 1, attention_weights, table, (expert_gate_up[0], expert_down[0])
        )
    else:
        weights = lax.all_gather(
            attention_weights, ("section", "expert", "shard"), axis=0, tiled=True
        )
        table = lax.all_to_all(table, "expert", split_axis=0, concat_axis=0, tiled=True)
        wide_in, wide_down = spread_call(
            plan, 1, expert_gate_up[0].astype(BF16), expert_down[0].astype(BF16)
        )
    weights = weights.reshape(layers, D, WIN + D)
    gains = weights[:, :, PROJ : PROJ + 2].transpose(0, 2, 1).astype(F32)
    wide_in = wide_in.reshape(layers, D, 2 * FF)
    wide_down = wide_down.reshape(layers, FF, D)
    one, weighted = slot_places(plan, table)

    offset = shard_index * tokens
    position = (offset + jnp.arange(tokens, dtype=jnp.int32)).astype(F32)
    frequency = rope_base ** (-jnp.arange(HD // 2, dtype=F32) / (HD // 2))
    angles = position[:, None] * frequency[None, :]
    cosine, sine = jnp.cos(angles), jnp.sin(angles)
    cosine = jnp.tile(jnp.concatenate([cosine, cosine], axis=1), (micro, 1))
    sine = jnp.tile(jnp.concatenate([-sine, sine], axis=1), (micro, 1))
    segment_all = mine(segments)[:, 0]
    segment_own = lax.dynamic_slice_in_dim(segment_all, offset, tokens, 1)
    query_place = offset + jnp.arange(tokens, dtype=jnp.int32)
    key_place = jnp.arange(length, dtype=jnp.int32)
    allowed = (segment_own[:, :, None] == segment_all[:, None, :]) & (
        query_place[:, None] >= key_place[None, :]
    )
    tables = (cosine, sine, allowed.astype(F32))

    hidden = mine(inputs).reshape(rows, D)
    grad = mine(cotangent).reshape(rows, D)
    kept, passed = [], []
    attention_terms = [None] * layers
    expert_terms = [None] * layers
    for layer in range(layers):
        start = hidden.astype(BF16)
        middle, normed, low, queries, kv, mixed = attend_call(
            plan, layer, 2 + layer, start, gains[layer], tables, weights
        )
        kept.append((middle, start, low, queries, kv, mixed))
        if layer == layers - 1 and both_fit(plan):
            hidden, grad_moe, expert_terms[layer] = moe_both_call(
                plan,
                layer,
                2 + layers + layer,
                normed,
                grad,
                one,
                weighted,
                wide_in,
                wide_down,
                middle,
            )
            passed.append(None)
        else:
            hidden, *saved = moe_call(
                plan,
                layer,
                F32 if layer == layers - 1 else BF16,
                2 + layers + layer,
                normed,
                one,
                weighted,
                wide_in,
                wide_down,
                middle,
            )
            passed.append(saved)
    output = hidden.reshape(micro, tokens, D)

    for layer in reversed(range(layers)):
        grad_out = grad.astype(BF16)
        if passed[layer] is not None:
            grad_moe, expert_terms[layer] = moe_back_call(
                plan,
                layer,
                2 + 2 * layers + layer,
                grad_out,
                weighted,
                one,
                wide_in,
                wide_down,
                passed[layer],
            )
        grad, attention_terms[layer] = return_call(
            plan,
            layer,
            2 + 3 * layers + layer,
            (grad_out, grad_moe),
            kept[layer],
            gains[layer],
            tables,
            weights,
        )
    input_grad = grad.reshape(micro, tokens, D)

    if paired:
        query_grad, key_value_grad, gain_grad, output_weight_grad, gate_up_grad, down_grad = (
            reduce_call(plan, 2 + 4 * layers, attention_terms, expert_terms)
        )
    else:
        gate_up_grad, down_grad = collect_call(plan, 2 + 4 * layers, expert_terms)
        term = lax.psum_scatter(
            jnp.concatenate(attention_terms),
            ("section", "expert", "shard"),
            scatter_dimension=0,
            tiled=True,
        )
        query_grad, key_value_grad, gain_grad, output_weight_grad = (
            term[:, :WQ],
            term[:, WQ:PROJ],
            term[:, PROJ:WIN],
            term[:, WIN:],
        )
    gain_grad = gain_grad[:, :2].T
    query_grad, key_value_grad, gain_grad, output_weight_grad, gate_up_grad, down_grad = (
        part.astype(F32)[None]
        for part in (
            query_grad,
            key_value_grad,
            gain_grad,
            output_weight_grad,
            gate_up_grad,
            down_grad,
        )
    )
    return (
        output,
        input_grad,
        query_grad,
        key_value_grad,
        output_weight_grad,
        gain_grad,
        gate_up_grad,
        down_grad,
    )


def solution(mesh):
    placed = (
        P(None, ("expert", "shard"), None),
        P(None, "expert", None),
        P(None, ("expert", "shard"), None),
        P(None, ("expert", "shard"), None),
        P("section", ("expert", "shard"), None),
        P("section", ("expert", "shard"), None),
        P("section", ("expert", "shard"), None),
        P("section", None, ("expert", "shard")),
        P("section", "expert", "shard", None),
        P("section", "expert", "shard", None),
        P(None, ("expert", "shard"), None),
    )
    return jax.shard_map(
        shards,
        mesh=mesh,
        in_specs=placed,
        out_specs=(
            P("section", ("expert", "shard"), None),
            P("section", ("expert", "shard"), None),
            P("section", ("expert", "shard"), None),
            P("section", ("expert", "shard"), None),
            P("section", ("expert", "shard"), None),
            P("section", None, ("expert", "shard")),
            P("section", "expert", "shard", None),
            P("section", "expert", "shard", None),
        ),
        check_vma=False,
    )
```

```python
import functools
import math
from types import SimpleNamespace

import jax
import jax.numpy as jnp
from jax import lax
from jax.experimental import pallas as pl
from jax.experimental.pallas import tpu as pltpu
from jax.sharding import PartitionSpec as P

D = 1536
HEADS = 12
KV_HEADS = 2
HD = 128
FF = 768
TOPK = 4
EXP_DEV = 4
MICRO = 4
GROUP = HEADS // KV_HEADS
PAD = 128
WQ = HEADS * HD
WK = KV_HEADS * HD
PROJ = WQ + 2 * WK
WIN = PROJ + PAD
SCALE = HD ** (-0.5)

epsilon = 1e-06
rope_base = 10000.0

MESH = pl.DeviceIdType.MESH
F32 = jnp.float32
BF16 = jnp.bfloat16
DMA = pltpu.SemaphoreType.DMA
VMEM_LIMIT = 62 * 2**20


class Plan:
    def __init__(self, mesh_shape, tokens):
        self.nx, self.nz, self.ns = mesh_shape
        self.tokens = tokens
        self.micro = MICRO // self.nx
        self.rows = self.micro * tokens
        self.ranks = self.nx * self.ns
        self.group = self.ranks // EXP_DEV
        self.halves = self.group // 2
        self.sources = self.ranks // self.halves
        self.experts = EXP_DEV * self.nz
        self.capacity = 5 * tokens * TOPK // (4 * self.experts)
        self.slots = -(-self.micro * self.capacity // 16) * 16
        self.blocks = self.nz // 2
        self.many = self.sources * self.slots


def me():
    return lax.axis_index("section"), lax.axis_index("expert"), lax.axis_index("shard")


def remote(src, dst, send, recv, device):
    return pltpu.make_async_remote_copy(
        src_ref=src,
        dst_ref=dst,
        send_sem=send,
        recv_sem=recv,
        device_id=device,
        device_id_type=MESH,
    )


def landed(ref, sem):
    pltpu.make_async_copy(ref, ref, sem).wait()


def greet_plane(plan, along=False):
    x, z, s = me()
    barrier = pltpu.get_barrier_semaphore()
    mine = x * plan.ns + s
    for step in range(1, plan.ranks):
        other = (mine + step) % plan.ranks
        pl.semaphore_signal(
            barrier, inc=1, device_id=(other // plan.ns, z, other % plan.ns), device_id_type=MESH
        )
    total = plan.ranks - 1
    if along:
        for step in range(1, plan.nz):
            pl.semaphore_signal(
                barrier, inc=1, device_id=(x, (z + step) % plan.nz, s), device_id_type=MESH
            )
        total += plan.nz - 1
    pl.semaphore_wait(barrier, total)


def nearest(place, index, count):
    left = place
    right = count - 1 - place
    short = jnp.minimum(left, right)
    odd = index % 2
    near = place + (1 - 2 * odd) * ((index + 1) // 2)
    far = jnp.where(left < right, index, count - 1 - index)
    return jnp.where(index <= 2 * short, near, far)


NARROW = (((1,), (1,)), ((), ()))
ACROSS = (((0,), (0,)), ((), ()))
TILE = 256
CUTS = 3
CUT = D // CUTS


def moe_stages(plan, backward, r):
    x, z, s = me()
    nz, ns, slots = plan.nz, plan.ns, plan.slots
    rank = x * ns + s
    own_expert = rank // plan.group
    own_turn = (rank % plan.group) // plan.halves
    own_half = rank % plan.halves
    part = ns // plan.halves
    own_source = x * part + s // plan.halves
    chunk = plan.tokens
    own_copy = pltpu.make_async_copy(r.rows_in, r.line.at[z], r.own_sem.at[0])

    def along(block, piece, step, own):
        at = pl.ds(piece * chunk, chunk)
        src = r.rows_in.at[at] if own else r.line.at[block, at]
        sem = r.line_right if step > 0 else r.line_left
        return remote(
            src,
            r.line.at[block, at],
            sem.at[block, piece],
            r.line_recv.at[block, piece],
            (x, z + step, s),
        )

    def owner(block, expert):
        rank_to = expert * plan.group + (block % 2) * plan.halves + s % plan.halves
        return rank_to // ns, rank_to % ns

    def dispatch_copy(block, expert):
        to_x, to_s = owner(block, expert)
        here = (to_x == x) & (to_s == s)
        return here, remote(
            r.sbuf.at[block, expert],
            r.xbuf.at[block // 2, own_source],
            r.to_send.at[block, expert],
            r.to_recv.at[block // 2, own_source],
            (to_x, z, to_s),
        )

    def return_copy(block, cut, source):
        to_x = source // part
        to_s = (source % part) * plan.halves + own_half
        here = (to_x == x) & (to_s == s)
        return here, remote(
            r.ybuf.at[block // 2, cut, source],
            r.rbuf.at[block, cut, own_expert],
            r.back_send.at[block // 2, cut, source],
            r.back_recv.at[block, cut, own_expert],
            (to_x, z, to_s),
        )

    def sum_copy(block, cut):
        rightward = (block > z).astype(jnp.int32)
        to = z - 1 + 2 * rightward
        into = jnp.where((rightward == 1) & (block == to), nz, block)
        return remote(
            r.pbuf.at[block, cut],
            r.qbuf.at[into, cut],
            r.sum_send.at[block, cut],
            r.sum_recv.at[into, cut],
            (x, to, s),
        )

    def begin():
        for piece in range(plan.micro):

            @pl.when(z + 1 < nz)
            def _():
                along(z, piece, 1, True).start()

            @pl.when(z > 0)
            def _():
                along(z, piece, -1, True).start()

        own_copy.start()

    def fetch(index):
        block = nearest(z, index, nz)
        if index == 0:
            own_copy.wait()
        for piece in range(plan.micro):

            @pl.when(block < z)
            def _():
                along(block, piece, 1, False).wait_recv()

                @pl.when(z + 1 < nz)
                def _():
                    along(block, piece, 1, False).start()

            @pl.when(block > z)
            def _():
                along(block, piece, -1, False).wait_recv()

                @pl.when(z > 0)
                def _():
                    along(block, piece, -1, False).start()

    def put(index):
        block = nearest(z, index, nz)

        def lay(step, _):
            at = pl.ds(pl.multiple_of(step * TILE, TILE), TILE)
            laid = jnp.dot(r.put[block], r.line[block, :, at], preferred_element_type=F32)
            r.sbuf[block, :, :, at] = laid.astype(BF16).reshape(EXP_DEV, slots, TILE)
            return 0

        lax.fori_loop(0, D // TILE, lay, 0)
        for expert in range(EXP_DEV):
            here, copy = dispatch_copy(block, expert)

            @pl.when(here)
            def _():
                pltpu.make_async_copy(
                    r.sbuf.at[block, expert],
                    r.xbuf.at[block // 2, own_source],
                    r.to_recv.at[block // 2, own_source],
                ).start()

            @pl.when(jnp.logical_not(here))
            def _():
                copy.start()

    def compute(block, now):
        pair = block // 2
        for source in range(plan.sources):
            landed(r.xbuf.at[pair, source], r.to_recv.at[pair, source])
        few = plan.sources // 2
        span = few * slots

        def middle(step, _):
            rows = pl.ds(pl.multiple_of(step * span, 16), span)
            taken = r.xbuf[pair, pl.ds(step * few, few)].reshape(span, D)
            if backward:
                grad_hidden = lax.dot_general(
                    taken, r.wdown_v[...], NARROW, preferred_element_type=F32
                )
                gate = r.gbuf[pair, rows, :FF].astype(F32)
                up = r.gbuf[pair, rows, FF:].astype(F32)
                sig = 1.0 / (1.0 + jnp.exp(-gate))
                gs = gate * sig
                grad_gate = grad_hidden * up * (sig + gs * (1.0 - sig))
                r.gbuf[pair, rows, :FF] = grad_gate.astype(BF16)
                r.gbuf[pair, rows, FF:] = (grad_hidden * gs).astype(BF16)
            else:
                gate = jnp.dot(taken, r.win_v[:, :FF], preferred_element_type=F32)
                up = jnp.dot(taken, r.win_v[:, FF:], preferred_element_type=F32)
                r.gbuf[pair, rows, :FF] = gate.astype(BF16)
                r.gbuf[pair, rows, FF:] = up.astype(BF16)
                r.zbuf[pair, rows] = (gate / (1.0 + jnp.exp(-gate)) * up).astype(BF16)
            return 0

        lax.fori_loop(0, 2, middle, 0)

        def last(cut, _):
            at = pl.ds(pl.multiple_of(cut * CUT, CUT), CUT)
            if backward:
                result = lax.dot_general(
                    r.gbuf[pair], r.win_v[at, :], NARROW, preferred_element_type=F32
                )
            else:
                result = jnp.dot(r.zbuf[pair], r.wdown_v[:, at], preferred_element_type=F32)
            r.ybuf[pair, cut] = result.astype(BF16).reshape(plan.sources, slots, CUT)
            if now:
                return_cut(block, cut)
            return 0

        lax.fori_loop(0, CUTS, last, 0)

    def return_cut(block, cut):
        pair = block // 2
        for source in range(plan.sources):
            here, copy = return_copy(block, cut, source)

            @pl.when(here)
            def _():
                pltpu.make_async_copy(
                    r.ybuf.at[pair, cut, source],
                    r.rbuf.at[block, cut, own_expert],
                    r.back_recv.at[block, cut, own_expert],
                ).start()

            @pl.when(jnp.logical_not(here))
            def _():
                copy.start()

    def own_turn_do(index, act):
        block = nearest(z, index, nz)

        @pl.when(block % 2 == own_turn)
        def _():
            act(block)

    def give_back(block):
        for cut in range(CUTS):
            return_cut(block, cut)

    def take(index):
        block = nearest(z, index, nz)
        origin = ((block < z) & (z == nz - 1)) | ((block > z) & (z == 0))
        for cut in range(CUTS):
            for expert in range(EXP_DEV):
                landed(r.rbuf.at[block, cut, expert], r.back_recv.at[block, cut, expert])
            got = lax.dot_general(
                r.take[block],
                r.rbuf[block, cut].reshape(EXP_DEV * slots, CUT),
                (((0,), (0,)), ((), ())),
                preferred_element_type=F32,
            )

            @pl.when(block == z)
            def _():
                at = pl.ds(cut * CUT, CUT)
                if backward:
                    r.out[:, at] = got
                else:
                    r.out[:, at] += got

            @pl.when(block != z)
            def _():
                r.pbuf[block, cut] = got.astype(BF16)

            @pl.when(origin)
            def _():
                sum_copy(block, cut).start()

    def relay(turn):
        lower = z < nz // 2
        first = jnp.where(lower, nz - 1 - z, z)
        early = turn < first
        ahead = jnp.where(early, first - turn, nz - 1 - turn)
        rightward = lower == early
        block = jnp.where(rightward, z + ahead, z - ahead)

        @pl.when((z > 0) & (z < nz - 1))
        def _():
            for cut in range(CUTS):
                landed(r.qbuf.at[block, cut], r.sum_recv.at[block, cut])
                r.pbuf[block, cut] = (
                    r.pbuf[block, cut].astype(F32) + r.qbuf[block, cut].astype(F32)
                ).astype(BF16)
                sum_copy(block, cut).start()

    def finish():
        for cut in range(CUTS):
            at = pl.ds(cut * CUT, CUT)

            @pl.when(z + 1 < nz)
            def _():
                landed(r.qbuf.at[z, cut], r.sum_recv.at[z, cut])
                r.out[:, at] += r.qbuf[z, cut].astype(F32)

            @pl.when(z > 0)
            def _():
                landed(r.qbuf.at[nz, cut], r.sum_recv.at[nz, cut])
                r.out[:, at] += r.qbuf[nz, cut].astype(F32)

    def free_put(block):
        for piece in range(plan.micro):

            @pl.when((block <= z) & (z + 1 < nz))
            def _():
                along(block, piece, 1, False).wait_send()

            @pl.when((block >= z) & (z > 0))
            def _():
                along(block, piece, -1, False).wait_send()

        for expert in range(EXP_DEV):
            here, copy = dispatch_copy(block, expert)

            @pl.when(jnp.logical_not(here))
            def _():
                copy.wait_send()

    def free_back(block):
        for cut in range(CUTS):
            for source in range(plan.sources):
                here, copy = return_copy(block, cut, source)

                @pl.when(jnp.logical_not(here))
                def _():
                    copy.wait_send()

    def free_sum(block):
        @pl.when(block != z)
        def _():
            for cut in range(CUTS):
                sum_copy(block, cut).wait_send()

    def free_all():
        def free(block, _):
            free_put(block)

            @pl.when(block % 2 == own_turn)
            def _():
                free_back(block)

            free_sum(block)
            return 0

        lax.fori_loop(0, nz, free, 0)

    return SimpleNamespace(
        begin=begin,
        fetch=fetch,
        put=put,
        expert=lambda index, now=True: own_turn_do(index, lambda block: compute(block, now)),
        give_back=lambda index: own_turn_do(index, give_back),
        take=take,
        relay=relay,
        finish=finish,
        free_put=lambda index: free_put(nearest(z, index, nz)),
        free_back=lambda index: own_turn_do(index, free_back),
        free_sum=lambda index: free_sum(nearest(z, index, nz)),
        free_all=free_all,
    )


def late_relays(nz):
    return (2, 1) if nz == 4 else range(1, nz - 1)


def first_part(plan, stages, loaded):
    last = plan.nz - 1
    stages.fetch(0)
    stages.put(0)
    loaded()
    for index in range(1, plan.nz):
        stages.fetch(index)
        stages.put(index)
        stages.expert(index - 1, 1 < index < last)


def second_part(plan, stages, steps=()):
    last = plan.nz - 1
    steps = iter(steps)

    def another():
        next(steps, lambda: None)()

    for index in range(1, plan.nz - 2):
        stages.take(index)
    stages.expert(last)
    another()
    stages.take(last)
    stages.give_back(last - 1)
    stages.give_back(0)
    another()
    stages.relay(0)
    stages.take(last - 1)
    another()
    stages.take(0)


def weight_tiles(plan, given, hidden, grad_both, grad_rows, in_term, down_term, tile_v, sem):
    counts = (D // TILE, FF // TILE)

    def copy(tile):
        if isinstance(tile, int) and tile >= counts[0]:
            to = down_term.at[pl.ds((tile - counts[0]) * TILE, TILE)]
        else:
            to = in_term.at[pl.ds(pl.multiple_of(tile * TILE, TILE), TILE)]
        return pltpu.make_async_copy(tile_v.at[tile % 2], to, sem.at[tile % 2])

    def summed(left, right):
        total = lax.dot_general(left(0), right(0), ACROSS, preferred_element_type=F32)
        for pair in range(1, plan.blocks):
            total += lax.dot_general(left(pair), right(pair), ACROSS, preferred_element_type=F32)
        return total.astype(BF16)

    def rows_of(ref, pair, at):
        return ref[pair, :, :, at].reshape(plan.many, -1)

    def in_tile(tile, _):
        @pl.when(tile >= 2)
        def _():
            copy(tile % 2).wait()

        at = pl.ds(pl.multiple_of(tile * TILE, TILE), TILE)
        tile_v[tile % 2] = summed(lambda p: rows_of(given, p, at), lambda p: grad_both[p])
        copy(tile).start()
        return 0

    def first():
        lax.fori_loop(0, counts[0], in_tile, 0)

    def second():
        for step in range(counts[1]):
            tile = counts[0] + step
            copy(tile % 2).wait()
            at = slice(step * TILE, (step + 1) * TILE)
            tile_v[tile % 2] = summed(
                lambda p: hidden[p, :, at], lambda p: grad_rows[p].reshape(plan.many, D)
            )
            copy(tile).start()

    def finish():
        for tile in range(sum(counts) - 2, sum(counts)):
            copy(tile).wait()

    return first, second, finish


PASS_BUFFERS = ("line", "xbuf", "rbuf", "qbuf")
PASS_SEMAPHORES = (
    "own_sem",
    "line_recv",
    "line_right",
    "line_left",
    "to_send",
    "to_recv",
    "back_send",
    "back_recv",
    "sum_send",
    "sum_recv",
)
SHARED_BUFFERS = ("sbuf", "ybuf", "pbuf", "win_v", "wdown_v", "gbuf", "zbuf")


def pass_scratch(plan):
    nz, blocks, slots, sources, rows = plan.nz, plan.blocks, plan.slots, plan.sources, plan.rows
    return [
        pltpu.VMEM((nz, rows, D), BF16),
        pltpu.VMEM((blocks, sources, slots, D), BF16),
        pltpu.VMEM((nz, CUTS, EXP_DEV, slots, CUT), BF16),
        pltpu.VMEM((nz + 1, CUTS, rows, CUT), BF16),
        DMA((1,)),
        DMA((nz, plan.micro)),
        DMA((nz, plan.micro)),
        DMA((nz, plan.micro)),
        DMA((nz, EXP_DEV)),
        DMA((blocks, sources)),
        DMA((blocks, CUTS, sources)),
        DMA((nz, CUTS, EXP_DEV)),
        DMA((nz, CUTS)),
        DMA((nz + 1, CUTS)),
    ]


def shared_scratch(plan):
    nz, blocks, slots, many = plan.nz, plan.blocks, plan.slots, plan.many
    return [
        pltpu.VMEM((nz, EXP_DEV, slots, D), BF16),
        pltpu.VMEM((blocks, CUTS, plan.sources, slots, CUT), BF16),
        pltpu.VMEM((nz, CUTS, plan.rows, CUT), BF16),
        pltpu.VMEM((D, 2 * FF), BF16),
        pltpu.VMEM((FF, D), BF16),
        pltpu.VMEM((blocks, many, 2 * FF), BF16),
        pltpu.VMEM((blocks, many, FF), BF16),
    ]


PASS_NAMES = PASS_BUFFERS + PASS_SEMAPHORES


def named(names, refs):
    return dict(zip(names, refs, strict=True))


def run_copies(copies):
    for copy in copies:
        copy.start()

    def wait():
        for copy in copies:
            copy.wait()

    return wait


def moe_kernel(plan, layer, *refs):
    rows_in, put, take, w_in, w_down, base, result, sent, gate_up, hidden = refs[:10]
    count = len(PASS_NAMES)
    r = SimpleNamespace(
        rows_in=rows_in,
        put=put,
        take=take,
        **named(PASS_NAMES, refs[10 : 10 + count]),
        **named(SHARED_BUFFERS, refs[10 + count : -3]),
    )
    out, load_sem, save_sem = refs[-3:]
    r.out = out
    loaded = run_copies(
        [
            pltpu.make_async_copy(w_in.at[layer], r.win_v, load_sem.at[0]),
            pltpu.make_async_copy(w_down.at[layer], r.wdown_v, load_sem.at[1]),
            pltpu.make_async_copy(base, out, load_sem.at[2]),
        ]
    )
    greet_plane(plan, along=True)
    stages = moe_stages(plan, False, r)
    stages.begin()
    first_part(plan, stages, loaded)
    second_part(plan, stages)
    saved = run_copies(
        [
            pltpu.make_async_copy(r.xbuf, sent, save_sem.at[0]),
            pltpu.make_async_copy(r.gbuf, gate_up, save_sem.at[1]),
            pltpu.make_async_copy(r.zbuf, hidden, save_sem.at[2]),
        ]
    )
    for turn in late_relays(plan.nz):
        stages.relay(turn)
    stages.finish()
    result[...] = out[...].astype(result.dtype)
    stages.free_all()
    saved()


def moe_back_kernel(plan, layer, *refs):
    rows_in, put, take, w_in, w_down, sent, gate_up, hidden, out, in_term, down_term = refs[:11]
    count = len(PASS_NAMES)
    r = SimpleNamespace(
        rows_in=rows_in,
        put=put,
        take=take,
        out=out,
        **named(PASS_NAMES, refs[11 : 11 + count]),
        **named(SHARED_BUFFERS, refs[11 + count : -4]),
    )
    given, tile_v, load_sem, tile_sem = refs[-4:]
    loaded = run_copies(
        [
            pltpu.make_async_copy(w_in.at[layer], r.win_v, load_sem.at[0]),
            pltpu.make_async_copy(w_down.at[layer], r.wdown_v, load_sem.at[1]),
            pltpu.make_async_copy(gate_up, r.gbuf, load_sem.at[2]),
            pltpu.make_async_copy(sent, given, load_sem.at[3]),
            pltpu.make_async_copy(hidden, r.zbuf, load_sem.at[4]),
        ]
    )
    greet_plane(plan, along=True)
    stages = moe_stages(plan, True, r)
    first, second, finish = weight_tiles(
        plan, given, r.zbuf, r.gbuf, r.xbuf, in_term, down_term, tile_v, tile_sem
    )
    stages.begin()
    first_part(plan, stages, loaded)
    second_part(plan, stages, (first, second))
    for turn in late_relays(plan.nz):
        stages.relay(turn)
    stages.finish()
    stages.free_all()
    finish()


def moe_both_kernel(plan, layer, *refs):
    rows_in, rows_back, one, weighted, w_in, w_down, base = refs[:7]
    out, out_back, in_term, down_term = refs[7:11]
    count = len(PASS_NAMES)
    shared = named(SHARED_BUFFERS, refs[11 + 2 * count : -2])
    ahead = SimpleNamespace(
        rows_in=rows_in,
        put=one,
        take=weighted,
        out=out,
        **named(PASS_NAMES, refs[11 : 11 + count]),
        **shared,
    )
    back = SimpleNamespace(
        rows_in=rows_back,
        put=weighted,
        take=one,
        out=out_back,
        **named(PASS_NAMES, refs[11 + count : 11 + 2 * count]),
        **shared,
    )
    load_sem, tile_sem = refs[-2:]
    loaded = run_copies(
        [
            pltpu.make_async_copy(w_in.at[layer], ahead.win_v, load_sem.at[0]),
            pltpu.make_async_copy(w_down.at[layer], ahead.wdown_v, load_sem.at[1]),
            pltpu.make_async_copy(base, out, load_sem.at[2]),
        ]
    )
    greet_plane(plan, along=True)
    forward = moe_stages(plan, False, ahead)
    backward = moe_stages(plan, True, back)
    first, second, finish = weight_tiles(
        plan,
        ahead.xbuf,
        back.zbuf,
        back.gbuf,
        back.xbuf,
        in_term,
        down_term,
        ahead.line,
        tile_sem,
    )
    nz, last = plan.nz, plan.nz - 1
    forward.begin()
    first_part(plan, forward, loaded)
    backward.begin()
    order = list(reversed(range(nz)))
    relays = list(late_relays(nz))

    def arrive():
        for index in range(3, nz):
            backward.fetch(index)

    second_part(
        plan,
        forward,
        (
            lambda: backward.fetch(1),
            lambda: backward.fetch(2),
            arrive,
        ),
    )
    backward.fetch(0)

    def put(index):
        forward.free_put(index)
        backward.put(index)

    def expert(index):
        forward.free_back(index)
        backward.expert(index)

    def take(index):
        forward.free_sum(index)
        backward.take(index)

    put(order[0])
    for turn in relays[: len(relays) // 2]:
        forward.relay(turn)
    put(order[1])
    expert(order[0])
    for turn in relays[len(relays) // 2 :]:
        forward.relay(turn)
    put(order[2])
    expert(order[1])
    forward.finish()
    take(order[0])
    for place in range(3, nz):
        put(order[place])
        expert(order[place - 1])
        take(order[place - 2])
    backward.relay(0)
    expert(order[-1])
    first()
    take(order[-2])
    for turn in relays:
        backward.relay(turn)
    second()
    take(order[-1])
    backward.finish()
    backward.free_all()
    finish()


def moe_specs(plan, collective_id):
    return dict(
        compiler_params=pltpu.CompilerParams(
            collective_id=collective_id, has_side_effects=True, vmem_limit_bytes=VMEM_LIMIT
        ),
    )


def saved_shapes(plan):
    return [
        jax.ShapeDtypeStruct((plan.blocks, plan.sources, plan.slots, D), BF16),
        jax.ShapeDtypeStruct((plan.blocks, plan.many, 2 * FF), BF16),
        jax.ShapeDtypeStruct((plan.blocks, plan.many, FF), BF16),
    ]


TERMS = [jax.ShapeDtypeStruct((D, 2 * FF), BF16), jax.ShapeDtypeStruct((FF, D), BF16)]


def moe_call(plan, layer, kind, collective_id, rows_in, put, take, w_in, w_down, base):
    vmem = pl.BlockSpec(memory_space=pltpu.VMEM)
    hbm = pl.BlockSpec(memory_space=pltpu.HBM)
    return pl.pallas_call(
        functools.partial(moe_kernel, plan, layer),
        out_shape=[jax.ShapeDtypeStruct((plan.rows, D), kind)] + saved_shapes(plan),
        in_specs=[vmem] * 3 + [hbm] * 3,
        out_specs=[vmem] + [hbm] * 3,
        scratch_shapes=pass_scratch(plan) + shared_scratch(plan) + [pltpu.VMEM((plan.rows, D), F32), DMA((3,)), DMA((3,))],
        **moe_specs(plan, collective_id),
    )(rows_in, put, take, w_in, w_down, base)


def moe_back_call(plan, layer, collective_id, rows_in, put, take, w_in, w_down, saved):
    vmem = pl.BlockSpec(memory_space=pltpu.VMEM)
    hbm = pl.BlockSpec(memory_space=pltpu.HBM)
    out, *terms = pl.pallas_call(
        functools.partial(moe_back_kernel, plan, layer),
        out_shape=[jax.ShapeDtypeStruct((plan.rows, D), F32)] + TERMS,
        in_specs=[vmem] * 3 + [hbm] * 5,
        out_specs=[vmem] + [hbm] * 2,
        scratch_shapes=pass_scratch(plan)
        + shared_scratch(plan)
        + [
            pltpu.VMEM((plan.blocks, plan.sources, plan.slots, D), BF16),
            pltpu.VMEM((2, TILE, D), BF16),
            DMA((5,)),
            DMA((2,)),
        ],
        **moe_specs(plan, collective_id),
    )(rows_in, put, take, w_in, w_down, *saved)
    return out, terms


def both_fit(plan):
    scratch = pass_scratch(plan) * 2 + shared_scratch(plan)
    words = sum(
        math.prod(part.shape) for part in scratch if getattr(part, "dtype", None) == BF16
    )
    return 2 * words + 10 * 2**20 < VMEM_LIMIT and plan.rows == TILE


def moe_both_call(plan, layer, collective_id, rows_in, rows_back, one, weighted, w_in, w_down, base):
    vmem = pl.BlockSpec(memory_space=pltpu.VMEM)
    hbm = pl.BlockSpec(memory_space=pltpu.HBM)
    out, out_back, *terms = pl.pallas_call(
        functools.partial(moe_both_kernel, plan, layer),
        out_shape=[jax.ShapeDtypeStruct((plan.rows, D), F32)] * 2 + TERMS,
        in_specs=[vmem, hbm, vmem, vmem] + [hbm] * 3,
        out_specs=[vmem] * 2 + [hbm] * 2,
        scratch_shapes=pass_scratch(plan) * 2
        + shared_scratch(plan)
        + [DMA((3,)), DMA((2,))],
        **moe_specs(plan, collective_id),
    )(rows_in, rows_back, one, weighted, w_in, w_down, base)
    return out, out_back, terms


def expert_spread(plan, ins, outs, send, recv, pass_send, pass_recv):
    x, z, s = me()
    nx, ns, group = plan.nx, plan.ns, plan.group
    rank = x * ns + s
    own_expert, own_part = rank // group, rank % group
    own = [(layer, k) for layer in range(nx) for k in range(ns // group)]

    def first(expert, which):
        to = expert * group + s % group
        return to == rank, remote(
            ins[which].at[expert],
            outs[which].at[x, s],
            send.at[expert, which],
            recv.at[x, s, which],
            (to // ns, z, to % ns),
        )

    def onward(layer, source, step, which):
        to = own_expert * group + (own_part + step) % group
        return remote(
            outs[which].at[layer, source],
            outs[which].at[layer, source],
            pass_send.at[layer, source, step - 1, which],
            pass_recv.at[layer, source, which],
            (to // ns, z, to % ns),
        )

    def start(expert, which):
        here, copy = first(expert, which)

        @pl.when(here)
        def _():
            pltpu.make_async_copy(
                ins[which].at[expert], outs[which].at[x, s], recv.at[x, s, which]
            ).start()

        @pl.when(jnp.logical_not(here))
        def _():
            copy.start()

    def pass_on():
        for layer, k in own:
            source = k * group + own_part
            for which in range(2):
                landed(outs[which].at[layer, source], recv.at[layer, source, which])
                for step in range(1, group):
                    onward(layer, source, step, which).start()

    def finish():
        for layer, k in own:
            for step in range(1, group):
                source = k * group + (own_part + step) % group
                for which in range(2):
                    landed(outs[which].at[layer, source], pass_recv.at[layer, source, which])
        for which in range(2):
            for expert in range(EXP_DEV):
                here, copy = first(expert, which)

                @pl.when(jnp.logical_not(here))
                def _():
                    copy.wait_send()

        for layer, k in own:
            source = k * group + own_part
            for which in range(2):
                for step in range(1, group):
                    onward(layer, source, step, which).wait_send()

    return start, pass_on, finish


def spread_scratch(plan):
    nx, ns, group = plan.nx, plan.ns, plan.group
    return [
        DMA((EXP_DEV, 2)),
        DMA((nx, ns, 2)),
        DMA((nx, ns, group - 1, 2)),
        DMA((nx, ns, 2)),
    ]


def spread_kernel(plan, *refs):
    greet_plane(plan)
    start, pass_on, finish = expert_spread(plan, refs[:2], refs[2:4], *refs[4:])
    for which in range(2):
        for expert in range(EXP_DEV):
            start(expert, which)
    pass_on()
    finish()


def spread_call(plan, collective_id, gate_up, down):
    hbm = pl.BlockSpec(memory_space=pltpu.HBM)
    vmem = pl.BlockSpec(memory_space=pltpu.VMEM)
    outs = [
        jax.ShapeDtypeStruct((plan.nx, plan.ns) + part.shape[1:], BF16) for part in (gate_up, down)
    ]
    return pl.pallas_call(
        functools.partial(spread_kernel, plan),
        out_shape=outs,
        in_specs=[vmem, vmem],
        out_specs=[hbm, hbm],
        scratch_shapes=spread_scratch(plan),
        compiler_params=pltpu.CompilerParams(
            collective_id=collective_id, has_side_effects=True, vmem_limit_bytes=VMEM_LIMIT
        ),
    )(gate_up, down)


def gather_kernel(plan, *refs):
    piece, table, wide_ins = refs[0], refs[1], refs[2:4]
    out, table_out, wide_outs = refs[4], refs[5], refs[6:8]
    (line_recv, right, left, copy_sem, plane_recv, to_core, to_x, to_y) = refs[8:16]
    (up_recv, up_right, up_left, table_send, table_recv) = refs[16:21]
    wide_v, low_v, load_sem = refs[21:23], refs[23:25], refs[25]
    x, z, s = me()
    nz = plan.nz
    row, side = s // 2, s % 2
    over = (s + 2) % 4
    loads = [
        pltpu.make_async_copy(wide_ins[which].at[expert], wide_v[which].at[expert], load_sem.at[which, expert])
        for which in range(2)
        for expert in range(EXP_DEV)
    ]
    for load in loads:
        load.start()
    greet_plane(plan, along=True)
    start, pass_on, finish = expert_spread(plan, low_v, wide_outs, *refs[26:])
    third = piece.shape[0] // 3
    parts = (
        (pl.ds(0, 2 * third), pl.ds(0, third), pl.ds(third, third)),
        (
            pl.ds(2 * third, third),
            pl.ds(2 * third, third // 2),
            pl.ds(2 * third + third // 2, third // 2),
        ),
    )
    core = (x, z, s + 1 - 2 * side)
    across_x = (1 - x, z, s)
    across_y = (x, z, over)

    def along(block, step, own):
        rows = parts[0][0]
        place = out.at[x, block, s, rows]
        sem = right if step > 0 else left
        return remote(
            piece.at[rows] if own else place,
            place,
            sem.at[block],
            line_recv.at[block],
            (x, z + step, s),
        )

    def upward(block, layer, to_row, step, own=False):
        rows = parts[1][0]
        place = out.at[layer, block, to_row * 2 + side, rows]
        sem = up_right if step > 0 else up_left
        return remote(
            piece.at[rows] if own else place,
            place,
            sem.at[block, layer, to_row],
            up_recv.at[block, layer, to_row],
            (x, z + step, s),
        )

    def passed(layer, block, shard, part, kind, sem, to, own=False):
        rows = parts[part][kind]
        place = out.at[layer, block, shard, rows]
        return remote(
            piece.at[rows] if own else place,
            place,
            sem.at[layer, block, shard // 2, part],
            plane_recv.at[layer, block, shard, part, kind],
            to,
        )

    def arrived(layer, block, shard, part, kind):
        landed(
            out.at[layer, block, shard, parts[part][kind]],
            plane_recv.at[layer, block, shard, part, kind],
        )

    def column_copies(block, part, own=False, ways=3):
        ways = ((to_x, across_x), (to_y, across_y), (to_core, core))[:ways]
        return [passed(x, block, s, part, 0, sem, to, own) for sem, to in ways]

    def neighbour_copies(block, part):
        return [
            passed(1 - x, block, s, part, 1, to_y, across_y),
            passed(1 - x, block, s, part, 0, to_core, core),
            passed(x, block, over, part, 2, to_x, across_x),
            passed(x, block, over, part, 0, to_core, core),
        ]

    def send_up(block, layer, to_row, own=False):
        @pl.when((block <= z) & (z + 1 < nz))
        def _():
            upward(block, layer, to_row, 1, own).start()

        @pl.when((block >= z) & (z > 0))
        def _():
            upward(block, layer, to_row, -1, own).start()

    def neighbours_of(block, part):
        copies = neighbour_copies(block, part)
        arrived(1 - x, block, s, part, 0)
        copies[0].start()
        copies[1].start()
        arrived(x, block, over, part, 0)
        copies[2].start()
        copies[3].start()

    def opposite_of(block, part):
        arrived(1 - x, block, over, part, 1)
        arrived(1 - x, block, over, part, 2)
        passed(1 - x, block, over, part, 0, to_core, core).start()

    @pl.when(z + 1 < nz)
    def _():
        along(z, 1, True).start()

    @pl.when(z > 0)
    def _():
        along(z, -1, True).start()

    send_up(z, x, row, True)
    own = pltpu.make_async_copy(piece, out.at[x, z, s], copy_sem.at[0])
    own.start()
    for part in (1, 0):
        for copy in column_copies(z, part, True):
            copy.start()

    def table_copy(step):
        to = (z + step) % nz
        return remote(
            table.at[to], table_out.at[z], table_send.at[step - 1], table_recv.at[z], (x, to, s)
        )

    for step in range(1, nz):
        table_copy(step).start()
    table_out[z] = table[z]
    neighbours_of(z, 1)
    send_up(z, 1 - x, row)
    send_up(z, x, 1 - row)
    opposite_of(z, 1)
    send_up(z, 1 - x, 1 - row)

    def column(index, _):
        block = nearest(z, index, nz)

        @pl.when(block < z)
        def _():
            along(block, 1, False).wait_recv()

            @pl.when(z + 1 < nz)
            def _():
                along(block, 1, False).start()

        @pl.when(block > z)
        def _():
            along(block, -1, False).wait_recv()

            @pl.when(z > 0)
            def _():
                along(block, -1, False).start()

        for copy in column_copies(block, 0):
            copy.start()
        for layer in range(2):
            for to_row in range(2):
                upward(block, layer, to_row, 1).wait_recv()
                send_up(block, layer, to_row)
                passed(layer, block, to_row * 2 + side, 1, 0, to_core, core).start()
        return 0

    def neighbours(index, _):
        neighbours_of(nearest(z, index, nz), 0)
        return 0

    def opposite(index, _):
        opposite_of(nearest(z, index, nz), 0)
        return 0

    for place, load in enumerate(loads):
        which, expert = place // EXP_DEV, place % EXP_DEV
        load.wait()
        low_v[which][expert] = wide_v[which][expert].astype(BF16)
        start(expert, which)
    lax.fori_loop(1, nz, column, 0)
    lax.fori_loop(0, nz, neighbours, 0)
    lax.fori_loop(0, nz, opposite, 0)
    own.wait()
    pass_on()
    for step in range(1, nz):
        block = (z + step) % nz
        landed(table_out.at[block], table_recv.at[block])
        table_copy(step).wait_send()

    def drain(block, _):
        other = s + 1 - 2 * side

        @pl.when((block <= z) & (z + 1 < nz))
        def _():
            along(block, 1, False).wait_send()

        @pl.when((block >= z) & (z > 0))
        def _():
            along(block, -1, False).wait_send()

        for layer in range(2):
            for to_row in range(2):
                for part in range(2):
                    arrived(layer, block, to_row * 2 + other % 2, part, 0)
                    passed(layer, block, to_row * 2 + side, part, 0, to_core, core).wait_send()

                @pl.when((block <= z) & (z + 1 < nz))
                def _():
                    upward(block, layer, to_row, 1).wait_send()

                @pl.when((block >= z) & (z > 0))
                def _():
                    upward(block, layer, to_row, -1).wait_send()

        def plane(part):
            for copy in column_copies(block, part, ways=2):
                copy.wait_send()
            passed(1 - x, block, s, part, 1, to_y, across_y).wait_send()
            passed(x, block, over, part, 2, to_x, across_x).wait_send()

        plane(0)

        @pl.when(block == z)
        def _():
            plane(1)

        return 0

    lax.fori_loop(0, nz, drain, 0)
    finish()


def gather_call(plan, collective_id, attention, table, experts):
    hbm = pl.BlockSpec(memory_space=pltpu.HBM)
    vmem = pl.BlockSpec(memory_space=pltpu.VMEM)
    nx, nz, ns = plan.nx, plan.nz, plan.ns
    outs = [
        jax.ShapeDtypeStruct((nx, nz, ns) + attention.shape, BF16),
        jax.ShapeDtypeStruct(table.shape, F32),
    ]
    outs += [jax.ShapeDtypeStruct((nx, ns) + part.shape[1:], BF16) for part in experts]
    return pl.pallas_call(
        functools.partial(gather_kernel, plan),
        out_shape=outs,
        in_specs=[vmem, vmem, hbm, hbm],
        out_specs=[hbm, vmem, hbm, hbm],
        scratch_shapes=[
            DMA((nz,)),
            DMA((nz,)),
            DMA((nz,)),
            DMA((1,)),
            DMA((nx, nz, ns, 2, 3)),
            DMA((nx, nz, 2, 2)),
            DMA((nx, nz, 2, 2)),
            DMA((nx, nz, 2, 2)),
            DMA((nz, nx, 2)),
            DMA((nz, nx, 2)),
            DMA((nz, nx, 2)),
            DMA((nz - 1,)),
            DMA((nz,)),
        ]
        + [pltpu.VMEM(part.shape, F32) for part in experts]
        + [pltpu.VMEM(part.shape, BF16) for part in experts]
        + [DMA((2, EXP_DEV))]
        + spread_scratch(plan),
        compiler_params=pltpu.CompilerParams(
            collective_id=collective_id, has_side_effects=True, vmem_limit_bytes=VMEM_LIMIT
        ),
    )(attention, table, *experts)


def expert_collect(plan, ins, outs, parts, stage, load, swap_send, swap_recv, send, recv):
    x, z, s = me()
    ns, group = plan.ns, plan.group
    rank = x * ns + s
    own_expert, own_part = rank // group, rank % group
    order = [(k, kind) for kind in range(len(ins)) for k in range(ns // group)]

    def swap(k, step, kind):
        part_to = (own_part + step) % group
        to = own_expert * group + part_to
        return remote(
            ins[kind].at[k * group + part_to],
            parts[kind].at[step - 1, k],
            swap_send.at[step - 1, k, kind],
            swap_recv.at[step - 1, k, kind],
            (to // ns, z, to % ns),
        )

    def own(k, kind):
        return pltpu.make_async_copy(
            ins[kind].at[k * group + own_part], stage[kind].at[k], load.at[k, kind]
        )

    def home(k, kind):
        layer, which = kind // 2, kind % 2
        here = (x == layer) & (s == k * group + own_part)
        return here, remote(
            stage[kind].at[k],
            outs[which].at[own_expert],
            send.at[k, kind],
            recv.at[own_expert, which],
            (layer, z, k * group + own_part),
        )

    def start():
        for k, kind in order:
            own(k, kind).start()
            for step in range(1, group):
                swap(k, step, kind).start()

    def add(place):
        k, kind = order[place]
        own(k, kind).wait()
        for step in range(1, group):
            swap(k, step, kind).wait_recv()
        total = stage[kind][k].astype(F32)
        for step in range(1, group):
            total += parts[kind][step - 1, k].astype(F32)
        stage[kind][k] = total.astype(BF16)
        here, copy = home(k, kind)

        @pl.when(here)
        def _():
            which = kind % 2
            pltpu.make_async_copy(
                stage[kind].at[k], outs[which].at[own_expert], recv.at[own_expert, which]
            ).start()

        @pl.when(jnp.logical_not(here))
        def _():
            copy.start()

    def finish():
        for which in range(2):
            for expert in range(EXP_DEV):
                landed(outs[which].at[expert], recv.at[expert, which])
        for k, kind in order:
            for step in range(1, group):
                swap(k, step, kind).wait_send()
            here, copy = home(k, kind)

            @pl.when(jnp.logical_not(here))
            def _():
                copy.wait_send()

    return len(order), start, add, finish


def collect_scratch(plan, values):
    group, each, kinds = plan.group, plan.ns // plan.group, len(values)
    return (
        [pltpu.VMEM((group - 1, each) + part.shape[1:], BF16) for part in values]
        + [pltpu.VMEM((each,) + part.shape[1:], BF16) for part in values]
        + [
            DMA((each, kinds)),
            DMA((group - 1, each, kinds)),
            DMA((group - 1, each, kinds)),
            DMA((each, kinds)),
            DMA((EXP_DEV, 2)),
        ]
    )


def collect_kernel(plan, *refs):
    kinds = 2 * plan.nx
    ins, outs = refs[:kinds], refs[kinds : kinds + 2]
    parts, stage = refs[kinds + 2 : 2 * kinds + 2], refs[2 * kinds + 2 : 3 * kinds + 2]
    greet_plane(plan)
    count, start, add, finish = expert_collect(
        plan, ins, outs, parts, stage, *refs[3 * kinds + 2 :]
    )
    start()
    for place in range(count):
        add(place)
    finish()


def collect_call(plan, collective_id, terms):
    ns = plan.ns
    hbm = pl.BlockSpec(memory_space=pltpu.HBM)
    values = [part.reshape(ns, part.shape[0] // ns, D) for layer in terms for part in layer]
    return pl.pallas_call(
        functools.partial(collect_kernel, plan),
        out_shape=[jax.ShapeDtypeStruct((EXP_DEV,) + part.shape[1:], BF16) for part in values[:2]],
        in_specs=[hbm] * len(values),
        out_specs=[hbm, hbm],
        scratch_shapes=collect_scratch(plan, values),
        compiler_params=pltpu.CompilerParams(
            collective_id=collective_id, has_side_effects=True, vmem_limit_bytes=VMEM_LIMIT
        ),
    )(*values)


ADDS = 5
OWN_UP = 4


def reduce_kernel(plan, *refs):
    grads, wide_ins, outs, wide_outs = refs[0:2], refs[2:6], refs[6:10], refs[10:12]
    scratch = refs[12:]
    (mine, given, x_one, y_one, y_two, x_two, chain) = scratch[:7]
    (up, x_up, y_up, y_up_two, x_up_two) = scratch[7:12]
    (
        load_sem,
        core_send,
        core_recv,
        x_one_send,
        x_one_recv,
        y_one_send,
        y_one_recv,
        x_two_send,
        x_two_recv,
        y_two_send,
        y_two_recv,
        chain_send,
        chain_recv,
        up_send,
        up_recv,
        plane_send,
        plane_recv,
    ) = scratch[12:29]
    parts, stage = scratch[29:33], scratch[33:37]
    x, z, s = me()
    nz = plan.nz
    row, side = s // 2, s % 2
    core = (x, z, s + 1 - 2 * side)
    across_x = (1 - x, z, s)
    across_y = (x, z, (s + 2) % 4)
    third = grads[0].shape[2] // 3
    greet_plane(plan, along=True)
    count, start, add, finish = expert_collect(
        plan, wide_ins, wide_outs, parts, stage, *scratch[37:]
    )
    both = range(2)
    most = pl.ds(0, 2 * third)
    low, high = pl.ds(0, third), pl.ds(third, third)
    rest = pl.ds(2 * third, third)
    rest_low = pl.ds(2 * third, third // 2)
    rest_high = pl.ds(2 * third + third // 2, third // 2)

    def load(layer, block, to_row):
        return pltpu.make_async_copy(
            grads[layer].at[block, to_row * 2 + side],
            mine.at[layer, block, to_row],
            load_sem.at[layer, block, to_row],
        )

    def give(layer, block, to_row):
        return remote(
            grads[layer].at[block, to_row * 2 + 1 - side],
            given.at[layer, block, to_row],
            core_send.at[layer, block, to_row],
            core_recv.at[layer, block, to_row],
            core,
        )

    def send_x_one(block, to_row):
        return remote(
            mine.at[1 - x, block, to_row, low],
            x_one.at[block, to_row],
            x_one_send.at[block, to_row],
            x_one_recv.at[block, to_row],
            across_x,
        )

    def send_y_one(layer, block):
        return remote(
            mine.at[layer, block, 1 - row, high],
            y_one.at[layer, block],
            y_one_send.at[layer, block],
            y_one_recv.at[layer, block],
            across_y,
        )

    def send_y_two(block):
        return remote(
            mine.at[x, block, 1 - row, low],
            y_two.at[block],
            y_two_send.at[block],
            y_two_recv.at[block],
            across_y,
        )

    def send_x_two(block):
        return remote(
            mine.at[1 - x, block, row, high],
            x_two.at[block],
            x_two_send.at[block],
            x_two_recv.at[block],
            across_x,
        )

    def onward(block):
        rightward = (block > z).astype(jnp.int32)
        to = z - 1 + 2 * rightward
        return to, jnp.where((rightward == 1) & (block == to), nz, block)

    def send_chain(block):
        to, into = onward(block)
        return remote(
            mine.at[x, block, row, most],
            chain.at[into],
            chain_send.at[block],
            chain_recv.at[into],
            (x, to, s),
        )

    def send_up(block, layer, to_row):
        to, into = onward(block)
        return remote(
            mine.at[layer, block, to_row, rest],
            up.at[into, layer, to_row],
            up_send.at[block, layer, to_row],
            up_recv.at[into, layer, to_row],
            (x, to, s),
        )

    def plane_copy(step, place):
        if step == 0:
            src, dst, to = mine.at[1 - x, z, place, rest_low], x_up.at[place], across_x
        elif step == 1:
            src, dst, to = mine.at[place, z, 1 - row, rest_high], y_up.at[place], across_y
        elif step == 2:
            src, dst, to = mine.at[x, z, 1 - row, rest_low], y_up_two.at[0], across_y
        else:
            src, dst, to = mine.at[1 - x, z, row, rest_high], x_up_two.at[0], across_x
        return remote(src, dst, plane_send.at[step, place], plane_recv.at[step, place], to)

    def gain(at, other):
        mine[at] = (mine[at].astype(F32) + other.astype(F32)).astype(BF16)

    def begin(index):
        block = nearest(z, nz - 1 - index, nz)
        for layer in both:
            for to_row in both:
                load(layer, block, to_row).start()
                give(layer, block, to_row).start()

    def is_origin(block):
        return ((block < z) & (z == nz - 1)) | ((block > z) & (z == 0))

    def stage_core(index):
        block = nearest(z, nz - 1 - index, nz)
        for layer in both:
            for to_row in both:
                load(layer, block, to_row).wait()
                give(layer, block, to_row).wait_recv()
                gain((layer, block, to_row), given[layer, block, to_row])
        for to_row in both:
            send_x_one(block, to_row).start()
        for layer in both:
            send_y_one(layer, block).start()

        @pl.when(is_origin(block))
        def _():
            for layer in both:
                for to_row in both:
                    send_up(block, layer, to_row).start()

    def relay_up(index):
        block = nearest(z, nz - 1 - index, nz)

        @pl.when((z > 0) & (z < nz - 1))
        def _():
            for layer in both:
                for to_row in both:
                    landed(up.at[block, layer, to_row], up_recv.at[block, layer, to_row])
                    gain((layer, block, to_row, rest), up[block, layer, to_row])
                    send_up(block, layer, to_row).start()

    def own_up():
        for layer in both:
            for to_row in both:

                @pl.when(z + 1 < nz)
                def _():
                    landed(up.at[z, layer, to_row], up_recv.at[z, layer, to_row])
                    gain((layer, z, to_row, rest), up[z, layer, to_row])

                @pl.when(z > 0)
                def _():
                    landed(up.at[nz, layer, to_row], up_recv.at[nz, layer, to_row])
                    gain((layer, z, to_row, rest), up[nz, layer, to_row])

        for place in both:
            plane_copy(0, place).start()
            plane_copy(1, place).start()

    def up_first():
        for place in both:
            plane_copy(0, place).wait_recv()
            gain((x, z, place, rest_low), x_up[place])
            plane_copy(1, place).wait_recv()
            gain((place, z, row, rest_high), y_up[place])
        plane_copy(2, 0).start()
        plane_copy(3, 0).start()

    def up_second():
        plane_copy(2, 0).wait_recv()
        gain((x, z, row, rest_low), y_up_two[0])
        plane_copy(3, 0).wait_recv()
        gain((x, z, row, rest_high), x_up_two[0])

    def stage_first(index):
        block = nearest(z, nz - 1 - index, nz)
        for to_row in both:
            send_x_one(block, to_row).wait_recv()
            gain((x, block, to_row, low), x_one[block, to_row])
        send_y_two(block).start()
        for layer in both:
            send_y_one(layer, block).wait_recv()
            gain((layer, block, row, high), y_one[layer, block])
        send_x_two(block).start()

    def stage_second(index):
        block = nearest(z, nz - 1 - index, nz)
        send_y_two(block).wait_recv()
        gain((x, block, row, low), y_two[block])
        send_x_two(block).wait_recv()
        gain((x, block, row, high), x_two[block])

        @pl.when(is_origin(block))
        def _():
            send_chain(block).start()

    begin(0)
    begin(1)
    adds = 0
    for index in range(nz + 3):
        if index < nz:
            stage_core(index)
        if index + 2 < nz:
            begin(index + 2)
        if index == 0:
            start()
        if 1 <= index < nz + 1:
            stage_first(index - 1)
        if 1 <= index < nz:
            relay_up(index - 1)
        if 2 <= index < nz + 2:
            stage_second(index - 2)
        if index == OWN_UP:
            own_up()
        if index == OWN_UP + 1:
            up_first()
        while adds < count and index >= ADDS:
            add(adds)
            adds += 1
    up_second()

    def relay(turn, _):
        lower = z < nz // 2
        first = jnp.where(lower, nz - 1 - z, z)
        early = turn < first
        ahead = jnp.where(early, first - turn, nz - 1 - turn)
        rightward = lower == early
        block = jnp.where(rightward, z + ahead, z - ahead)

        @pl.when((z > 0) & (z < nz - 1))
        def _():
            landed(chain.at[block], chain_recv.at[block])
            gain((x, block, row, most), chain[block])
            send_chain(block).start()

        return 0

    lax.fori_loop(0, nz - 1, relay, 0)
    columns = (slice(0, WQ), slice(WQ, PROJ), slice(PROJ, WIN), slice(WIN, WIN + D))
    for out, at in zip(outs, columns):
        out[...] = mine[x, z, row, :, at].astype(F32)
    for place, there in ((z, z + 1 < nz), (nz, z > 0)):

        @pl.when(there)
        def _():
            landed(chain.at[place], chain_recv.at[place])
            for out, at in zip(outs, columns):
                out[: 2 * third] += chain[place, :, at].astype(F32)

    def drain(block, _):
        for layer in both:
            for to_row in both:
                give(layer, block, to_row).wait_send()

                @pl.when(block != z)
                def _():
                    send_up(block, layer, to_row).wait_send()

            send_y_one(layer, block).wait_send()
        for to_row in both:
            send_x_one(block, to_row).wait_send()
        send_y_two(block).wait_send()
        send_x_two(block).wait_send()

        @pl.when(block != z)
        def _():
            send_chain(block).wait_send()

        return 0

    lax.fori_loop(0, nz, drain, 0)
    for step, place in ((0, 0), (0, 1), (1, 0), (1, 1), (2, 0), (3, 0)):
        plane_copy(step, place).wait_send()
    finish()


def reduce_call(plan, collective_id, attention, terms):
    nx, nz, ns = plan.nx, plan.nz, plan.ns
    hbm = pl.BlockSpec(memory_space=pltpu.HBM)
    vmem = pl.BlockSpec(memory_space=pltpu.VMEM)
    grads = [part.reshape(nz, ns, -1, part.shape[1]) for part in attention]
    values = [part.reshape(ns, part.shape[0] // ns, D) for layer in terms for part in layer]
    held = [(EXP_DEV,) + part.shape[1:] for part in values[:2]]
    rows, width = grads[0].shape[2:]
    third = rows // 3
    return pl.pallas_call(
        functools.partial(reduce_kernel, plan),
        out_shape=[jax.ShapeDtypeStruct((rows, part), F32) for part in (WQ, 2 * WK, PAD, D)]
        + [jax.ShapeDtypeStruct(shape, BF16) for shape in held],
        in_specs=[hbm] * 6,
        out_specs=[vmem] * 4 + [hbm] * 2,
        scratch_shapes=[
            pltpu.VMEM((nx, nz, 2, rows, width), BF16),
            pltpu.VMEM((nx, nz, 2, rows, width), BF16),
            pltpu.VMEM((nz, 2, third, width), BF16),
            pltpu.VMEM((nx, nz, third, width), BF16),
            pltpu.VMEM((nz, third, width), BF16),
            pltpu.VMEM((nz, third, width), BF16),
            pltpu.VMEM((nz + 1, 2 * third, width), BF16),
            pltpu.VMEM((nz + 1, nx, 2, third, width), BF16),
            pltpu.VMEM((2, third // 2, width), BF16),
            pltpu.VMEM((2, third // 2, width), BF16),
            pltpu.VMEM((1, third // 2, width), BF16),
            pltpu.VMEM((1, third // 2, width), BF16),
            DMA((nx, nz, 2)),
            DMA((nx, nz, 2)),
            DMA((nx, nz, 2)),
            DMA((nz, 2)),
            DMA((nz, 2)),
            DMA((nx, nz)),
            DMA((nx, nz)),
            DMA((nz,)),
            DMA((nz,)),
            DMA((nz,)),
            DMA((nz,)),
            DMA((nz,)),
            DMA((nz + 1,)),
            DMA((nz, nx, 2)),
            DMA((nz + 1, nx, 2)),
            DMA((4, 2)),
            DMA((4, 2)),
        ]
        + collect_scratch(plan, values),
        compiler_params=pltpu.CompilerParams(
            collective_id=collective_id, has_side_effects=True, vmem_limit_bytes=VMEM_LIMIT
        ),
    )(*grads, *values)


def greet_shards(plan):
    x, z, s = me()
    barrier = pltpu.get_barrier_semaphore()
    for step in range(1, plan.ns):
        pl.semaphore_signal(
            barrier, inc=1, device_id=(x, z, (s + step) % plan.ns), device_id_type=MESH
        )
    pl.semaphore_wait(barrier, plan.ns - 1)


def turned(value, cosine, sine):
    return value * cosine + pltpu.roll(value, HD // 2, 1) * sine


def weights_of(queries, keys, allowed):
    raw = lax.dot_general(queries, keys, NARROW, preferred_element_type=F32)
    raw = jnp.where(allowed, raw * SCALE, -1e30)
    raw = jnp.exp(raw - jnp.max(raw, axis=1, keepdims=True))
    return raw / jnp.sum(raw, axis=1, keepdims=True)


def attend_kernel(plan, layer, *refs):
    (start, gains, cosine, sine, mask, weights) = refs[:6]
    (middle, normed, low, queries, kv, mixed) = refs[6:12]
    (win_v, wout_v, load_sem, send, recv) = refs[12:]
    x, z, s = me()
    tokens, rows, micro, ns = plan.tokens, plan.rows, plan.micro, plan.ns
    length = ns * tokens
    load_in = pltpu.make_async_copy(weights.at[layer, :, pl.ds(0, WIN)], win_v, load_sem.at[0])
    load_out = pltpu.make_async_copy(weights.at[layer, :, pl.ds(WIN, D)], wout_v, load_sem.at[1])
    load_in.start()
    load_out.start()
    greet_shards(plan)

    hidden = start[...].astype(F32)
    inverse = lax.rsqrt(jnp.mean(hidden * hidden, axis=1, keepdims=True) + epsilon)
    low[...] = (hidden * inverse * gains[0:1, :]).astype(BF16)
    load_in.wait()
    own = jnp.dot(low[...], win_v[:, WQ : WQ + 2 * WK], preferred_element_type=F32)
    for head in range(KV_HEADS):
        at = slice(head * HD, (head + 1) * HD)
        key = turned(own[:, at], cosine[...], sine[...]).astype(BF16)
        value = own[:, WK + head * HD : WK + (head + 1) * HD].astype(BF16)
        for m in range(micro):
            block = slice(m * tokens, (m + 1) * tokens)
            kv[s, m, :, at] = key[block]
            kv[s, m, :, WK + head * HD : WK + (head + 1) * HD] = value[block]

    def share(step, m):
        return remote(
            kv.at[s, m],
            kv.at[s, m],
            send.at[step - 1, m],
            recv.at[s, m],
            (x, z, (s + step) % ns),
        )

    for m in range(micro):
        for step in range(1, ns):
            share(step, m).start()

    def project(step, _):
        at = pl.multiple_of(step * 4 * HD, 4 * HD)
        part = jnp.dot(low[...], win_v[:, pl.ds(at, 4 * HD)], preferred_element_type=F32)
        for head in range(4):
            here = part[:, head * HD : (head + 1) * HD]
            queries[:, pl.ds(at + head * HD, HD)] = turned(here, cosine[...], sine[...]).astype(
                BF16
            )
        return 0

    lax.fori_loop(0, HEADS // 4, project, 0)

    def group(turn, _):
        m, pair = turn // KV_HEADS, turn % KV_HEADS

        @pl.when(pair == 0)
        def _():
            for step in range(1, ns):
                landed(kv.at[(s + step) % ns, m], recv.at[(s + step) % ns, m])

        span = pl.ds(pl.multiple_of(m * tokens, tokens), tokens)
        keys = kv[:, m, :, pl.ds(pl.multiple_of(pair * HD, HD), HD)].reshape(length, HD)
        values = kv[:, m, :, pl.ds(pl.multiple_of(WK + pair * HD, HD), HD)].reshape(length, HD)
        allowed = mask[m] > 0
        for i in range(GROUP):
            at = pl.ds(pl.multiple_of((pair * GROUP + i) * HD, HD), HD)
            probs = weights_of(queries[span, at], keys, allowed).astype(BF16)
            mixed[span, at] = jnp.dot(probs, values, preferred_element_type=F32).astype(BF16)
        return 0

    lax.fori_loop(0, micro * KV_HEADS, group, 0)
    load_out.wait()

    def back(step, _):
        at = pl.ds(pl.multiple_of(step * 512, 512), 512)
        middle[:, at] = start[:, at].astype(F32) + jnp.dot(
            mixed[...], wout_v[:, at], preferred_element_type=F32
        )
        return 0

    lax.fori_loop(0, D // 512, back, 0)
    after = middle[...]
    inverse = lax.rsqrt(jnp.mean(after * after, axis=1, keepdims=True) + epsilon)
    normed[...] = (after * inverse * gains[1:2, :]).astype(BF16)
    for m in range(micro):
        for step in range(1, ns):
            share(step, m).wait_send()


def attend_call(plan, layer, collective_id, start, gains, tables, weights):
    rows, ns, micro = plan.rows, plan.ns, plan.micro
    vmem = pl.BlockSpec(memory_space=pltpu.VMEM)
    hbm = pl.BlockSpec(memory_space=pltpu.HBM)
    shape = jax.ShapeDtypeStruct
    return pl.pallas_call(
        functools.partial(attend_kernel, plan, layer),
        out_shape=[
            shape((rows, D), F32),
            shape((rows, D), BF16),
            shape((rows, D), BF16),
            shape((rows, WQ), BF16),
            shape((ns, micro, plan.tokens, 2 * WK), BF16),
            shape((rows, WQ), BF16),
        ],
        in_specs=[vmem] * 5 + [hbm],
        out_specs=[vmem] * 6,
        scratch_shapes=[
            pltpu.VMEM((D, WIN), BF16),
            pltpu.VMEM((WQ, D), BF16),
            DMA((2,)),
            DMA((ns - 1, micro)),
            DMA((ns, micro)),
        ],
        compiler_params=pltpu.CompilerParams(
            collective_id=collective_id, has_side_effects=True, vmem_limit_bytes=VMEM_LIMIT
        ),
    )(start, gains, *tables, weights)


def return_kernel(plan, layer, *refs):
    (grad_out, grad_moe, middle, start, low, queries, kv, mixed) = refs[:8]
    (gains, cosine, sine, mask, weights) = refs[8:13]
    (result, terms) = refs[13:15]
    (win_v, wout_v, branch, grad_mixed, both, part, got, in_v, out_v, grad_in) = refs[15:25]
    (load_sem, save_in, save_out, send, recv) = refs[25:]
    x, z, s = me()
    tokens, rows, micro, ns = plan.tokens, plan.rows, plan.micro, plan.ns
    length = ns * tokens
    load_in = pltpu.make_async_copy(weights.at[layer, :, pl.ds(0, WIN)], win_v, load_sem.at[0])
    load_out = pltpu.make_async_copy(weights.at[layer, :, pl.ds(WIN, D)], wout_v, load_sem.at[1])
    load_out.start()
    load_in.start()
    greet_shards(plan)

    after = middle[...]
    inverse = lax.rsqrt(jnp.mean(after * after, axis=1, keepdims=True) + epsilon)
    scaled = grad_moe[...] * gains[1:2, :]
    inner = jnp.mean(scaled * after, axis=1, keepdims=True)
    total = grad_out[...].astype(F32) + inverse * scaled - after * (
        inverse * inverse * inverse * inner
    )
    grad_in[...] = total
    branch[...] = total.astype(BF16)
    gain_two = jnp.sum(grad_moe[...] * after * inverse, axis=0, keepdims=True)
    load_out.wait()

    def mix(step, _):
        at = pl.ds(pl.multiple_of(step * 512, 512), 512)
        grad_mixed[:, at] = lax.dot_general(
            branch[...], wout_v[at, :], NARROW, preferred_element_type=F32
        ).astype(BF16)
        return 0

    lax.fori_loop(0, WQ // 512, mix, 0)

    def share(step, m):
        to = (s + step) % ns
        return remote(
            part.at[to, m],
            got.at[s, m],
            send.at[step - 1, m],
            recv.at[s, m],
            (x, z, to),
        )

    def group(turn, _):
        m, pair = turn // KV_HEADS, turn % KV_HEADS
        span = pl.ds(pl.multiple_of(m * tokens, tokens), tokens)
        key_at = pl.ds(pl.multiple_of(pair * HD, HD), HD)
        value_at = pl.ds(pl.multiple_of(WK + pair * HD, HD), HD)
        keys = kv[:, m, :, key_at].reshape(length, HD)
        values = kv[:, m, :, value_at].reshape(length, HD)
        allowed = mask[m] > 0
        grad_keys = jnp.zeros((length, HD), F32)
        grad_values = jnp.zeros((length, HD), F32)
        for i in range(GROUP):
            at = pl.ds(pl.multiple_of((pair * GROUP + i) * HD, HD), HD)
            mine, given = queries[span, at], grad_mixed[span, at]
            probs = weights_of(mine, keys, allowed)
            grad_probs = lax.dot_general(given, values, NARROW, preferred_element_type=F32)
            inside = jnp.sum(grad_probs * probs, axis=1, keepdims=True)
            raw = (probs * (grad_probs - inside) * SCALE).astype(BF16)
            grad_query = jnp.dot(raw, keys, preferred_element_type=F32)
            both[span, at] = turned(grad_query, cosine[span], -sine[span]).astype(BF16)
            grad_keys += lax.dot_general(raw, mine, ACROSS, preferred_element_type=F32)
            grad_values += lax.dot_general(
                probs.astype(BF16), given, ACROSS, preferred_element_type=F32
            )
        part[:, m, :, key_at] = grad_keys.astype(BF16).reshape(ns, tokens, HD)
        part[:, m, :, value_at] = grad_values.astype(BF16).reshape(ns, tokens, HD)

        @pl.when(pair == KV_HEADS - 1)
        def _():
            for step in range(1, ns):
                share(step, m).start()

        return 0

    lax.fori_loop(0, micro * KV_HEADS, group, 0)

    def out_copy(step):
        at = pl.ds(step * 256, 256)
        return pltpu.make_async_copy(out_v.at[at], terms.at[at, pl.ds(WIN, D)], save_out.at[step])

    def in_copy(step):
        at = pl.ds(step * 256, 256)
        return pltpu.make_async_copy(in_v.at[at], terms.at[at, pl.ds(0, WIN)], save_in.at[step])

    def out_tile(step, _):
        at = pl.ds(pl.multiple_of(step * 256, 256), 256)
        out_v[at, :] = lax.dot_general(
            mixed[:, at], branch[...], ACROSS, preferred_element_type=F32
        ).astype(BF16)
        out_copy(step).start()
        return 0

    lax.fori_loop(0, WQ // 256, out_tile, 0)
    load_in.wait()

    def query_tile(step, _):
        at = pl.ds(pl.multiple_of(step * 256, 256), 256)
        in_v[at, :WQ] = lax.dot_general(
            low[:, at], both[:, :WQ], ACROSS, preferred_element_type=F32
        ).astype(BF16)
        return 0

    lax.fori_loop(0, D // 256, query_tile, 0)
    grad_normed = []
    for step in range(D // 512):
        at = slice(step * 512, (step + 1) * 512)
        grad_normed.append(
            lax.dot_general(both[:, :WQ], win_v[at, :WQ], NARROW, preferred_element_type=F32)
        )
    for m in range(micro):
        for step in range(1, ns):
            landed(got.at[(s + step) % ns, m], recv.at[(s + step) % ns, m])
        span = slice(m * tokens, (m + 1) * tokens)
        total = part[s, m].astype(F32)
        for step in range(1, ns):
            total += got[(s + step) % ns, m].astype(F32)
        for head in range(KV_HEADS):
            at = slice(head * HD, (head + 1) * HD)
            both[span, WQ + head * HD : WQ + (head + 1) * HD] = turned(
                total[:, at], cosine[span], -sine[span]
            ).astype(BF16)
        both[span, WQ + WK :] = total[:, WK:].astype(BF16)

    def key_tile(step, _):
        at = pl.ds(pl.multiple_of(step * 512, 512), 512)
        in_v[at, WQ:PROJ] = lax.dot_general(
            low[:, at], both[:, WQ:], ACROSS, preferred_element_type=F32
        ).astype(BF16)
        return 0

    lax.fori_loop(0, D // 512, key_tile, 0)
    for step in range(D // 512):
        at = slice(step * 512, (step + 1) * 512)
        grad_normed[step] += lax.dot_general(
            both[:, WQ:], win_v[at, WQ:PROJ], NARROW, preferred_element_type=F32
        )
    grad_normed = jnp.concatenate(grad_normed, axis=1)
    hidden = start[...].astype(F32)
    inverse = lax.rsqrt(jnp.mean(hidden * hidden, axis=1, keepdims=True) + epsilon)
    scaled = grad_normed * gains[0:1, :]
    inner = jnp.mean(scaled * hidden, axis=1, keepdims=True)
    grad_in[...] += inverse * scaled - hidden * (inverse * inverse * inverse * inner)
    result[...] = grad_in[...].astype(result.dtype)
    gain_one = jnp.sum(grad_normed * hidden * inverse, axis=0, keepdims=True)
    place = lax.broadcasted_iota(jnp.int32, (128, D), 0)
    rows_of = jnp.where(place == 0, gain_one, jnp.where(place == 1, gain_two, 0.0))
    in_v[:, WQ + 2 * WK :] = rows_of.T.astype(BF16)
    for step in range(D // 256):
        in_copy(step).start()
    for step in range(D // 256):
        in_copy(step).wait()
        out_copy(step).wait()
    for m in range(micro):
        for step in range(1, ns):
            share(step, m).wait_send()


def return_call(plan, layer, collective_id, grads, saved, gains, tables, weights):
    rows, ns, micro, tokens = plan.rows, plan.ns, plan.micro, plan.tokens
    vmem = pl.BlockSpec(memory_space=pltpu.VMEM)
    hbm = pl.BlockSpec(memory_space=pltpu.HBM)
    shape = jax.ShapeDtypeStruct
    exchange = (ns, micro, tokens, 2 * WK)
    return pl.pallas_call(
        functools.partial(return_kernel, plan, layer),
        out_shape=[
            shape((rows, D), BF16 if layer > 0 else F32),
            shape((D, WIN + D), BF16),
        ],
        in_specs=[vmem] * 12 + [hbm],
        out_specs=[vmem, hbm],
        scratch_shapes=[
            pltpu.VMEM((D, WIN), BF16),
            pltpu.VMEM((WQ, D), BF16),
            pltpu.VMEM((rows, D), BF16),
            pltpu.VMEM((rows, WQ), BF16),
            pltpu.VMEM((rows, WQ + 2 * WK), BF16),
            pltpu.VMEM(exchange, BF16),
            pltpu.VMEM(exchange, BF16),
            pltpu.VMEM((D, WIN), BF16),
            pltpu.VMEM((WQ, D), BF16),
            pltpu.VMEM((rows, D), F32),
            DMA((2,)),
            DMA((D // 256,)),
            DMA((WQ // 256,)),
            DMA((ns - 1, micro)),
            DMA((ns, micro)),
        ],
        compiler_params=pltpu.CompilerParams(
            collective_id=collective_id, has_side_effects=True, vmem_limit_bytes=VMEM_LIMIT
        ),
    )(*grads, *saved, gains, *tables, weights)


def slot_table(plan, routes, gates):
    experts, nz = plan.experts, plan.nz
    named = routes[..., None] == jnp.arange(experts, dtype=jnp.int32)
    gate = jnp.sum(jnp.where(named, gates[..., None], 0.0), axis=2)
    named = jnp.any(named, axis=2)
    earlier = jnp.tril(jnp.ones((plan.tokens, plan.tokens), BF16), -1)
    rank = jnp.einsum("ut,mte->mue", earlier, named.astype(BF16), preferred_element_type=F32)
    table = jnp.stack([jnp.where(named, rank, -1.0), gate])
    table = table.reshape(2, plan.micro, plan.tokens, nz, EXP_DEV).transpose(3, 0, 1, 4, 2)
    return table.reshape(nz, -1, plan.tokens)


def slot_places(plan, table):
    nz = plan.nz
    table = table.reshape(nz, 2, plan.micro, EXP_DEV, plan.tokens)
    rank, gate = table[:, 0], table[:, 1]
    first = jnp.arange(plan.micro, dtype=F32)[:, None, None] * plan.capacity
    place = jnp.where(rank >= 0, rank + first, -1.0).transpose(0, 2, 1, 3)
    hit = place[:, :, None] == jnp.arange(plan.slots, dtype=F32)[:, None, None]
    shape = (nz, EXP_DEV * plan.slots, plan.rows)
    one = hit.astype(BF16).reshape(shape)
    weighted = jnp.where(hit, gate.transpose(0, 2, 1, 3)[:, :, None], 0.0)
    weighted = weighted.astype(BF16).reshape(shape)
    return one, weighted


def shards(
    inputs,
    segments,
    routes,
    gate_weights,
    query_weight,
    key_value_weight,
    output_weight,
    norm_gains,
    expert_gate_up,
    expert_down,
    cotangent,
):
    section = lax.axis_index("section")
    shard_index = lax.axis_index("shard")
    tokens = inputs.shape[1]
    plan = Plan((lax.axis_size("section"), lax.axis_size("expert"), lax.axis_size("shard")), tokens)
    micro, rows, layers = plan.micro, plan.rows, plan.nx
    length = tokens * plan.ns

    def mine(value):
        return lax.dynamic_slice_in_dim(value, section * micro, micro, 0)

    paired = plan.nx == 2 and plan.ns == 4 and query_weight.shape[1] % 96 == 0
    gain_columns = jnp.pad(norm_gains[0].T, ((0, 0), (0, PAD - 2)))
    attention_weights = jnp.concatenate(
        [query_weight[0], key_value_weight[0], gain_columns, output_weight[0]], axis=1
    ).astype(BF16)
    table = slot_table(plan, mine(routes), mine(gate_weights))
    if paired:
        weights, table, wide_in, wide_down = gather_call(
            plan, 1, attention_weights, table, (expert_gate_up[0], expert_down[0])
        )
    else:
        weights = lax.all_gather(
            attention_weights, ("section", "expert", "shard"), axis=0, tiled=True
        )
        table = lax.all_to_all(table, "expert", split_axis=0, concat_axis=0, tiled=True)
        wide_in, wide_down = spread_call(
            plan, 1, expert_gate_up[0].astype(BF16), expert_down[0].astype(BF16)
        )
    weights = weights.reshape(layers, D, WIN + D)
    gains = weights[:, :, PROJ : PROJ + 2].transpose(0, 2, 1).astype(F32)
    wide_in = wide_in.reshape(layers, D, 2 * FF)
    wide_down = wide_down.reshape(layers, FF, D)
    one, weighted = slot_places(plan, table)

    offset = shard_index * tokens
    position = (offset + jnp.arange(tokens, dtype=jnp.int32)).astype(F32)
    frequency = rope_base ** (-jnp.arange(HD // 2, dtype=F32) / (HD // 2))
    angles = position[:, None] * frequency[None, :]
    cosine, sine = jnp.cos(angles), jnp.sin(angles)
    cosine = jnp.tile(jnp.concatenate([cosine, cosine], axis=1), (micro, 1))
    sine = jnp.tile(jnp.concatenate([-sine, sine], axis=1), (micro, 1))
    segment_all = mine(segments)[:, 0]
    segment_own = lax.dynamic_slice_in_dim(segment_all, offset, tokens, 1)
    query_place = offset + jnp.arange(tokens, dtype=jnp.int32)
    key_place = jnp.arange(length, dtype=jnp.int32)
    allowed = (segment_own[:, :, None] == segment_all[:, None, :]) & (
        query_place[:, None] >= key_place[None, :]
    )
    tables = (cosine, sine, allowed.astype(F32))

    hidden = mine(inputs).reshape(rows, D)
    grad = mine(cotangent).reshape(rows, D)
    kept, passed = [], []
    attention_terms = [None] * layers
    expert_terms = [None] * layers
    for layer in range(layers):
        start = hidden.astype(BF16)
        middle, normed, low, queries, kv, mixed = attend_call(
            plan, layer, 2 + layer, start, gains[layer], tables, weights
        )
        kept.append((middle, start, low, queries, kv, mixed))
        if layer == layers - 1 and both_fit(plan):
            hidden, grad_moe, expert_terms[layer] = moe_both_call(
                plan,
                layer,
                2 + layers + layer,
                normed,
                grad,
                one,
                weighted,
                wide_in,
                wide_down,
                middle,
            )
            passed.append(None)
        else:
            hidden, *saved = moe_call(
                plan,
                layer,
                F32 if layer == layers - 1 else BF16,
                2 + layers + layer,
                normed,
                one,
                weighted,
                wide_in,
                wide_down,
                middle,
            )
            passed.append(saved)
    output = hidden.reshape(micro, tokens, D)

    for layer in reversed(range(layers)):
        grad_out = grad.astype(BF16)
        if passed[layer] is not None:
            grad_moe, expert_terms[layer] = moe_back_call(
                plan,
                layer,
                2 + 2 * layers + layer,
                grad_out,
                weighted,
                one,
                wide_in,
                wide_down,
                passed[layer],
            )
        grad, attention_terms[layer] = return_call(
            plan,
            layer,
            2 + 3 * layers + layer,
            (grad_out, grad_moe),
            kept[layer],
            gains[layer],
            tables,
            weights,
        )
    input_grad = grad.reshape(micro, tokens, D)

    if paired:
        query_grad, key_value_grad, gain_grad, output_weight_grad, gate_up_grad, down_grad = (
            reduce_call(plan, 2 + 4 * layers, attention_terms, expert_terms)
        )
    else:
        gate_up_grad, down_grad = collect_call(plan, 2 + 4 * layers, expert_terms)
        term = lax.psum_scatter(
            jnp.concatenate(attention_terms),
            ("section", "expert", "shard"),
            scatter_dimension=0,
            tiled=True,
        )
        query_grad, key_value_grad, gain_grad, output_weight_grad = (
            term[:, :WQ],
            term[:, WQ:PROJ],
            term[:, PROJ:WIN],
            term[:, WIN:],
        )
    gain_grad = gain_grad[:, :2].T
    query_grad, key_value_grad, gain_grad, output_weight_grad, gate_up_grad, down_grad = (
        part.astype(F32)[None]
        for part in (
            query_grad,
            key_value_grad,
            gain_grad,
            output_weight_grad,
            gate_up_grad,
            down_grad,
        )
    )
    return (
        output,
        input_grad,
        query_grad,
        key_value_grad,
        output_weight_grad,
        gain_grad,
        gate_up_grad,
        down_grad,
    )


def solution(mesh):
    placed = (
        P(None, ("expert", "shard"), None),
        P(None, "expert", None),
        P(None, ("expert", "shard"), None),
        P(None, ("expert", "shard"), None),
        P("section", ("expert", "shard"), None),
        P("section", ("expert", "shard"), None),
        P("section", ("expert", "shard"), None),
        P("section", None, ("expert", "shard")),
        P("section", "expert", "shard", None),
        P("section", "expert", "shard", None),
        P(None, ("expert", "shard"), None),
    )
    return jax.shard_map(
        shards,
        mesh=mesh,
        in_specs=placed,
        out_specs=(
            P("section", ("expert", "shard"), None),
            P("section", ("expert", "shard"), None),
            P("section", ("expert", "shard"), None),
            P("section", ("expert", "shard"), None),
            P("section", ("expert", "shard"), None),
            P("section", None, ("expert", "shard")),
            P("section", "expert", "shard", None),
            P("section", "expert", "shard", None),
        ),
        check_vma=False,
    )
```
